32 devices in a mesh: seq: 8 (over y, x, core), tp: 4 (over z).
Axes of the slice: x: 2, y: 2, z: 4, core: 2. Of those that a mesh axis runs over, the one named last changes fastest.
Arguments:
- tokens: bfloat16 [6144, 2048], P('seq'), may hold values from -6 to 6
- q_weight: bfloat16 [2048, 2048], P('seq', 'tp'), may hold values from -0.125 to 0.125
- key_matrix: bfloat16 [2048, 1024], P('seq', 'tp'), may hold values from -0.125 to 0.125
- value_matrix: bfloat16 [2048, 1024], P('seq', 'tp'), may hold values from -0.125 to 0.125
- o_weight: bfloat16 [2048, 2048], P('tp', 'seq'), may hold values from -4 to 4
- gate_weight: bfloat16 [2048, 6144], P('seq', 'tp'), may hold values from -0.125 to 0.125
- up_weight: bfloat16 [2048, 6144], P('seq', 'tp'), may hold values from -0.125 to 0.125
- down_weight: bfloat16 [6144, 2048], P('tp', 'seq'), may hold values from -0.078125 to 0.078125
- attn_gain: bfloat16 [2048], P('seq'), may hold values from 0.5 to 1.5
- mlp_gain: bfloat16 [2048], P('seq'), may hold values from 0.5 to 1.5
- query_gain: bfloat16 [128], P('seq'), may hold values from 0.099609375 to 1.8984375
- key_gain: bfloat16 [128], P('seq'), may hold values from 0.099609375 to 1.8984375
- positions: int32 [6144], P('seq'), may hold values from 0 to 5759, as said below
- seq_ids: int32 [6144], replicated, may hold values from 0 to 2, as said below
- cotangent: bfloat16 [6144, 2048], P('seq'), may hold values from -6 to 6
Outputs:
- layer_out: bfloat16 [6144, 2048], P('seq')
- grad_tokens: float32 [6144, 2048], P('seq')
- grad_q_weight: float32 [2048, 2048], P('seq', 'tp')
- grad_k_weight: float32 [2048, 1024], P('seq', 'tp')
- grad_v_weight: float32 [2048, 1024], P('seq', 'tp')
- grad_o_weight: float32 [2048, 2048], P('tp', 'seq')
- grad_gate_weight: float32 [2048, 6144], P('seq', 'tp')
- grad_up_weight: float32 [2048, 6144], P('seq', 'tp')
- grad_down_weight: float32 [6144, 2048], P('tp', 'seq')
- grad_attn_gain: float32 [2048], P('seq')
- grad_mlp_gain: float32 [2048], P('seq')
- grad_query_gain: float32 [128], P('seq')
- grad_key_gain: float32 [128], P('seq')
The draws below stay inside these ranges and needn't reach their ends.
Inputs may be any that keep to these rules, and one draw needn't show every extreme that they name: `seq_ids`: document 0 starts at the first token and ends inside the last 768 tokens; documents 1 and 2 fill the rest of that block in order, each with one token or more. `positions`: position of each token within its document, counting from 0.
All inputs are finite; a program needn't handle non-finite values.
Results may differ from the reference program's by a relative error of at most 0.025.
Values may be sent and summed in bfloat16 or wider, within the bound.
A program may use at most 192 MiB of HBM per device.

```python
import math
import jax
import jax.numpy as jnp
from jax import lax

MODEL_WIDTH = 2048
QUERY_HEADS = 16
KEY_VALUE_HEADS = 8
HEAD_SIZE = 128
FF = 6144
TOK_DEV = 768
TOKENS = 6144


def doc_layout(key):
    tail_len = max(2, TOK_DEV // 2)
    split_len = jax.random.randint(jax.random.fold_in(key, 12), (), 1, tail_len)
    first_end = TOKENS - tail_len
    second_end = first_end + split_len
    token_index = jnp.arange(TOKENS, dtype=jnp.int32)
    doc_number = (token_index >= first_end).astype(jnp.int32) + (token_index >= second_end).astype(jnp.int32)
    doc_start = jnp.where(doc_number == 0, 0, jnp.where(doc_number == 1, first_end, second_end))
    return (doc_number, (token_index - doc_start).astype(jnp.int32))


def draw_seq_ids(key, part):
    layout = doc_layout(key)
    return layout[0]


def draw_positions(key, part):
    layout = doc_layout(key)
    return layout[1]


def block_levels(key, dims, shards, low, high):
    gain, own = 1.0, jax.random.fold_in(key, 6)
    for position, blocks in shards:
        draws = jnp.exp(jax.random.uniform(jax.random.fold_in(own, position), (blocks,), jnp.float32, low / len(shards), high / len(shards)))
        gain = gain * jnp.repeat(draws, dims[position] // blocks).reshape([-1 if axis == position else 1 for axis in range(len(dims))])
    return gain


def centred(rng, extent, deviation, bound, cuts=(), held_as=jnp.bfloat16):
    values = jax.random.normal(rng, extent, jnp.float32) * deviation
    if len(cuts) > 0:
        values = block_levels(rng, extent, cuts, -0.22, 0.18) * values
    return jnp.clip(values, min=-bound, max=bound).astype(held_as)


def setup_inputs(seed: int = 0) -> dict:
    keys = jax.random.split(jax.random.key(seed), 16)
    return {
        "tokens": centred(keys[0], (TOKENS, MODEL_WIDTH), 1.0, 6.0, ((0, 8),)),
        "q_weight": centred(keys[1], (MODEL_WIDTH, QUERY_HEADS * HEAD_SIZE), MODEL_WIDTH ** -0.5, 0.125, ((0, 8), (1, 4))),
        "key_matrix": centred(keys[2], (MODEL_WIDTH, KEY_VALUE_HEADS * HEAD_SIZE), MODEL_WIDTH ** -0.5, 0.125, ((0, 8), (1, 4))),
        "value_matrix": centred(keys[3], (MODEL_WIDTH, KEY_VALUE_HEADS * HEAD_SIZE), MODEL_WIDTH ** -0.5, 0.125, ((0, 8), (1, 4))),
        "o_weight": centred(keys[4], (QUERY_HEADS * HEAD_SIZE, MODEL_WIDTH), (max(1, QUERY_HEADS * HEAD_SIZE * 8 // TOKENS)) ** -0.5, 4.0, ((0, 4), (1, 8))),
        "gate_weight": centred(keys[5], (MODEL_WIDTH, FF), MODEL_WIDTH ** -0.5, 0.125, ((0, 8), (1, 4))),
        "up_weight": centred(keys[6], (MODEL_WIDTH, FF), MODEL_WIDTH ** -0.5, 0.125, ((0, 8), (1, 4))),
        "down_weight": centred(keys[7], (FF, MODEL_WIDTH), FF ** -0.5, 0.078125, ((0, 4), (1, 8))),
        "attn_gain": jnp.clip(1.0 + 0.1 * jax.random.normal(keys[8], (MODEL_WIDTH,), jnp.float32), 0.5, 1.5).astype(jnp.bfloat16),
        "mlp_gain": jnp.clip(1.0 + 0.1 * jax.random.normal(keys[9], (MODEL_WIDTH,), jnp.float32), 0.5, 1.5).astype(jnp.bfloat16),
        "query_gain": jnp.clip(1.0 + 0.18 * jax.random.normal(keys[10], (HEAD_SIZE,), jnp.float32), 0.099609375, 1.8984375).astype(jnp.bfloat16),
        "key_gain": jnp.clip(1.0 + 0.18 * jax.random.normal(keys[11], (HEAD_SIZE,), jnp.float32), 0.099609375, 1.8984375).astype(jnp.bfloat16),
        "positions": draw_positions(jax.random.fold_in(keys[15], 71), 0),
        "seq_ids": draw_seq_ids(jax.random.fold_in(keys[15], 71), 0),
        "cotangent": centred(keys[14], (TOKENS, MODEL_WIDTH), 1.0, 6.0, ((0, 8),)),
    }


@jax.custom_vjp
def low_precise(v):
    return lax.optimization_barrier(v.astype(jnp.bfloat16)).astype(jnp.float32)

@jax.custom_vjp
def low_precise_backward(v):
    return v

def low_keep(v):
    return (low_precise(v), None)

def low_pass(kept, grad):
    return (grad,)

def back_keep(v):
    return (v, None)

def back_low(kept, grad):
    return (low_precise(grad),)
low_precise.defvjp(low_keep, low_pass)
low_precise_backward.defvjp(back_keep, back_low)
EPS = 1e-06
BASE = 1000000.0
HIGH_PRECISE = lax.Precision.HIGHEST

def norm_rows(values, gain_vec):
    return values * lax.rsqrt(lax.optimization_barrier(jnp.mean(values * values, axis=-1, keepdims=True)) + EPS) * gain_vec

def rotate(values, positions):
    half_dim = values.shape[-1] // 2
    frequency = BASE ** (-2.0 * jnp.arange(half_dim, dtype=jnp.float32) / values.shape[-1])
    angles = positions.astype(jnp.float32)[:, None] * frequency[None, :]
    cosines = jnp.cos(angles)[:, None, :]
    sine_values = jnp.sin(angles)[:, None, :]
    lower_half = values[..., :half_dim]
    upper_half = values[..., half_dim:]
    return jnp.concatenate([lower_half * cosines - upper_half * sine_values, upper_half * cosines + lower_half * sine_values], axis=-1)

def attend_block(query_tensor, all_keys, all_values, seq_ids, offset):
    count_of_rows = query_tensor.shape[0]
    key_count = all_keys.shape[0]
    heads_per_group = QUERY_HEADS // KEY_VALUE_HEADS
    q_index = offset + jnp.arange(count_of_rows, dtype=jnp.int32)
    k_index = jnp.arange(key_count, dtype=jnp.int32)
    q_docs = lax.dynamic_slice_in_dim(seq_ids, offset, count_of_rows)
    allowed = (q_docs[:, None] == seq_ids[None, :]) & (k_index[None, :] <= q_index[:, None])
    grouped_queries = query_tensor.reshape(count_of_rows, KEY_VALUE_HEADS, heads_per_group, HEAD_SIZE)
    scores = jnp.einsum('qkgd,tkd->kgqt', grouped_queries, all_keys, precision=HIGH_PRECISE) * HEAD_SIZE ** (-0.5)
    scores = low_precise_backward(jnp.where(allowed[None, None], scores, -1e+30))
    weights = jax.nn.softmax(scores, axis=-1)
    attended = jnp.einsum('kgqt,tkd->qkgd', low_precise(weights), all_values, precision=HIGH_PRECISE)
    return attended.reshape(count_of_rows, QUERY_HEADS * HEAD_SIZE)

def block_forward(tokens, q_weight, key_matrix, value_matrix, o_weight, gate_weight, up_weight, down_weight, attn_gain, mlp_gain, query_gain, key_gain, positions, seq_ids):
    count_of_tokens = tokens.shape[0]
    normalized_input = low_precise(norm_rows(tokens, attn_gain))
    q_proj = low_precise_backward(jnp.dot(normalized_input, q_weight, precision=HIGH_PRECISE)).reshape(count_of_tokens, QUERY_HEADS, HEAD_SIZE)
    key_projected = low_precise_backward(jnp.dot(normalized_input, key_matrix, precision=HIGH_PRECISE)).reshape(count_of_tokens, KEY_VALUE_HEADS, HEAD_SIZE)
    value_projected = low_precise(low_precise_backward(jnp.dot(normalized_input, value_matrix, precision=HIGH_PRECISE))).reshape(count_of_tokens, KEY_VALUE_HEADS, HEAD_SIZE)
    query_tensor = low_precise(rotate(norm_rows(q_proj, query_gain), positions))
    all_keys = low_precise(rotate(norm_rows(key_projected, key_gain), positions))
    q_block = math.gcd(count_of_tokens, 512)
    starts = jnp.arange(count_of_tokens // q_block, dtype=jnp.int32) * q_block
    checked = jax.checkpoint(attend_block)

    def one_block(offset):
        query_rows = lax.dynamic_slice_in_dim(query_tensor, offset, q_block)
        return checked(query_rows, all_keys, value_projected, seq_ids, offset)
    attended = lax.map(one_block, starts).reshape(count_of_tokens, QUERY_HEADS * HEAD_SIZE)
    attended = low_precise(low_precise_backward(attended))
    after_attn = tokens + low_precise_backward(jnp.dot(attended, o_weight, precision=HIGH_PRECISE))
    normed_mid = low_precise(norm_rows(after_attn, mlp_gain))
    gate_pre = low_precise_backward(jnp.dot(normed_mid, gate_weight, precision=HIGH_PRECISE))
    up_pre = low_precise_backward(jnp.dot(normed_mid, up_weight, precision=HIGH_PRECISE))
    activation = low_precise(jax.nn.silu(gate_pre) * up_pre)
    return after_attn + low_precise_backward(jnp.dot(activation, down_weight, precision=HIGH_PRECISE))

def reference(tokens, q_weight, key_matrix, value_matrix, o_weight, gate_weight, up_weight, down_weight, attn_gain, mlp_gain, query_gain, key_gain, positions, seq_ids, cotangent):
    floats = [array.astype(jnp.float32) for array in (tokens, q_weight, key_matrix, value_matrix, o_weight, gate_weight, up_weight, down_weight, attn_gain, mlp_gain, query_gain, key_gain)]

    def forward(*operands):
        return block_forward(*operands, positions, seq_ids)
    result, pullback = jax.vjp(forward, *floats)
    gradients = pullback(cotangent.astype(jnp.float32))
    return (result.astype(jnp.bfloat16), gradients[0], gradients[1], gradients[2], gradients[3], gradients[4], gradients[5], gradients[6], gradients[7], gradients[8], gradients[9], gradients[10], gradients[11])
```

```python
import functools
import math

import jax
import jax.numpy as jnp
from jax import lax
from jax.experimental import pallas as pl
from jax.experimental.pallas import tpu as pltpu

from jax.sharding import PartitionSpec as P

HEAD_SIZE = 128
LOG2E = 1.4426950408889634
VMEM_BYTES = 60 << 20
NT = (((1,), (1,)), ((), ()))
TN = (((0,), (0,)), ((), ()))


def mm(a, b, dims=(((1,), (0,)), ((), ()))):
    return lax.dot_general(a, b, dims, preferred_element_type=jnp.float32)


def cut(rows, most=256):
    return math.gcd(rows, most)


def attn_fwd_block(q_ref, k_ref, v_ref, out_ref, sum_ref, bias_ref, kv, rows, tile):
    scale = HEAD_SIZE ** -0.5 * LOG2E
    all_rows = q_ref.shape[1]
    for h in range(kv):
        cols = slice(h * HEAD_SIZE, (h + 1) * HEAD_SIZE)
        for start in range(0, all_rows, tile):
            at = start % rows
            n_keys = rows if bias_ref is None else at + tile
            scores = mm(q_ref[h, start:start + tile], k_ref[:n_keys, cols], NT) * scale
            if bias_ref is not None:
                scores = scores + bias_ref[at:at + tile, :n_keys]
            weights = jnp.exp2(scores)
            part = weights[:, :HEAD_SIZE]
            for c in range(HEAD_SIZE, n_keys, HEAD_SIZE):
                part = part + weights[:, c:c + HEAD_SIZE]
            sum_ref[h, start:start + tile] += part
            out_ref[h, start:start + tile] += mm(weights.astype(jnp.bfloat16), v_ref[:n_keys, cols])


def fill_bias(bias_ref, q_docs, k_docs):
    rows, keys = bias_ref.shape
    visible = (lax.broadcasted_iota(jnp.int32, (rows, keys), 1)
               <= lax.broadcasted_iota(jnp.int32, (rows, keys), 0)) & (q_docs == k_docs)
    bias_ref[...] = jnp.where(visible, 0.0, -1e30)


def fwd_kernel(q_ref, k_ref, v_ref, qd_ref, kd_ref, out_ref, lse_ref, acc, total, bias):
    kv, all_rows, _ = q_ref.shape
    rows = k_ref.shape[1]
    me = lax.axis_index("seq")
    tile = cut(rows)
    acc[...] = jnp.zeros_like(acc)
    total[...] = jnp.zeros_like(total)
    fill_bias(bias, qd_ref[...], kd_ref[...])

    @pl.loop(0, me)
    def _(j):
        attn_fwd_block(q_ref, k_ref.at[j], v_ref.at[j], acc, total, None, kv, rows, tile)

    first = jnp.where(qd_ref[...] == 0, 1.0, 0.0)
    for h in range(kv):
        for start in range(0, all_rows, rows):
            acc[h, start:start + rows] *= first
            total[h, start:start + rows] *= first
    attn_fwd_block(q_ref, k_ref.at[me], v_ref.at[me], acc, total, bias, kv, rows, tile)
    for h in range(kv):
        for start in range(0, all_rows, tile):
            t = total[h, start:start + tile]
            s = jnp.sum(t, axis=1, keepdims=True)
            out_ref[h, start:start + tile] = acc[h, start:start + tile] / s
            lse_ref[h, :, start:start + tile] = jnp.log2(jnp.sum(t.T, axis=0, keepdims=True))


def attention_forward(q, k, v, q_docs, k_docs):
    kv, all_rows, _ = q.shape
    n, rows, _ = k.shape
    vm = pl.BlockSpec(memory_space=pltpu.VMEM)
    return pl.pallas_call(
        fwd_kernel,
        out_shape=(jax.ShapeDtypeStruct(q.shape, jnp.float32),
                   jax.ShapeDtypeStruct((kv, 1, all_rows), jnp.float32)),
        in_specs=[vm] * 5, out_specs=(vm, vm),
        scratch_shapes=[pltpu.VMEM(q.shape, jnp.float32), pltpu.VMEM(q.shape, jnp.float32),
                        pltpu.VMEM((rows, rows), jnp.float32)],
        compiler_params=pltpu.CompilerParams(vmem_limit_bytes=VMEM_BYTES),
        name="attn_fwd",
    )(q, k, v, q_docs, k_docs)


def attn_bwd_block(q_ref, do_ref, lse_ref, delta_ref, k_ref, v_ref, dq_ref, dk_ref, dv_ref, bias_ref, kv, rows, tile):
    scale = HEAD_SIZE ** -0.5 * LOG2E
    all_rows = q_ref.shape[1]
    for h in range(kv):
        cols = slice(h * HEAD_SIZE, (h + 1) * HEAD_SIZE)
        dk_ref[:, cols] = jnp.zeros((rows, HEAD_SIZE), jnp.float32)
        dv_ref[:, cols] = jnp.zeros((rows, HEAD_SIZE), jnp.float32)
        for start in range(0, all_rows, tile):
            at = start % rows
            n_keys = rows if bias_ref is None else at + tile
            q = q_ref[h, start:start + tile]
            do = do_ref[h, start:start + tile]
            k = k_ref[:n_keys, cols]
            scores = mm(k, q, NT) * scale - lse_ref[h, :, start:start + tile]
            if bias_ref is not None:
                scores = scores + bias_ref[:n_keys, at:at + tile]
            probs = jnp.exp2(scores)
            grad = mm(v_ref[:n_keys, cols], do, NT)
            grad = (probs * (grad - delta_ref[h, :, start:start + tile])).astype(jnp.bfloat16)
            dv_ref[:n_keys, cols] += mm(probs.astype(jnp.bfloat16), do)
            dk_ref[:n_keys, cols] += mm(grad, q)
            dq_ref[h, start:start + tile] += mm(grad, k, TN)


def bwd_kernel(q_ref, do_ref, o_ref, lse_ref, k_ref, v_ref, kd_ref, qdr_ref, dq_ref, dk_ref, dv_ref,
               delta, lse_off, dk, dv, bias):
    kv, all_rows, _ = q_ref.shape
    n, rows, _ = k_ref.shape
    me = lax.axis_index("seq")
    tile = cut(rows)
    visible = (lax.broadcasted_iota(jnp.int32, (rows, rows), 0)
               <= lax.broadcasted_iota(jnp.int32, (rows, rows), 1)) & (kd_ref[...] == qdr_ref[...])
    bias[...] = jnp.where(visible, 0.0, -1e30)
    dq_ref[...] = jnp.zeros_like(dq_ref)
    off = jnp.where(qdr_ref[...] == 0, 0.0, 1e30)
    for h in range(kv):
        for start in range(0, all_rows, rows):
            at = slice(start, start + rows)
            prod = do_ref[h, at].astype(jnp.float32) * o_ref[h, at]
            delta[h, :, at] = jnp.sum(prod.T, axis=0, keepdims=True)
            lse_off[h, :, at] = lse_ref[h, :, at] + off
    scale = HEAD_SIZE ** -0.5

    @pl.loop(0, me)
    def _(j):
        attn_bwd_block(q_ref, do_ref, lse_off, delta, k_ref.at[j], v_ref.at[j], dq_ref, dk, dv, None, kv, rows, tile)
        dk_ref[j] = (dk[...] * scale).astype(jnp.bfloat16)
        dv_ref[j] = dv[...].astype(jnp.bfloat16)

    attn_bwd_block(q_ref, do_ref, lse_ref, delta, k_ref.at[me], v_ref.at[me], dq_ref, dk, dv, bias, kv, rows, tile)
    dk_ref[me] = (dk[...] * scale).astype(jnp.bfloat16)
    dv_ref[me] = dv[...].astype(jnp.bfloat16)

    @pl.loop(me + 1, n)
    def _(j):
        dk_ref[j] = jnp.zeros(dk_ref.shape[1:], jnp.bfloat16)
        dv_ref[j] = jnp.zeros(dv_ref.shape[1:], jnp.bfloat16)

    dq_ref[...] *= scale


def attention_backward(q, do, o, lse, k, v, q_docs, k_docs):
    kv, all_rows, _ = q.shape
    n, rows, width = k.shape
    vm = pl.BlockSpec(memory_space=pltpu.VMEM)
    return pl.pallas_call(
        bwd_kernel,
        out_shape=(jax.ShapeDtypeStruct(q.shape, jnp.float32),
                   jax.ShapeDtypeStruct(k.shape, jnp.bfloat16),
                   jax.ShapeDtypeStruct(k.shape, jnp.bfloat16)),
        in_specs=[vm] * 8, out_specs=(vm, vm, vm),
        scratch_shapes=[pltpu.VMEM((kv, 1, all_rows), jnp.float32), pltpu.VMEM((kv, 1, all_rows), jnp.float32),
                        pltpu.VMEM((rows, width), jnp.float32), pltpu.VMEM((rows, width), jnp.float32),
                        pltpu.VMEM((rows, rows), jnp.float32)],
        compiler_params=pltpu.CompilerParams(vmem_limit_bytes=VMEM_BYTES),
        name="attn_bwd",
    )(q, do, o, lse, k, v, q_docs, k_docs)


EPS = 1e-06
BASE = 1000000.0


def norm_rows(values, gain_vec):
    return values * lax.rsqrt(jnp.mean(values * values, axis=-1, keepdims=True) + EPS) * gain_vec


def norm_back(values, gain_vec, grad_out):
    inverse = lax.rsqrt(jnp.mean(values * values, axis=-1, keepdims=True) + EPS)
    normed = values * inverse
    scaled = grad_out * gain_vec
    grad_in = inverse * (scaled - normed * jnp.mean(scaled * normed, axis=-1, keepdims=True))
    return (grad_in, grad_out * normed)


def rope_tables(positions, head_dim):
    half_dim = head_dim // 2
    frequency = BASE ** (-2.0 * jnp.arange(half_dim, dtype=jnp.float32) / head_dim)
    angles = positions.astype(jnp.float32)[:, None] * frequency[None, :]
    return (jnp.cos(angles)[:, None, :], jnp.sin(angles)[:, None, :])


def rotate(values, cosines, sine_values, direction):
    half_dim = values.shape[-1] // 2
    lower_half = values[..., :half_dim]
    upper_half = values[..., half_dim:]
    signed = sine_values * direction
    return jnp.concatenate(
        [lower_half * cosines - upper_half * signed, upper_half * cosines + lower_half * signed],
        axis=-1,
    )


def per_device(
    tokens,
    q_weight,
    key_matrix,
    value_matrix,
    o_weight,
    gate_weight,
    up_weight,
    down_weight,
    attn_gain,
    mlp_gain,
    query_gain,
    key_gain,
    positions,
    seq_ids,
    cotangent,
):
    f32 = jnp.float32
    b16 = jnp.bfloat16
    local_rows = tokens.shape[0]
    q_local = q_weight.shape[1] // HEAD_SIZE
    kv_local = key_matrix.shape[1] // HEAD_SIZE
    heads_per_group = q_local // kv_local
    share_rows = local_rows // lax.axis_size("tp")
    share_start = lax.axis_index("tp") * share_rows
    row_parts = (
        lax.all_gather(q_weight, "seq", axis=0, tiled=True),
        lax.all_gather(key_matrix, "seq", axis=0, tiled=True),
        lax.all_gather(value_matrix, "seq", axis=0, tiled=True),
        lax.all_gather(gate_weight, "seq", axis=0, tiled=True),
        lax.all_gather(up_weight, "seq", axis=0, tiled=True),
        lax.all_gather(attn_gain, "seq", axis=0, tiled=True),
        lax.all_gather(mlp_gain, "seq", axis=0, tiled=True),
        lax.all_gather(query_gain, "seq", axis=0, tiled=True),
        lax.all_gather(key_gain, "seq", axis=0, tiled=True),
    )
    col_parts = (
        lax.all_gather(o_weight, "seq", axis=1, tiled=True),
        lax.all_gather(down_weight, "seq", axis=1, tiled=True),
    )
    full_q, full_k, full_v, full_gate, full_up, gain_attn, gain_mlp, gain_query, gain_key = (
        row_parts
    )
    full_o, full_down = col_parts
    gain_attn = gain_attn.astype(f32)
    gain_mlp = gain_mlp.astype(f32)
    gain_query = gain_query.astype(f32)
    gain_key = gain_key.astype(f32)
    token_f = tokens.astype(f32)
    normalized_input = norm_rows(token_f, gain_attn).astype(b16)
    q_proj = jnp.dot(normalized_input, full_q, preferred_element_type=f32).reshape(
        local_rows, q_local, HEAD_SIZE
    )
    key_projected = jnp.dot(normalized_input, full_k, preferred_element_type=f32).reshape(
        local_rows, kv_local, HEAD_SIZE
    )
    v_local = (
        jnp.dot(normalized_input, full_v, preferred_element_type=f32)
        .astype(b16)
        .reshape(local_rows, kv_local, HEAD_SIZE)
    )
    cosines, sine_values = rope_tables(positions, HEAD_SIZE)
    q_final = rotate(norm_rows(q_proj, gain_query), cosines, sine_values, 1.0).astype(b16)
    k_local = rotate(norm_rows(key_projected, gain_key), cosines, sine_values, 1.0).astype(b16)
    all_keys, all_values = (
        lax.all_gather(k_local, "seq", axis=0, tiled=True),
        lax.all_gather(v_local, "seq", axis=0, tiled=True),
    )
    row_offset = lax.axis_index("seq") * local_rows
    seq_count = lax.axis_size("seq")
    own_docs = lax.dynamic_slice_in_dim(seq_ids, row_offset, local_rows)
    doc_column, doc_row = own_docs[:, None], own_docs[None, :]

    def by_head(flat):
        heads = flat.reshape(local_rows, kv_local, heads_per_group, HEAD_SIZE)
        return heads.transpose(1, 2, 0, 3).reshape(kv_local, heads_per_group * local_rows, HEAD_SIZE)

    def by_row(heads):
        split = heads.reshape(kv_local, heads_per_group, local_rows, HEAD_SIZE)
        return split.transpose(2, 0, 1, 3).reshape(local_rows, q_local * HEAD_SIZE)

    queries_h = by_head(q_final)
    keys_b = all_keys.reshape(seq_count, local_rows, kv_local * HEAD_SIZE)
    values_b = all_values.reshape(seq_count, local_rows, kv_local * HEAD_SIZE)
    attended_h, lse = attention_forward(queries_h, keys_b, values_b, doc_column, doc_row)
    attended = by_row(attended_h)
    attended_low = attended.astype(b16)
    attn_part = jnp.dot(attended_low, full_o, preferred_element_type=f32)
    after_attn = token_f + lax.psum(attn_part.astype(jnp.bfloat16), "tp").astype(jnp.float32)
    normed_mid = norm_rows(after_attn, gain_mlp).astype(b16)
    gate_pre = jnp.dot(normed_mid, full_gate, preferred_element_type=f32)
    up_pre = jnp.dot(normed_mid, full_up, preferred_element_type=f32)
    sigmoid_g = jax.nn.sigmoid(gate_pre)
    silu_gate = gate_pre * sigmoid_g
    activation = (silu_gate * up_pre).astype(b16)
    mlp_part = jnp.dot(activation, full_down, preferred_element_type=f32)
    layer_out = (
        after_attn + lax.psum(mlp_part.astype(jnp.bfloat16), "tp").astype(jnp.float32)
    ).astype(b16)
    back_rows = (
        lax.all_gather(q_weight, "seq", axis=0, tiled=True),
        lax.all_gather(key_matrix, "seq", axis=0, tiled=True),
        lax.all_gather(value_matrix, "seq", axis=0, tiled=True),
        lax.all_gather(gate_weight, "seq", axis=0, tiled=True),
        lax.all_gather(up_weight, "seq", axis=0, tiled=True),
        lax.all_gather(attn_gain, "seq", axis=0, tiled=True),
        lax.all_gather(mlp_gain, "seq", axis=0, tiled=True),
        lax.all_gather(query_gain, "seq", axis=0, tiled=True),
        lax.all_gather(key_gain, "seq", axis=0, tiled=True),
    )
    back_cols = (
        lax.all_gather(o_weight, "seq", axis=1, tiled=True),
        lax.all_gather(down_weight, "seq", axis=1, tiled=True),
    )
    full_q, full_k, full_v, full_gate, full_up = (
        back_rows[0],
        back_rows[1],
        back_rows[2],
        back_rows[3],
        back_rows[4],
    )
    full_o, full_down = back_cols
    grad_out = cotangent.astype(f32)
    grad_down = jnp.einsum("lf,ld->fd", activation, cotangent, preferred_element_type=f32)
    grad_act = jnp.einsum("ld,fd->lf", cotangent, full_down, preferred_element_type=f32)
    grad_gate = (grad_act * up_pre * sigmoid_g * (1.0 + gate_pre * (1.0 - sigmoid_g))).astype(b16)
    grad_up = (grad_act * silu_gate).astype(b16)
    grad_gate_w = jnp.einsum("ld,lf->df", normed_mid, grad_gate, preferred_element_type=f32)
    grad_up_w = jnp.einsum("ld,lf->df", normed_mid, grad_up, preferred_element_type=f32)
    mid_part = jnp.einsum(
        "lf,df->ld", grad_gate, full_gate, preferred_element_type=f32
    ) + jnp.einsum("lf,df->ld", grad_up, full_up, preferred_element_type=f32)
    grad_mid = lax.psum(mid_part.astype(jnp.bfloat16), "tp").astype(jnp.float32)
    grad_in_mid, mlp_gain_terms = norm_back(after_attn, gain_mlp, grad_mid)
    grad_after = grad_out + grad_in_mid
    mlp_gain_part = jnp.sum(
        lax.dynamic_slice_in_dim(mlp_gain_terms, share_start, share_rows), axis=0
    )
    grad_after_low = grad_after.astype(b16)
    grad_o_w = jnp.einsum("lh,ld->hd", attended_low, grad_after_low, preferred_element_type=f32)
    grad_att = jnp.einsum("ld,hd->lh", grad_after_low, full_o, preferred_element_type=f32).astype(
        b16
    )
    grad_query_h, grad_keys, grad_values = attention_backward(
        queries_h, by_head(grad_att), attended_h, lse, keys_b, values_b, doc_column, doc_row
    )
    grad_query = by_row(grad_query_h).reshape(local_rows, q_local, HEAD_SIZE)
    key_rows = seq_count * local_rows
    own_keys, own_values = (
        lax.psum_scatter(
            grad_keys.reshape(key_rows, kv_local, HEAD_SIZE).astype(jnp.bfloat16),
            "seq",
            scatter_dimension=0,
            tiled=True,
        ).astype(jnp.float32),
        lax.psum_scatter(
            grad_values.reshape(key_rows, kv_local, HEAD_SIZE).astype(jnp.bfloat16),
            "seq",
            scatter_dimension=0,
            tiled=True,
        ).astype(jnp.float32),
    )
    grad_v_low = own_values.astype(b16).reshape(local_rows, kv_local * HEAD_SIZE)
    grad_k_in, key_gain_terms = norm_back(
        key_projected, gain_key, rotate(own_keys, cosines, sine_values, -1.0)
    )
    grad_q_in, query_gain_terms = norm_back(
        q_proj, gain_query, rotate(grad_query, cosines, sine_values, -1.0)
    )
    grad_k_low = grad_k_in.astype(b16).reshape(local_rows, kv_local * HEAD_SIZE)
    grad_q_low = grad_q_in.astype(b16).reshape(local_rows, q_local * HEAD_SIZE)
    in_part = (
        jnp.einsum("lh,dh->ld", grad_q_low, full_q, preferred_element_type=f32)
        + jnp.einsum("lh,dh->ld", grad_k_low, full_k, preferred_element_type=f32)
        + jnp.einsum("lh,dh->ld", grad_v_low, full_v, preferred_element_type=f32)
    )
    grad_in, grad_mgain, grad_qgain, grad_kgain = (
        lax.psum(in_part.astype(jnp.bfloat16), "tp").astype(jnp.float32),
        lax.psum(mlp_gain_part.astype(jnp.bfloat16), "tp").astype(jnp.float32),
        lax.psum(jnp.sum(query_gain_terms, axis=(0, 1)).astype(jnp.bfloat16), "tp").astype(
            jnp.float32
        ),
        lax.psum(jnp.sum(key_gain_terms, axis=(0, 1)).astype(jnp.bfloat16), "tp").astype(
            jnp.float32
        ),
    )
    grad_in_tok, attn_gain_terms = norm_back(token_f, gain_attn, grad_in)
    grad_tokens = grad_after + grad_in_tok
    grad_q_w = jnp.einsum("ld,lh->dh", normalized_input, grad_q_low, preferred_element_type=f32)
    grad_k_w = jnp.einsum("ld,lh->dh", normalized_input, grad_k_low, preferred_element_type=f32)
    grad_v_w = jnp.einsum("ld,lh->dh", normalized_input, grad_v_low, preferred_element_type=f32)
    owned_rows = (
        lax.psum_scatter(
            grad_q_w.astype(jnp.bfloat16), "seq", scatter_dimension=0, tiled=True
        ).astype(jnp.float32),
        lax.psum_scatter(
            grad_k_w.astype(jnp.bfloat16), "seq", scatter_dimension=0, tiled=True
        ).astype(jnp.float32),
        lax.psum_scatter(
            grad_v_w.astype(jnp.bfloat16), "seq", scatter_dimension=0, tiled=True
        ).astype(jnp.float32),
        lax.psum_scatter(
            grad_gate_w.astype(jnp.bfloat16), "seq", scatter_dimension=0, tiled=True
        ).astype(jnp.float32),
        lax.psum_scatter(
            grad_up_w.astype(jnp.bfloat16), "seq", scatter_dimension=0, tiled=True
        ).astype(jnp.float32),
        lax.psum_scatter(
            jnp.sum(attn_gain_terms, axis=0).astype(jnp.bfloat16),
            "seq",
            scatter_dimension=0,
            tiled=True,
        ).astype(jnp.float32),
        lax.psum_scatter(
            grad_mgain.astype(jnp.bfloat16), "seq", scatter_dimension=0, tiled=True
        ).astype(jnp.float32),
        lax.psum_scatter(
            grad_qgain.astype(jnp.bfloat16), "seq", scatter_dimension=0, tiled=True
        ).astype(jnp.float32),
        lax.psum_scatter(
            grad_kgain.astype(jnp.bfloat16), "seq", scatter_dimension=0, tiled=True
        ).astype(jnp.float32),
    )
    owned_cols = (
        lax.psum_scatter(
            grad_o_w.astype(jnp.bfloat16), "seq", scatter_dimension=1, tiled=True
        ).astype(jnp.float32),
        lax.psum_scatter(
            grad_down.astype(jnp.bfloat16), "seq", scatter_dimension=1, tiled=True
        ).astype(jnp.float32),
    )
    return (
        layer_out,
        grad_tokens,
        owned_rows[0],
        owned_rows[1],
        owned_rows[2],
        owned_cols[0],
        owned_rows[3],
        owned_rows[4],
        owned_cols[1],
        owned_rows[5],
        owned_rows[6],
        owned_rows[7],
        owned_rows[8],
    )


def solution(mesh):
    placed = (
        P("seq", None),
        P("seq", "tp"),
        P("seq", "tp"),
        P("seq", "tp"),
        P("tp", "seq"),
        P("seq", "tp"),
        P("seq", "tp"),
        P("tp", "seq"),
        P("seq"),
        P("seq"),
        P("seq"),
        P("seq"),
        P("seq"),
        P(),
        P("seq", None),
    )
    return jax.shard_map(
        per_device,
        mesh=mesh,
        in_specs=placed,
        out_specs=(
            P("seq", None),
            P("seq", None),
            P("seq", "tp"),
            P("seq", "tp"),
            P("seq", "tp"),
            P("tp", "seq"),
            P("seq", "tp"),
            P("seq", "tp"),
            P("tp", "seq"),
            P("seq"),
            P("seq"),
            P("seq"),
            P("seq"),
        ),
        check_vma=False,
    )
```

```python
import functools
import math

import jax
import jax.numpy as jnp
from jax import lax
from jax.experimental import pallas as pl
from jax.experimental.pallas import tpu as pltpu

from jax.sharding import PartitionSpec as P

HEAD_SIZE = 128
EPS = 1e-06
BASE = 1000000.0
LOG2E = 1.4426950408889634
VMEM_BYTES = 62 << 20
NT = (((1,), (1,)), ((), ()))
TN = (((0,), (0,)), ((), ()))


def mm(a, b, dims=(((1,), (0,)), ((), ()))):
    return lax.dot_general(a, b, dims, preferred_element_type=jnp.float32)


def cut(rows, most=256):
    return math.gcd(rows, most)


MESH = pl.DeviceIdType.MESH
ANY = pl.BlockSpec(memory_space=pl.ANY)
VM = pl.BlockSpec(memory_space=pltpu.VMEM)


def bit_of(index, bit):
    return lax.rem(index // (1 << bit), 2)


def toggled(index, offset, bits):
    for bit in range(bits):
        if offset >> bit & 1:
            index = index + (1 - 2 * bit_of(index, bit)) * (1 << bit)
    return index


def seq_bits():
    return lax.axis_size("seq").bit_length() - 1


def bit_order(half):
    outer = list(range(1, seq_bits()))
    return (outer if half == 0 else outer[::-1]) + [0]


def last_bit(half, offset):
    return [b for b in bit_order(half) if offset >> b & 1][-1]


def greet(over_seq, over_tp):
    barrier = pltpu.get_barrier_semaphore()
    s, t, count = lax.axis_index("seq"), lax.axis_index("tp"), lax.axis_size("tp")
    expected = 0
    if over_seq:
        for bit in range(seq_bits()):
            pl.semaphore_signal(barrier, inc=1, device_id=(toggled(s, 1 << bit, seq_bits()), t), device_id_type=MESH)
        expected = seq_bits()
    if over_tp:
        @pl.when(t > 0)
        def _():
            pl.semaphore_signal(barrier, inc=1, device_id=(s, t - 1), device_id_type=MESH)

        @pl.when(t < count - 1)
        def _():
            pl.semaphore_signal(barrier, inc=1, device_id=(s, t + 1), device_id_type=MESH)

        expected = expected + jnp.where(t > 0, 1, 0) + jnp.where(t < count - 1, 1, 0)
    pl.semaphore_wait(barrier, expected)


class SeqGather:
    def __init__(self, buf, send, recv, halves=2):
        self.buf, self.send, self.recv, self.halves = buf, send, recv, halves
        self.bits = seq_bits()
        self.n = 1 << self.bits
        self.me, self.t = lax.axis_index("seq"), lax.axis_index("tp")

    def block(self, half, offset):
        rows = self.buf.shape[1] // self.halves
        return self.buf.at[toggled(self.me, offset, self.bits), pl.ds(half * rows, rows)]

    def copy(self, half, offset):
        bit = last_bit(half, offset)
        ref = self.block(half, offset ^ (1 << bit))
        return pltpu.make_async_remote_copy(
            src_ref=ref, dst_ref=ref, send_sem=self.send.at[half, offset], recv_sem=self.recv.at[half, offset],
            device_id=(toggled(self.me, 1 << bit, self.bits), self.t), device_id_type=MESH)

    def start(self, half):
        for bit in bit_order(half):
            self.copy(half, 1 << bit).start()

    def arrive(self, half, offset):
        ref = self.block(half, offset)
        pltpu.make_async_remote_copy(
            src_ref=ref, dst_ref=ref, send_sem=self.send.at[half, offset], recv_sem=self.recv.at[half, offset],
            device_id=(self.me, self.t), device_id_type=MESH).wait_recv()
        order = bit_order(half)
        for bit in order[order.index(last_bit(half, offset)) + 1:]:
            self.copy(half, offset | 1 << bit).start()

    def finish(self):
        for half in range(self.halves):
            for offset in range(1, self.n):
                self.copy(half, offset).wait_send()

    def events(self):
        def due(event):
            half, offset = event
            order = bit_order(half)
            steps = [order.index(b) for b in range(1, self.bits) if offset >> b & 1]
            return (sum(2 ** k for k in steps), offset & 1, half)
        return sorted(((h, r) for h in range(self.halves) for r in range(1, self.n)), key=due)


def gather_sems(halves=2):
    n = lax.axis_size("seq")
    return [pltpu.SemaphoreType.DMA((halves, n)), pltpu.SemaphoreType.DMA((halves, n))]


class LineSum:
    def __init__(self, part, recv, send_sem, recv_sem):
        self.part, self.recv, self.send_sem, self.recv_sem = part, recv, send_sem, recv_sem
        self.m = part.shape[1]
        self.s, self.t = lax.axis_index("seq"), lax.axis_index("tp")

    def copy(self, p, j, slot, to):
        return pltpu.make_async_remote_copy(
            src_ref=self.part.at[p, j], dst_ref=self.recv.at[p, slot], send_sem=self.send_sem.at[p, j],
            recv_sem=self.recv_sem.at[p, slot], device_id=(self.s, to), device_id_type=MESH)

    def add(self, p, j):
        self.copy(p, j, j, self.t).wait_recv()
        self.part[p, j] = (self.part[p, j].astype(jnp.float32) + self.recv[p, j].astype(jnp.float32)).astype(jnp.bfloat16)

    def left(self, p, j):
        @pl.when(self.t > j)
        def _():
            @pl.when(self.t < self.m - 1)
            def _():
                self.add(p, j)

            self.sent(p, j - 1, j > 0)
            if p > 0 and j == 0:
                self.sent(p - 1, self.t - 1, True)
            self.copy(p, j, j, self.t - 1).start()

    def right(self, p, j):
        @pl.when(self.t < j)
        def _():
            @pl.when(self.t > 0)
            def _():
                self.add(p, j)

            self.sent(p, j + 1, j < self.m - 1)
            if p > 0 and j == self.m - 1:
                self.sent(p - 1, self.t + 1, True)
            self.copy(p, j, jnp.where(self.t + 1 == j, self.m, j), self.t + 1).start()

    def sent(self, p, j, some):
        if some:
            self.copy(p, j, j, self.t).wait_send()

    def step(self, p, k):
        self.left(p, k)
        self.right(p, self.m - 1 - k)

    def clear(self, p):
        @pl.when(self.t == self.m - 1)
        def _():
            self.recv[p, self.m - 1] = jnp.zeros(self.recv.shape[2:], self.recv.dtype)

        @pl.when(self.t == 0)
        def _():
            self.recv[p, self.m] = jnp.zeros(self.recv.shape[2:], self.recv.dtype)

    def total(self, p):
        @pl.when(self.t < self.m - 1)
        def _():
            self.copy(p, self.t, self.t, self.t).wait_recv()

        @pl.when(self.t > 0)
        def _():
            self.copy(p, self.t, self.m, self.t).wait_recv()

        f32 = jnp.float32
        return self.part[p, self.t].astype(f32) + (self.recv[p, self.t].astype(f32) + self.recv[p, self.m].astype(f32))

    def finish(self, p):
        @pl.when(self.t > 0)
        def _():
            self.copy(p, self.t - 1, 0, self.t).wait_send()

        @pl.when(self.t < self.m - 1)
        def _():
            self.copy(p, self.t + 1, 0, self.t).wait_send()


class LineGather:
    def __init__(self, buf, send_sem, recv_sem):
        self.buf, self.send_sem, self.recv_sem = buf, send_sem, recv_sem
        self.m = buf.shape[1]
        self.s, self.t = lax.axis_index("seq"), lax.axis_index("tp")

    def copy(self, p, j, way):
        ref = self.buf.at[p, j]
        return pltpu.make_async_remote_copy(
            src_ref=ref, dst_ref=ref, send_sem=self.send_sem.at[p, way, j], recv_sem=self.recv_sem.at[p, j],
            device_id=(self.s, self.t + (2 * way - 1)), device_id_type=MESH)

    def pass_on(self, p, j, way):
        @pl.when(self.t > 0 if way == 0 else self.t < self.m - 1)
        def _():
            self.copy(p, j, way).start()

    def start(self, p):
        self.pass_on(p, self.t, 0)
        self.pass_on(p, self.t, 1)

    def arrive(self, p, distance):
        @pl.when(self.t + distance < self.m)
        def _():
            self.copy(p, self.t + distance, 0).wait_recv()
            self.pass_on(p, self.t + distance, 0)

        @pl.when(self.t >= distance)
        def _():
            self.copy(p, self.t - distance, 1).wait_recv()
            self.pass_on(p, self.t - distance, 1)

    def finish(self, p):
        for j in range(self.m):
            @pl.when((self.t > 0) & (self.t <= j))
            def _(j=j):
                self.copy(p, j, 0).wait_send()

            @pl.when((self.t < self.m - 1) & (self.t >= j))
            def _(j=j):
                self.copy(p, j, 1).wait_send()


def line_sems(pieces):
    m = lax.axis_size("tp")
    return [pltpu.SemaphoreType.DMA((pieces, m)), pltpu.SemaphoreType.DMA((pieces, m + 1)),
            pltpu.SemaphoreType.DMA((pieces, 2, m)), pltpu.SemaphoreType.DMA((pieces, m))]


class Plan:
    def __init__(self):
        self.steps = []

    def at(self, time, step, *args):
        self.steps.append((time, len(self.steps), step, args))

    def run(self):
        for _, _, step, args in sorted(self.steps, key=lambda one: one[:2]):
            step(*args)


def attn_fwd_block(q_ref, kv_ref, out_ref, sum_ref, bias_ref, kv, rows, tile):
    scale = HEAD_SIZE ** -0.5 * LOG2E
    all_rows = q_ref.shape[1]
    for h in range(kv):
        cols = slice(h * HEAD_SIZE, (h + 1) * HEAD_SIZE)
        v_cols = slice((kv + h) * HEAD_SIZE, (kv + h + 1) * HEAD_SIZE)
        for start in range(0, all_rows, tile):
            at = start % rows
            n_keys = rows if bias_ref is None else at + tile
            scores = mm(q_ref[h, start:start + tile], kv_ref[:n_keys, cols], NT) * scale
            if bias_ref is not None:
                scores = scores + bias_ref[at:at + tile, :n_keys]
            weights = jnp.exp2(scores)
            part = weights[:, :HEAD_SIZE]
            for c in range(HEAD_SIZE, n_keys, HEAD_SIZE):
                part = part + weights[:, c:c + HEAD_SIZE]
            sum_ref[h, start:start + tile] += part
            out_ref[h, start:start + tile] += mm(weights.astype(jnp.bfloat16), kv_ref[:n_keys, v_cols])


def rms_inverse(values):
    return lax.rsqrt(jnp.mean(values * values, axis=-1, keepdims=True) + EPS)


def forward_kernel(tok_ref, wq_ref, wk_ref, wv_ref, gain_ref, cos_ref, sin_ref, qd_ref, kd_ref, o_ref, gate_ref,
                   norm_ref, proj_ref, q_ref, kv_ref, att_ref, lse_ref, gains_ref, w, o_all, gate_all,
                   inv, acc, total, bias, local_sem, *sems):
    f32, b16 = jnp.float32, jnp.bfloat16
    n, rows, _ = kv_ref.shape
    kv, all_rows, _ = q_ref.shape
    group = all_rows // rows
    me = lax.axis_index("seq")
    bits = seq_bits()
    tile = cut(rows)
    depth = w.shape[1]
    q_width, k_width = wq_ref.shape[1], wk_ref.shape[1]
    w_gather = SeqGather(w, sems[0], sems[1])
    gain_gather = SeqGather(gains_ref, sems[2], sems[3], halves=1)
    kv_gather = SeqGather(kv_ref, sems[4], sems[5])
    o_gather = SeqGather(o_all, sems[6], sems[7])
    gate_gather = SeqGather(gate_all, sems[8], sems[9])

    own = [pltpu.make_async_copy(wq_ref, w.at[me, :, pl.ds(0, q_width)], local_sem.at[0]),
           pltpu.make_async_copy(wk_ref, w.at[me, :, pl.ds(q_width, k_width)], local_sem.at[1]),
           pltpu.make_async_copy(wv_ref, w.at[me, :, pl.ds(q_width + k_width, k_width)], local_sem.at[2]),
           pltpu.make_async_copy(o_ref, o_all.at[me], local_sem.at[3]),
           pltpu.make_async_copy(gate_ref, gate_all.at[me], local_sem.at[4])]
    for copy in own:
        copy.start()
    gains_ref[me] = gain_ref[...]
    greet(True, False)
    for copy in own[:3]:
        copy.wait()
    w_gather.start(0)
    w_gather.start(1)
    gain_gather.start(0)

    @pl.loop(0, rows // tile)
    def _(i):
        at = pl.ds(i * tile, tile)
        inv[at] = rms_inverse(tok_ref[at].astype(f32))

    visible = (lax.broadcasted_iota(jnp.int32, (rows, rows), 1)
               <= lax.broadcasted_iota(jnp.int32, (rows, rows), 0)) & (qd_ref[...] == kd_ref[...])
    bias[...] = jnp.where(visible, 0.0, -1e30)
    for event in gain_gather.events():
        gain_gather.arrive(*event)

    def project(offset):
        source = toggled(me, offset, bits)
        cols = pl.ds(pl.multiple_of(source * depth, depth), depth)

        @pl.loop(0, rows // tile)
        def _(i):
            at = pl.ds(i * tile, tile)
            block = (tok_ref[at, cols].astype(f32) * inv[at] * gains_ref[source, 0:1, :depth]).astype(b16)
            norm_ref[at, cols] = block
            part = mm(block, w[source])
            if offset == 0:
                proj_ref[at] = part
            else:
                proj_ref[at] += part

    project(0)
    came = {}
    for half, offset in w_gather.events():
        w_gather.arrive(half, offset)
        came[offset] = came.get(offset, 0) + 1
        if came[offset] == 2:
            project(offset)

    gain_q, gain_k = gains_ref[0, 2:3, :HEAD_SIZE], gains_ref[0, 3:4, :HEAD_SIZE]
    for j in range(1, n):
        gain_q = gain_q + gains_ref[j, 2:3, :HEAD_SIZE]
        gain_k = gain_k + gains_ref[j, 3:4, :HEAD_SIZE]

    def rotated(at, first, gain):
        u = proj_ref[at, first:first + HEAD_SIZE]
        u = u * rms_inverse(u) * gain
        return (u * cos_ref[at] + pltpu.roll(u, HEAD_SIZE // 2, 1) * sin_ref[at]).astype(b16)

    @pl.loop(0, rows // tile)
    def _(i):
        at = pl.ds(i * tile, tile)
        for h in range(kv):
            kv_ref[me, at, h * HEAD_SIZE:(h + 1) * HEAD_SIZE] = rotated(at, q_width + h * HEAD_SIZE, gain_k)
        kv_ref[me, at, k_width:] = proj_ref[at, q_width + k_width:].astype(b16)

    kv_gather.start(0)
    kv_gather.start(1)

    @pl.loop(0, rows // tile)
    def _(i):
        at = pl.ds(i * tile, tile)
        for h in range(kv):
            for g in range(group):
                q_ref[h, pl.ds(g * rows + i * tile, tile)] = rotated(at, (h * group + g) * HEAD_SIZE, gain_q)

    acc[...] = jnp.zeros_like(acc)
    total[...] = jnp.zeros_like(total)
    attn_fwd_block(q_ref, kv_ref.at[me], acc.at[0], total.at[0], bias, kv, rows, tile)
    own[3].wait()
    own[4].wait()

    kv_steps = [[] for _ in range(n)]
    seen = set()
    order = kv_gather.events()
    offsets = sorted(range(1, n), key=lambda r: max(order.index((h, r)) for h in range(2)))
    taken = 0
    for k, offset in enumerate(offsets):
        need = max(order.index((h, offset)) for h in range(2)) + 1
        kv_steps[k] = order[taken:max(need, taken)]
        taken = max(need, taken)
    only_first = jnp.where(qd_ref[...] == 0, 1.0, 0.0)

    @pl.loop(0, n - 1)
    def _(k):
        source = 0
        for i, offset in enumerate(offsets):
            source = source + jnp.where(k == i, toggled(me, offset, bits), 0)

            @pl.when(k == i)
            def _(i=i):
                for event in kv_steps[i]:
                    kv_gather.arrive(*event)
                if i == n - 2:
                    for gather in (o_gather, gate_gather):
                        gather.start(0)
                        gather.start(1)

        @pl.when(source < me)
        def _():
            attn_fwd_block(q_ref, kv_ref.at[source], acc.at[1], total.at[1], None, kv, rows, tile)

    for gather in (o_gather, gate_gather):
        for event in gather.events():
            gather.arrive(*event)
    for h in range(kv):
        for g in range(group):
            for start in range(0, rows, tile):
                at = slice(g * rows + start, g * rows + start + tile)
                t = total[0, h, at] + total[1, h, at] * only_first[start:start + tile]
                out = acc[0, h, at] + acc[1, h, at] * only_first[start:start + tile]
                cols = slice((h * group + g) * HEAD_SIZE, (h * group + g + 1) * HEAD_SIZE)
                att_ref[start:start + tile, cols] = (out / jnp.sum(t, axis=1, keepdims=True)).astype(b16)
                lse_ref[h, :, at] = jnp.log2(jnp.sum(t.T, axis=0, keepdims=True))
    for gather in (w_gather, gain_gather, kv_gather, o_gather, gate_gather):
        gather.finish()


def forward_attention(tokens, q_weight, key_matrix, value_matrix, gains, cosines, sines, doc_column, doc_row, o_weight, gate_weight):
    n = lax.axis_size("seq")
    rows, width = tokens.shape
    depth, q_width = q_weight.shape
    k_width = key_matrix.shape[1]
    kv, group = k_width // HEAD_SIZE, q_width // k_width
    f32, b16 = jnp.float32, jnp.bfloat16
    wide = q_width + 2 * k_width
    heads = (kv, group * rows, HEAD_SIZE)
    out = [((rows, width), b16), ((rows, wide), f32), (heads, b16), ((n, rows, 2 * k_width), b16), ((rows, q_width), b16),
           ((kv, 1, group * rows), f32), ((n,) + gains.shape, f32), ((n, depth, wide), b16), ((n,) + o_weight.shape, b16), ((n,) + gate_weight.shape, b16)]
    sems = []
    for halves in (2, 1, 2, 2, 2):
        sems += gather_sems(halves)
    return pl.pallas_call(
        forward_kernel,
        out_shape=[jax.ShapeDtypeStruct(*one) for one in out],
        in_specs=[VM] + [ANY] * 3 + [VM] * 5 + [ANY] * 2,
        out_specs=[VM] * 8 + [ANY] * 2,
        scratch_shapes=[pltpu.VMEM((rows, 1), f32), pltpu.VMEM((2,) + heads, f32),
                        pltpu.VMEM((2,) + heads, f32), pltpu.VMEM((rows, rows), f32), pltpu.SemaphoreType.DMA((5,))] + sems,
        compiler_params=pltpu.CompilerParams(vmem_limit_bytes=VMEM_BYTES, collective_id=1, has_side_effects=True),
        name="forward_attention",
    )(tokens, q_weight, key_matrix, value_matrix, gains, cosines, sines, doc_column, doc_row, o_weight, gate_weight)


class SeqSum:
    def __init__(self, source, loc, near, far, sems):
        self.source, self.loc, self.near, self.far = source, loc, near, far
        self.load_sem, self.near_sem, self.far_sem = sems
        self.bits = seq_bits()
        self.count = 1 << (self.bits - 1)
        self.me, self.t = lax.axis_index("seq"), lax.axis_index("tp")
        self.half_rows = loc.shape[1] // 2

    def first(self, half, e):
        order = bit_order(half)[:-1]
        return min(order.index(b) for b in range(1, self.bits) if 2 * e >> b & 1)

    def load(self, e):
        return pltpu.make_async_copy(self.source(toggled(self.me, 2 * e, self.bits)), self.loc.at[e], self.load_sem.at[e])

    def cross(self, e):
        return pltpu.make_async_remote_copy(
            src_ref=self.source(toggled(self.me, 2 * e + 1, self.bits)), dst_ref=self.near.at[e],
            send_sem=self.near_sem.at[0, e], recv_sem=self.near_sem.at[1, e],
            device_id=(toggled(self.me, 1, self.bits), self.t), device_id_type=MESH)

    def begin(self):
        for e in reversed(range(self.count)):
            self.cross(e).start()
            self.load(e).start()

    def meet(self, e):
        self.load(e).wait()
        self.cross(e).wait_recv()
        self.loc[e] += self.near[e]
        for half in range(2):
            if e and self.first(half, e) == 0:
                self.hop(half, e).start()

    def hop(self, half, e):
        bit = bit_order(half)[self.first(half, e)]
        return pltpu.make_async_remote_copy(
            src_ref=self.loc.at[e, pl.ds(half * self.half_rows, self.half_rows)], dst_ref=self.far.at[half, e - 1],
            send_sem=self.far_sem.at[0, half, e - 1], recv_sem=self.far_sem.at[1, half, e - 1],
            device_id=(toggled(self.me, 1 << bit, self.bits), self.t), device_id_type=MESH)

    def arrive(self, half, e):
        place = self.first(half, e)
        to = (2 * e ^ 1 << bit_order(half)[place]) // 2
        self.hop(half, e).wait_recv()
        self.loc[to, half * self.half_rows:(half + 1) * self.half_rows] += self.far[half, e - 1]
        if to and self.first(half, to) == place + 1:
            self.hop(half, to).start()

    def rounds(self):
        found = [[] for _ in range(self.bits - 1)]
        for e in reversed(range(1, self.count)):
            for half in range(2):
                found[self.first(half, e)].append((half, e))
        return found

    def finish(self):
        for e in range(self.count):
            self.cross(e).wait_send()
            for half in range(2 if e else 0):
                self.hop(half, e).wait_send()


def sum_scratch(rows, columns):
    count = lax.axis_size("seq") // 2
    b16 = jnp.bfloat16
    return [pltpu.VMEM((count, rows, columns), b16), pltpu.VMEM((count, rows, columns), b16),
            pltpu.VMEM((2, max(count - 1, 1), rows // 2, columns), b16), pltpu.SemaphoreType.DMA((count,)),
            pltpu.SemaphoreType.DMA((2, count)), pltpu.SemaphoreType.DMA((2, 2, max(count - 1, 1)))]


SUM_SCRATCH = 6


def seq_sum(source, scratch):
    return SeqSum(source, *scratch[:3], scratch[3:])


def middle_kernel(att_ref, o_all, gate_all, up_ref, down_ref, tok_ref, cot_ref, gains_ref,
                  low_ref, after_grad_ref, mlp_ref, gain_out, grads_ref,
                  up_all, down_all, part, recv, norm_mid, act, gg, gu, after_own, tok_own, stage,
                  local_sem, stage_sem, *sems):
    f32, b16 = jnp.float32, jnp.bfloat16
    pieces, m, sub, width = cot_ref.shape
    n, depth, ff = gate_all.shape
    piece = m * sub
    me, t = lax.axis_index("seq"), lax.axis_index("tp")
    up_gather = SeqGather(up_all, sems[0], sems[1])
    down_gather = SeqGather(down_all, sems[2], sems[3])
    attn_sum = LineSum(part, recv, sems[4], sems[5])
    mid_sum = LineSum(part, recv, sems[8], sems[9])
    norm_gather = LineGather(norm_mid, sems[6], sems[7])
    low_gather = LineGather(low_ref, sems[10], sems[11])

    own = [pltpu.make_async_copy(up_ref, up_all.at[me], local_sem.at[0]),
           pltpu.make_async_copy(down_ref, down_all.at[me], local_sem.at[1])]
    own += [pltpu.make_async_copy(tok_ref.at[p, t], tok_own.at[p], local_sem.at[2 + p]) for p in range(pieces)]
    for copy in own:
        copy.start()
    greet(True, True)
    for copy in own:
        copy.wait()
    for half in range(2):
        up_gather.start(half)
    for p in range(pieces):
        attn_sum.clear(p)
    gain_out[...] = jnp.zeros_like(gain_out)
    plan = Plan()

    def mlp_gain(j):
        return gains_ref[j, 1:2, :depth]

    def project(p):
        rows = att_ref[p * piece:(p + 1) * piece]
        for j in range(n):
            block = mm(rows, o_all[j]).astype(b16)
            part[p, :, :, j * depth:(j + 1) * depth] = block.reshape(m, sub, depth)

    def normalise(p):
        after = tok_own[p].astype(f32) + attn_sum.total(p)
        after_own[p] = after
        normed = after * rms_inverse(after)
        for j in range(n):
            cols = slice(j * depth, (j + 1) * depth)
            norm_mid[p, t, :, cols] = (normed[:, cols] * mlp_gain(j)).astype(b16)
        norm_gather.start(p)

    def hidden(p, first, count):
        rows = slice(p * piece, (p + 1) * piece)
        cols = slice(first, first + count)
        x = norm_mid[p].reshape(piece, width)
        gate = mm(x, gate_all[:, :, cols].reshape(width, count))
        up = mm(x, up_all[:, :, cols].reshape(width, count))
        grad = mm(cot_ref[p, :, :, :depth].reshape(piece, depth), down_all[0, cols], NT)
        for j in range(1, n):
            c = cot_ref[p, :, :, j * depth:(j + 1) * depth].reshape(piece, depth)
            grad = grad + mm(c, down_all[j, cols], NT)
        sig = jax.nn.sigmoid(gate)
        silu = gate * sig
        act[rows, cols] = (silu * up).astype(b16)
        gg[rows, cols] = (grad * up * sig * (1.0 + gate * (1.0 - sig))).astype(b16)
        gu[rows, cols] = (grad * silu).astype(b16)

    def mid(p, first, count):
        rows = slice(p * piece, (p + 1) * piece)
        for j in range(first, first + count):
            block = mm(gg[rows], gate_all[j], NT) + mm(gu[rows], up_all[j], NT)
            part[p, :, :, j * depth:(j + 1) * depth] = block.astype(b16).reshape(m, sub, depth)

    def mlp_out(p):
        rows = slice(p * piece, (p + 1) * piece)
        for j in range(n):
            block = mm(act[rows], down_all[j]).astype(b16)
            mlp_ref[p, :, :, j * depth:(j + 1) * depth] = block.reshape(m, sub, depth)
        mlp_ref[p, t] = (mlp_ref[p, t].astype(f32) + after_own[p]).astype(b16)

    def mid_back(p):
        grad = mid_sum.total(p)
        after = after_own[p]
        inverse = rms_inverse(after)
        normed = after * inverse
        mean = 0.0
        for j in range(n):
            cols = slice(j * depth, (j + 1) * depth)
            gain_out[:, cols] += jnp.sum(grad[:, cols] * normed[:, cols], axis=0, keepdims=True)
            mean = mean + jnp.sum(grad[:, cols] * mlp_gain(j) * normed[:, cols], axis=1, keepdims=True)
        mean = mean * (1.0 / width)
        for j in range(n):
            cols = slice(j * depth, (j + 1) * depth)
            back = inverse * (grad[:, cols] * mlp_gain(j) - normed[:, cols] * mean)
            back = back + cot_ref[p, t, :, cols].astype(f32)
            after_grad_ref[p, :, cols] = back
            low_ref[p, t, :, cols] = back.astype(b16)
        low_gather.start(p)

    def staged(j, slot):
        return pltpu.make_async_copy(stage.at[slot], grads_ref.at[j], stage_sem.at[slot])

    def weight_grads(j):
        slot = j % 2
        if j >= 2:
            staged(j - 2, slot).wait()
        cols = slice(j * depth, (j + 1) * depth)
        x = cot_ref[:, :, :, cols].reshape(pieces * piece, depth)
        stage[slot, 0] = mm(x, act[...], TN).astype(b16)
        x = norm_mid[:, :, :, cols].reshape(pieces * piece, depth)
        stage[slot, 1] = mm(x, gg[...], TN).astype(b16)
        stage[slot, 2] = mm(x, gu[...], TN).astype(b16)
        staged(j, slot).start()

    hop = 6.0
    ready = []
    for p in range(pieces):
        plan.at(2.0 * p, project, p)
        start = 4.0 + 3 * hop * p
        for k in range(m - 1):
            plan.at(start + hop * k, attn_sum.step, p, k)
        start += hop * m
        plan.at(start, normalise, p)
        for d in range(1, m):
            plan.at(start + hop * d, norm_gather.arrive, p, d)
        ready.append(start + hop * m - 3.0)

    def due(gather, event, base):
        half, offset = event
        order = bit_order(half)
        steps = sum(2 ** order.index(b) for b in range(1, gather.bits) if offset >> b & 1)
        return base + 9.0 * max(steps, 0.2)

    def begin_down():
        for half in range(2):
            down_gather.start(half)

    for event in up_gather.events():
        plan.at(due(up_gather, event, 3.0), up_gather.arrive, *event)
    plan.at(22.0, begin_down)
    for event in down_gather.events():
        plan.at(due(down_gather, event, 29.0), down_gather.arrive, *event)

    chunk = cut(ff, 512)
    chunks = ff // chunk
    clock = 58.0
    for p in range(pieces):
        clock = max(clock, ready[p])
        for c in range(chunks):
            plan.at(clock, hidden, p, c * chunk, chunk)
            clock += 2.4

        def reuse(p=p):
            if p == pieces - 1:
                attn_sum.finish(p)
            mid_sum.clear(p)

        plan.at(clock, reuse)
        for half in range(2):
            plan.at(clock, mid, p, half * (n // 2), n // 2)
            clock += 2.2
        start = max(clock, 70.0 + 3 * hop * p)
        for k in range(m - 1):
            plan.at(start + hop * k, mid_sum.step, p, k)
        start += hop * m
        plan.at(start, mid_back, p)
        for d in range(1, m):
            plan.at(start + hop * d, low_gather.arrive, p, d)
    for j in range(n):
        plan.at(clock, weight_grads, j)
        clock += 3.5
    for p in range(pieces):
        plan.at(clock, mlp_out, p)
        clock += 2.2
    plan.run()

    for j in range(n - 2, n):
        staged(j, j % 2).wait()
    up_gather.finish()
    down_gather.finish()
    mid_sum.finish(pieces - 1)
    for p in range(pieces):
        norm_gather.finish(p)
        low_gather.finish(p)


def middle(attended, o_all, gate_all, up_weight, down_weight, tokens, cotangent, gains):
    f32, b16 = jnp.float32, jnp.bfloat16
    pieces, m, sub, width = tokens.shape
    n, depth, ff = gate_all.shape
    rows = pieces * m * sub
    blocks = tokens.shape
    out = [(blocks, b16), ((pieces, sub, width), f32), (blocks, b16), ((1, width), f32), ((n, 3, depth, ff), b16)]
    return pl.pallas_call(
        middle_kernel,
        out_shape=[jax.ShapeDtypeStruct(*one) for one in out],
        in_specs=[VM] * 3 + [ANY] * 3 + [VM] * 2,
        out_specs=[VM] * 4 + [ANY],
        scratch_shapes=[pltpu.VMEM((n, depth, ff), b16), pltpu.VMEM((n, ff, depth), b16), pltpu.VMEM(blocks, b16),
                        pltpu.VMEM((pieces, m + 1, sub, width), b16), pltpu.VMEM(blocks, b16),
                        pltpu.VMEM((rows, ff), b16), pltpu.VMEM((rows, ff), b16), pltpu.VMEM((rows, ff), b16),
                        pltpu.VMEM((pieces, sub, width), f32), pltpu.VMEM((pieces, sub, width), b16),
                        pltpu.VMEM((2, 3, depth, ff), b16), pltpu.SemaphoreType.DMA((2 + pieces,)),
                        pltpu.SemaphoreType.DMA((2,))]
        + gather_sems() + gather_sems() + line_sems(pieces) + line_sems(pieces),
        compiler_params=pltpu.CompilerParams(vmem_limit_bytes=VMEM_BYTES, collective_id=2, has_side_effects=True),
        name="middle",
    )(attended, o_all, gate_all, up_weight, down_weight, tokens, cotangent, gains)


def attn_bwd_block(h, q_ref, do_ref, lse_ref, delta_ref, kv_ref, dq_ref, dk_ref, dv_ref, bias_ref, kv, rows, tile):
    scale = HEAD_SIZE ** -0.5 * LOG2E
    all_rows = q_ref.shape[1]
    k_cols = pl.ds(pl.multiple_of(h * HEAD_SIZE, HEAD_SIZE), HEAD_SIZE)
    v_cols = pl.ds(pl.multiple_of((kv + h) * HEAD_SIZE, HEAD_SIZE), HEAD_SIZE)
    dk_ref[...] = jnp.zeros_like(dk_ref)
    dv_ref[...] = jnp.zeros_like(dv_ref)
    for start in range(0, all_rows, tile):
        at = start % rows
        n_keys = rows if bias_ref is None else at + tile
        q = q_ref[h, start:start + tile]
        do = do_ref[h, start:start + tile]
        k = kv_ref[:n_keys, k_cols]
        scores = mm(k, q, NT) * scale - lse_ref[h, :, start:start + tile]
        if bias_ref is not None:
            scores = scores + bias_ref[:n_keys, at:at + tile]
        probs = jnp.exp2(scores)
        grad = mm(kv_ref[:n_keys, v_cols], do, NT)
        grad = (probs * (grad - delta_ref[h, :, start:start + tile])).astype(jnp.bfloat16)
        dv_ref[:n_keys] += mm(probs.astype(jnp.bfloat16), do)
        dk_ref[:n_keys] += mm(grad, q)
        dq_ref[h, start:start + tile] += mm(grad, k, TN)


def backward_kernel(q_ref, low_ref, o_all, att_ref, lse_ref, kv_ref, kd_ref, qdr_ref, grads_ref,
                    dq_ref, dkv_ref, gate_out, up_out, o_grads, do, delta, lse_off, dk, dv, bias, *scratch):
    f32, b16 = jnp.float32, jnp.bfloat16
    kv, all_rows, _ = q_ref.shape
    n, rows, _ = kv_ref.shape
    group = all_rows // rows
    depth = o_all.shape[2]
    me = lax.axis_index("seq")
    tile = cut(rows)
    scale = HEAD_SIZE ** -0.5
    gate_sum = seq_sum(lambda j: grads_ref.at[j, 1], scratch[:SUM_SCRATCH])
    up_sum = seq_sum(lambda j: grads_ref.at[j, 2], scratch[SUM_SCRATCH:])

    greet(True, False)
    gate_sum.begin()
    dq_ref[...] = jnp.zeros_like(dq_ref)
    off = jnp.where(qdr_ref[...] == 0, 0.0, 1e30)
    visible = (lax.broadcasted_iota(jnp.int32, (rows, rows), 0)
               <= lax.broadcasted_iota(jnp.int32, (rows, rows), 1)) & (kd_ref[...] == qdr_ref[...])
    bias[...] = jnp.where(visible, 0.0, -1e30)
    for start in range(0, rows, tile):
        grad = mm(low_ref[start:start + tile, :depth], o_all[0], NT)
        for j in range(1, n):
            grad = grad + mm(low_ref[start:start + tile, j * depth:(j + 1) * depth], o_all[j], NT)
        grad = grad.astype(b16)
        for h in range(kv):
            for g in range(group):
                cols = slice((h * group + g) * HEAD_SIZE, (h * group + g + 1) * HEAD_SIZE)
                at = slice(g * rows + start, g * rows + start + tile)
                part = grad[:, cols]
                do[h, at] = part
                prod = part.astype(f32) * att_ref[start:start + tile, cols].astype(f32)
                delta[h, :, at] = jnp.sum(prod.T, axis=0, keepdims=True)
    for j in range(n):
        o_grads[j] = mm(low_ref[:, j * depth:(j + 1) * depth], att_ref[...], TN).astype(b16)
    for h in range(kv):
        for g in range(group):
            at = slice(g * rows, (g + 1) * rows)
            lse_off[h, :, at] = lse_ref[h, :, at] + off

    def keep(j, h):
        k_cols = pl.ds(pl.multiple_of(h * HEAD_SIZE, HEAD_SIZE), HEAD_SIZE)
        v_cols = pl.ds(pl.multiple_of((kv + h) * HEAD_SIZE, HEAD_SIZE), HEAD_SIZE)
        dkv_ref[j, :, k_cols] = (dk[...] * scale).astype(b16)
        dkv_ref[j, :, v_cols] = dv[...].astype(b16)

    @pl.loop(0, kv)
    def _(h):
        attn_bwd_block(h, q_ref, do, lse_ref, delta, kv_ref.at[me], dq_ref, dk, dv, bias, kv, rows, tile)
        keep(me, h)

    steps = n * kv
    events = [[] for _ in range(steps)]

    def at_time(time, step, *args):
        events[min(int(time / 3.8), steps - 1)].append((step, args))

    def plan_sum(one, base, share):
        for e in reversed(range(one.count)):
            at_time(base, one.meet, e)
        for k, found in enumerate(one.rounds()):
            for event in found:
                at_time(base + share * 18.0 * (2.0 - 0.5 ** k), one.arrive, *event)

    plan_sum(gate_sum, 0.0, 1.0)
    at_time(4.0, up_sum.begin)
    plan_sum(up_sum, 15.0, 1.0)

    @pl.loop(0, steps)
    def _(i):
        for k in range(steps):
            if events[k]:
                @pl.when(i == k)
                def _(k=k):
                    for step, args in events[k]:
                        step(*args)

        j, h = i // kv, i % kv

        @pl.when(j < me)
        def _():
            attn_bwd_block(h, q_ref, do, lse_off, delta, kv_ref.at[j], dq_ref, dk, dv, None, kv, rows, tile)
            keep(j, h)

    @pl.loop(me + 1, n)
    def _(j):
        dkv_ref[j] = jnp.zeros(dkv_ref.shape[1:], b16)

    dq_ref[...] *= scale
    gate_out[...] = gate_sum.loc[0].astype(f32)
    up_out[...] = up_sum.loc[0].astype(f32)
    gate_sum.finish()
    up_sum.finish()


def attention_backward(queries, low, o_all, attended, lse, all_kv, doc_column, doc_row, grads):
    f32, b16 = jnp.float32, jnp.bfloat16
    kv, all_rows, _ = queries.shape
    n, rows, _ = all_kv.shape
    _, _, depth, ff = grads.shape
    out = [(queries.shape, f32), (all_kv.shape, b16), ((depth, ff), f32), ((depth, ff), f32),
           ((n, depth, attended.shape[1]), b16)]
    return pl.pallas_call(
        backward_kernel,
        out_shape=[jax.ShapeDtypeStruct(*one) for one in out],
        in_specs=[VM] * 8 + [ANY],
        out_specs=[VM] * 5,
        scratch_shapes=[pltpu.VMEM(queries.shape, b16), pltpu.VMEM((kv, 1, all_rows), f32), pltpu.VMEM((kv, 1, all_rows), f32),
                        pltpu.VMEM((rows, HEAD_SIZE), f32), pltpu.VMEM((rows, HEAD_SIZE), f32), pltpu.VMEM((rows, rows), f32)]
        + sum_scratch(depth, ff) + sum_scratch(depth, ff),
        compiler_params=pltpu.CompilerParams(vmem_limit_bytes=VMEM_BYTES, collective_id=3, has_side_effects=True),
        name="attention_backward",
    )(queries, low, o_all, attended, lse, all_kv, doc_column, doc_row, grads)


def final_kernel(dq_ref, proj_ref, norm_ref, w_ref, cos_ref, sin_ref, gains_ref, after_ref, mlp_gain_ref,
                 dkv_ref, grads_ref, o_grads_ref, tok_ref,
                 buf, down_out, o_out, q_out, k_out, v_out, gain_out,
                 dproj, part, recv, tok_own, w_grads, gain_seq, gain_line, local_sem, *scratch):
    f32, b16 = jnp.float32, jnp.bfloat16
    pieces, m, sub, width = part.shape
    n, depth, wide = w_ref.shape
    kv, all_rows, _ = dq_ref.shape
    rows = norm_ref.shape[0]
    group = all_rows // rows
    q_width, k_width = kv * group * HEAD_SIZE, kv * HEAD_SIZE
    piece = m * sub
    me, t = lax.axis_index("seq"), lax.axis_index("tp")
    tile = cut(rows)
    kv_sum = seq_sum(lambda j: dkv_ref.at[j], scratch[:6])
    down_sum = seq_sum(lambda j: grads_ref.at[j, 0], scratch[6:12])
    o_sum = seq_sum(lambda j: o_grads_ref.at[j], scratch[12:18])
    w_sum = seq_sum(lambda j: w_grads.at[j], scratch[18:24])
    in_sum = LineSum(part, recv, scratch[24], scratch[25])
    out_gather = LineGather(buf, scratch[26], scratch[27])
    gain_gather = SeqGather(gain_seq, scratch[28], scratch[29], halves=1)
    gain_total = LineGather(gain_line, scratch[30], scratch[31])

    own = [pltpu.make_async_copy(tok_ref.at[p, t], tok_own.at[p], local_sem.at[p]) for p in range(pieces)]
    for copy in own:
        copy.start()
    greet(True, True)
    kv_sum.begin()
    gain_q, gain_k = gains_ref[0, 2:3, :HEAD_SIZE], gains_ref[0, 3:4, :HEAD_SIZE]
    for j in range(1, n):
        gain_q = gain_q + gains_ref[j, 2:3, :HEAD_SIZE]
        gain_k = gain_k + gains_ref[j, 3:4, :HEAD_SIZE]
    gain_seq[me] = jnp.zeros(gain_seq.shape[1:], f32)
    gain_seq[me, 1:2] = mlp_gain_ref[...]
    for p in range(pieces):
        in_sum.clear(p)
    for copy in own:
        copy.wait()
    plan = Plan()

    def head_back(grad, at, first, gain):
        e = grad * cos_ref[at] - pltpu.roll(grad, HEAD_SIZE // 2, 1) * sin_ref[at]
        u = proj_ref[at, first:first + HEAD_SIZE]
        inverse = rms_inverse(u)
        normed = u * inverse
        scaled = e * gain
        back = inverse * (scaled - normed * jnp.mean(scaled * normed, axis=-1, keepdims=True))
        dproj[at, first:first + HEAD_SIZE] = back.astype(b16)
        return jnp.sum(e * normed, axis=0, keepdims=True)

    def queries_back(h, g):
        terms = jnp.zeros((1, HEAD_SIZE), f32)
        for start in range(0, rows, tile):
            grad = dq_ref[h, g * rows + start:g * rows + start + tile]
            terms += head_back(grad, slice(start, start + tile), (h * group + g) * HEAD_SIZE, gain_q)
        gain_seq[me, 2:3, :HEAD_SIZE] += terms

    def keys_back():
        for h in range(kv):
            cols = slice(h * HEAD_SIZE, (h + 1) * HEAD_SIZE)
            terms = jnp.zeros((1, HEAD_SIZE), f32)
            for start in range(0, rows, tile):
                at = slice(start, start + tile)
                terms += head_back(kv_sum.loc[0, at, cols].astype(f32), at, q_width + h * HEAD_SIZE, gain_k)
            gain_seq[me, 3:4, :HEAD_SIZE] += terms
        dproj[:, q_width + k_width:] = kv_sum.loc[0, :, k_width:]

    def in_part(p):
        for j in range(n):
            block = mm(dproj[p * piece:(p + 1) * piece], w_ref[j], NT)
            part[p, :, :, j * depth:(j + 1) * depth] = block.astype(b16).reshape(m, sub, depth)

    def weight_grads(j):
        w_grads[j] = mm(norm_ref[:, j * depth:(j + 1) * depth], dproj[...], TN).astype(b16)

    def norm_back(p):
        grad = in_sum.total(p)
        tok = tok_own[p].astype(f32)
        inverse = rms_inverse(tok)
        normed = tok * inverse
        mean = 0.0
        for j in range(n):
            cols = slice(j * depth, (j + 1) * depth)
            gain_seq[me, 0:1, cols] += jnp.sum(grad[:, cols] * normed[:, cols], axis=0, keepdims=True)
            mean = mean + jnp.sum(grad[:, cols] * gains_ref[j, 0:1, :depth] * normed[:, cols], axis=1, keepdims=True)
        mean = mean * (1.0 / width)
        for j in range(n):
            cols = slice(j * depth, (j + 1) * depth)
            back = inverse * (grad[:, cols] * gains_ref[j, 0:1, :depth] - normed[:, cols] * mean)
            buf[p, t, :, cols] = (after_ref[p, :, cols] + back).astype(b16)
        out_gather.start(p)

    def plan_sum(one, base, length):
        for e in reversed(range(one.count)):
            plan.at(base, one.meet, e)
        for k, found in enumerate(one.rounds()):
            for event in found:
                plan.at(base + length * (2.0 - 0.5 ** k), one.arrive, *event)

    for h in range(kv):
        for g in range(group):
            plan.at(1.0, queries_back, h, g)
    plan_sum(kv_sum, 7.0, 18.0)
    plan.at(33.0, down_sum.begin)
    plan.at(33.5, o_sum.begin)
    plan.at(43.5, keys_back)
    clock = 44.0
    hop = 8.0
    last = 0.0
    for p in range(pieces):
        plan.at(clock, in_part, p)
        clock += 2.2
        start = 47.0 + 3 * hop * p
        for k in range(m - 1):
            plan.at(start + hop * k, in_sum.step, p, k)
        start += hop * (m - 1) + 1
        plan.at(start, norm_back, p)
        for d in range(1, m):
            last = start + hop * d
            plan.at(last, out_gather.arrive, p, d)
    for j in range(n):
        plan.at(50.0 + 0.8 * j, weight_grads, j)
    plan.at(57.0, w_sum.begin)
    plan_sum(down_sum, 48.0, 18.0)
    plan_sum(o_sum, 49.0, 18.0)
    plan_sum(w_sum, 76.0, 20.0)
    gain_time = last - 3 * hop + 0.5
    plan.at(gain_time, gain_gather.start, 0)
    for k, event in enumerate(gain_gather.events()):
        plan.at(gain_time + 1.0 + 0.5 * k, gain_gather.arrive, *event)

    def over_tp():
        total = gain_seq[0]
        for j in range(1, n):
            total = total + gain_seq[j]
        gain_line[0, t] = total
        gain_total.start(0)

    plan.at(gain_time + 1.0 + 0.5 * n, over_tp)
    for d in range(1, m):
        plan.at(gain_time + 2.0 + 0.5 * n + 2.0 * d, gain_total.arrive, 0, d)
    plan.run()

    total = gain_line[0, 0]
    for j in range(1, m):
        total = total + gain_line[0, j]
    gain_out[...] = total
    down_out[...] = down_sum.loc[0].astype(f32).T
    o_out[...] = o_sum.loc[0].astype(f32).T
    q_out[...] = w_sum.loc[0, :, :q_width].astype(f32)
    k_out[...] = w_sum.loc[0, :, q_width:q_width + k_width].astype(f32)
    v_out[...] = w_sum.loc[0, :, q_width + k_width:].astype(f32)
    for one in (kv_sum, down_sum, o_sum, w_sum, gain_gather):
        one.finish()
    in_sum.finish(pieces - 1)
    for p in range(pieces):
        out_gather.finish(p)
    gain_total.finish(0)


def final(grad_queries, projected, normalized, w_all, cosines, sines, gains, after_grad, mlp_gain, grad_kv, grads, o_grads, tokens):
    f32, b16 = jnp.float32, jnp.bfloat16
    pieces, m, sub, width = tokens.shape
    n, depth, wide = w_all.shape
    kv, all_rows, _ = grad_queries.shape
    rows, k_width = normalized.shape[0], kv * HEAD_SIZE
    q_width = wide - 2 * k_width
    ff = grads.shape[3]
    out = [(tokens.shape, b16), ((ff, depth), f32), ((q_width, depth), f32), ((depth, q_width), f32), ((depth, k_width), f32),
           ((depth, k_width), f32), ((8, width), f32)]
    return pl.pallas_call(
        final_kernel,
        out_shape=[jax.ShapeDtypeStruct(*one) for one in out],
        in_specs=[VM] * 9 + [ANY] * 4,
        out_specs=[VM] * 7,
        scratch_shapes=[pltpu.VMEM((rows, wide), b16), pltpu.VMEM(tokens.shape, b16),
                        pltpu.VMEM((pieces, m + 1, sub, width), b16), pltpu.VMEM((pieces, sub, width), b16),
                        pltpu.VMEM((n, depth, wide), b16), pltpu.VMEM((n, 8, width), f32), pltpu.VMEM((1, m, 8, width), f32),
                        pltpu.SemaphoreType.DMA((pieces,))]
        + sum_scratch(rows, 2 * k_width) + sum_scratch(depth, ff) + sum_scratch(depth, q_width) + sum_scratch(depth, wide)
        + line_sems(pieces) + gather_sems(1) + line_sems(1)[2:],
        compiler_params=pltpu.CompilerParams(vmem_limit_bytes=VMEM_BYTES, collective_id=4, has_side_effects=True),
        name="final",
    )(grad_queries, projected, normalized, w_all, cosines, sines, gains, after_grad, mlp_gain, grad_kv, grads, o_grads, tokens)


def pack_gains(attn_gain, mlp_gain, query_gain, key_gain):
    width = max(attn_gain.shape[0], HEAD_SIZE)
    place = lax.axis_index("seq") * query_gain.shape[0]

    def placed(gain):
        return lax.dynamic_update_slice(jnp.zeros((width,), jnp.float32), gain.astype(jnp.float32), (place,))

    def padded(gain):
        return jnp.pad(gain.astype(jnp.float32), (0, width - gain.shape[0]))

    lines = [padded(attn_gain), padded(mlp_gain), placed(query_gain), placed(key_gain)]
    return jnp.stack(lines + [jnp.zeros((width,), jnp.float32)] * 4)


def norm_rows(values, gain_vec):
    return values * lax.rsqrt(jnp.mean(values * values, axis=-1, keepdims=True) + EPS) * gain_vec


def norm_back(values, gain_vec, grad_out):
    inverse = lax.rsqrt(jnp.mean(values * values, axis=-1, keepdims=True) + EPS)
    normed = values * inverse
    scaled = grad_out * gain_vec
    grad_in = inverse * (scaled - normed * jnp.mean(scaled * normed, axis=-1, keepdims=True))
    return (grad_in, grad_out * normed)


def rope_tables(positions, head_dim):
    half_dim = head_dim // 2
    frequency = BASE ** (-2.0 * jnp.arange(half_dim, dtype=jnp.float32) / head_dim)
    angles = positions.astype(jnp.float32)[:, None] * frequency[None, :]
    return (jnp.cos(angles)[:, None, :], jnp.sin(angles)[:, None, :])


def rotate(values, cosines, sine_values, direction):
    half_dim = values.shape[-1] // 2
    lower_half = values[..., :half_dim]
    upper_half = values[..., half_dim:]
    signed = sine_values * direction
    return jnp.concatenate(
        [lower_half * cosines - upper_half * signed, upper_half * cosines + lower_half * signed],
        axis=-1,
    )


def per_device(
    tokens,
    q_weight,
    key_matrix,
    value_matrix,
    o_weight,
    gate_weight,
    up_weight,
    down_weight,
    attn_gain,
    mlp_gain,
    query_gain,
    key_gain,
    positions,
    seq_ids,
    cotangent,
):
    f32 = jnp.float32
    b16 = jnp.bfloat16
    local_rows = tokens.shape[0]
    q_local = q_weight.shape[1] // HEAD_SIZE
    kv_local = key_matrix.shape[1] // HEAD_SIZE
    heads_per_group = q_local // kv_local
    share_rows = local_rows // lax.axis_size("tp")
    share_start = lax.axis_index("tp") * share_rows
    s = lax.axis_index("seq")
    own_docs = lax.dynamic_slice_in_dim(seq_ids, s * local_rows, local_rows)
    doc_column, doc_row = own_docs[:, None], own_docs[None, :]
    seq_count = lax.axis_size("seq")
    gains = pack_gains(attn_gain, mlp_gain, query_gain, key_gain)
    cosines, sine_values = rope_tables(positions, HEAD_SIZE)
    cos_wide = jnp.concatenate([cosines, cosines], axis=-1).reshape(local_rows, HEAD_SIZE)
    sin_wide = jnp.concatenate([-sine_values, sine_values], axis=-1).reshape(local_rows, HEAD_SIZE)
    (normalized_input, projected, queries_h, all_kv, attended_low, lse, all_gains, w_all, o_all, gate_all) = forward_attention(
        tokens, q_weight, key_matrix, value_matrix, gains, cos_wide, sin_wide, doc_column, doc_row, o_weight, gate_weight)
    model = tokens.shape[1]
    ff = gate_weight.shape[1]
    q_width, k_width = q_local * HEAD_SIZE, kv_local * HEAD_SIZE
    tp_count = lax.axis_size("tp")
    sub = math.gcd(local_rows // tp_count, 64)
    while local_rows // tp_count // sub > 3:
        sub *= 2
    split = (local_rows // tp_count // sub, tp_count, sub, model)
    low_b, after_grad_own, mlp_part, mlp_gain_own, mlp_grads = middle(
        attended_low, o_all, gate_all, up_weight, down_weight, tokens.reshape(split), cotangent.reshape(split), all_gains)
    grad_after_low = low_b.reshape(local_rows, model)
    layer_out = lax.psum(mlp_part, "tp").reshape(local_rows, model)

    grad_query_h, grad_kv, grad_gate_w, grad_up_w, o_grads = attention_backward(
        queries_h, grad_after_low, o_all, attended_low, lse, all_kv, doc_column, doc_row, mlp_grads)
    grad_tokens, grad_down, grad_o_w, grad_q_w, grad_k_w, grad_v_w, gain_sums = final(
        grad_query_h, projected, normalized_input, w_all, cos_wide, sin_wide, all_gains, after_grad_own, mlp_gain_own,
        grad_kv, mlp_grads, o_grads, tokens.reshape(split))

    def own_part(line, width):
        count = width // seq_count
        return lax.dynamic_slice_in_dim(gain_sums[line], s * count, count)

    return (
        layer_out,
        grad_tokens.reshape(local_rows, model).astype(f32),
        grad_q_w,
        grad_k_w,
        grad_v_w,
        grad_o_w,
        grad_gate_w,
        grad_up_w,
        grad_down,
        own_part(0, model),
        own_part(1, model),
        own_part(2, HEAD_SIZE),
        own_part(3, HEAD_SIZE),
    )


def solution(mesh):
    placed = (
        P("seq", None),
        P("seq", "tp"),
        P("seq", "tp"),
        P("seq", "tp"),
        P("tp", "seq"),
        P("seq", "tp"),
        P("seq", "tp"),
        P("tp", "seq"),
        P("seq"),
        P("seq"),
        P("seq"),
        P("seq"),
        P("seq"),
        P(),
        P("seq", None),
    )
    return jax.shard_map(
        per_device,
        mesh=mesh,
        in_specs=placed,
        out_specs=(
            P("seq", None),
            P("seq", None),
            P("seq", "tp"),
            P("seq", "tp"),
            P("seq", "tp"),
            P("tp", "seq"),
            P("seq", "tp"),
            P("seq", "tp"),
            P("tp", "seq"),
            P("seq"),
            P("seq"),
            P("seq"),
            P("seq"),
        ),
        check_vma=False,
    )
```

```python
import functools
import math

import jax
import jax.numpy as jnp
from jax import lax
from jax.experimental import pallas as pl
from jax.experimental.pallas import tpu as pltpu

from jax.sharding import PartitionSpec as P

HEAD_SIZE = 128
EPS = 1e-06
BASE = 1000000.0
LOG2E = 1.4426950408889634
VMEM_BYTES = 62 << 20
NT = (((1,), (1,)), ((), ()))
TN = (((0,), (0,)), ((), ()))


def mm(a, b, dims=(((1,), (0,)), ((), ()))):
    return lax.dot_general(a, b, dims, preferred_element_type=jnp.float32)


def cut(rows, most=256):
    return math.gcd(rows, most)


MESH = pl.DeviceIdType.MESH
ANY = pl.BlockSpec(memory_space=pl.ANY)
VM = pl.BlockSpec(memory_space=pltpu.VMEM)


def bit_of(index, bit):
    return lax.rem(index // (1 << bit), 2)


def toggled(index, offset, bits):
    for bit in range(bits):
        if offset >> bit & 1:
            index = index + (1 - 2 * bit_of(index, bit)) * (1 << bit)
    return index


def seq_bits():
    return lax.axis_size("seq").bit_length() - 1


def bit_order(half):
    outer = list(range(1, seq_bits()))
    return (outer if half == 0 else outer[::-1]) + [0]


def last_bit(half, offset):
    return [b for b in bit_order(half) if offset >> b & 1][-1]


def greet(over_seq, over_tp):
    barrier = pltpu.get_barrier_semaphore()
    s, t, count = lax.axis_index("seq"), lax.axis_index("tp"), lax.axis_size("tp")
    expected = 0
    if over_seq:
        for bit in range(seq_bits()):
            pl.semaphore_signal(barrier, inc=1, device_id=(toggled(s, 1 << bit, seq_bits()), t), device_id_type=MESH)
        expected = seq_bits()
    if over_tp == "all":
        for j in range(count):
            @pl.when(t != j)
            def _(j=j):
                pl.semaphore_signal(barrier, inc=1, device_id=(s, j), device_id_type=MESH)
        expected = expected + count - 1
    elif over_tp:
        @pl.when(t > 0)
        def _():
            pl.semaphore_signal(barrier, inc=1, device_id=(s, t - 1), device_id_type=MESH)

        @pl.when(t < count - 1)
        def _():
            pl.semaphore_signal(barrier, inc=1, device_id=(s, t + 1), device_id_type=MESH)

        expected = expected + jnp.where(t > 0, 1, 0) + jnp.where(t < count - 1, 1, 0)
    pl.semaphore_wait(barrier, expected)


class SeqGather:
    def __init__(self, buf, send, recv, halves=2):
        self.buf, self.send, self.recv, self.halves = buf, send, recv, halves
        self.bits = seq_bits()
        self.n = 1 << self.bits
        self.me, self.t = lax.axis_index("seq"), lax.axis_index("tp")

    def block(self, half, offset):
        rows = self.buf.shape[1] // self.halves
        return self.buf.at[toggled(self.me, offset, self.bits), pl.ds(half * rows, rows)]

    def copy(self, half, offset):
        bit = last_bit(half, offset)
        ref = self.block(half, offset ^ (1 << bit))
        return pltpu.make_async_remote_copy(
            src_ref=ref, dst_ref=ref, send_sem=self.send.at[half, offset], recv_sem=self.recv.at[half, offset],
            device_id=(toggled(self.me, 1 << bit, self.bits), self.t), device_id_type=MESH)

    def start(self, half):
        for bit in bit_order(half):
            self.copy(half, 1 << bit).start()

    def arrive(self, half, offset):
        ref = self.block(half, offset)
        pltpu.make_async_remote_copy(
            src_ref=ref, dst_ref=ref, send_sem=self.send.at[half, offset], recv_sem=self.recv.at[half, offset],
            device_id=(self.me, self.t), device_id_type=MESH).wait_recv()
        order = bit_order(half)
        for bit in order[order.index(last_bit(half, offset)) + 1:]:
            self.copy(half, offset | 1 << bit).start()

    def finish(self):
        for half in range(self.halves):
            for offset in range(1, self.n):
                self.copy(half, offset).wait_send()

    def level(self, half, offset):
        order = bit_order(half)
        return sum(2 ** order.index(b) for b in range(1, self.bits) if offset >> b & 1)

    def events(self):
        def due(event):
            return self.level(*event), event[1] & 1, event[0]
        return sorted(((h, r) for h in range(self.halves) for r in range(1, self.n)), key=due)


def gather_sems(halves=2):
    n = lax.axis_size("seq")
    return [pltpu.SemaphoreType.DMA((halves, n)), pltpu.SemaphoreType.DMA((halves, n))]


class LineSum:
    def __init__(self, part, recv, send_sem, recv_sem):
        self.part, self.recv, self.send_sem, self.recv_sem = part, recv, send_sem, recv_sem
        self.m = part.shape[1]
        self.s, self.t = lax.axis_index("seq"), lax.axis_index("tp")

    def copy(self, p, j, slot, to):
        return pltpu.make_async_remote_copy(
            src_ref=self.part.at[p, j], dst_ref=self.recv.at[p, slot], send_sem=self.send_sem.at[p, j],
            recv_sem=self.recv_sem.at[p, slot], device_id=(self.s, to), device_id_type=MESH)

    def add(self, p, j):
        self.copy(p, j, j, self.t).wait_recv()
        self.part[p, j] = (self.part[p, j].astype(jnp.float32) + self.recv[p, j].astype(jnp.float32)).astype(jnp.bfloat16)

    def left(self, p, j):
        @pl.when(self.t > j)
        def _():
            @pl.when(self.t < self.m - 1)
            def _():
                self.add(p, j)

            self.sent(p, j - 1, j > 0)
            if p > 0 and j == 0:
                self.sent(p - 1, self.t - 1, True)
            self.copy(p, j, j, self.t - 1).start()

    def right(self, p, j):
        @pl.when(self.t < j)
        def _():
            @pl.when(self.t > 0)
            def _():
                self.add(p, j)

            self.sent(p, j + 1, j < self.m - 1)
            if p > 0 and j == self.m - 1:
                self.sent(p - 1, self.t + 1, True)
            self.copy(p, j, jnp.where(self.t + 1 == j, self.m, j), self.t + 1).start()

    def sent(self, p, j, some):
        if some:
            self.copy(p, j, j, self.t).wait_send()

    def step(self, p, k):
        self.left(p, k)
        self.right(p, self.m - 1 - k)

    def clear(self, p):
        @pl.when(self.t == self.m - 1)
        def _():
            self.recv[p, self.m - 1] = jnp.zeros(self.recv.shape[2:], self.recv.dtype)

        @pl.when(self.t == 0)
        def _():
            self.recv[p, self.m] = jnp.zeros(self.recv.shape[2:], self.recv.dtype)

    def total(self, p):
        @pl.when(self.t < self.m - 1)
        def _():
            self.copy(p, self.t, self.t, self.t).wait_recv()

        @pl.when(self.t > 0)
        def _():
            self.copy(p, self.t, self.m, self.t).wait_recv()

        f32 = jnp.float32
        return self.part[p, self.t].astype(f32) + (self.recv[p, self.t].astype(f32) + self.recv[p, self.m].astype(f32))

    def finish(self, p):
        @pl.when(self.t > 0)
        def _():
            self.copy(p, self.t - 1, 0, self.t).wait_send()

        @pl.when(self.t < self.m - 1)
        def _():
            self.copy(p, self.t + 1, 0, self.t).wait_send()


class DirectSum:
    def __init__(self, part, recv, send_sem, recv_sem):
        self.part, self.recv, self.send_sem, self.recv_sem = part, recv, send_sem, recv_sem
        self.m = part.shape[1]
        self.s, self.t = lax.axis_index("seq"), lax.axis_index("tp")

    def copy(self, p, j, sender):
        return pltpu.make_async_remote_copy(
            src_ref=self.part.at[p, j], dst_ref=self.recv.at[p, sender], send_sem=self.send_sem.at[p, j],
            recv_sem=self.recv_sem.at[p, sender], device_id=(self.s, j), device_id_type=MESH)

    def others(self, act):
        for j in range(self.m):
            @pl.when(self.t != j)
            def _(j=j):
                act(j)

    def start(self, p):
        self.others(lambda j: self.copy(p, j, self.t).start())
        self.recv[p, self.t] = self.part[p, self.t]

    def total(self, p):
        self.others(lambda j: self.copy(p, j, j).wait_recv())
        total = self.recv[p, 0].astype(jnp.float32)
        for j in range(1, self.m):
            total = total + self.recv[p, j].astype(jnp.float32)
        return total

    def finish(self, p):
        self.others(lambda j: self.copy(p, j, self.t).wait_send())


class LineGather:
    def __init__(self, buf, send_sem, recv_sem):
        self.buf, self.send_sem, self.recv_sem = buf, send_sem, recv_sem
        self.m = buf.shape[1]
        self.s, self.t = lax.axis_index("seq"), lax.axis_index("tp")

    def copy(self, p, j, way):
        ref = self.buf.at[p, j]
        return pltpu.make_async_remote_copy(
            src_ref=ref, dst_ref=ref, send_sem=self.send_sem.at[p, way, j], recv_sem=self.recv_sem.at[p, j],
            device_id=(self.s, self.t + (2 * way - 1)), device_id_type=MESH)

    def pass_on(self, p, j, way):
        @pl.when(self.t > 0 if way == 0 else self.t < self.m - 1)
        def _():
            self.copy(p, j, way).start()

    def start(self, p):
        self.pass_on(p, self.t, 0)
        self.pass_on(p, self.t, 1)

    def arrive(self, p, distance):
        @pl.when(self.t + distance < self.m)
        def _():
            self.copy(p, self.t + distance, 0).wait_recv()
            self.pass_on(p, self.t + distance, 0)

        @pl.when(self.t >= distance)
        def _():
            self.copy(p, self.t - distance, 1).wait_recv()
            self.pass_on(p, self.t - distance, 1)

    def finish(self, p):
        for j in range(self.m):
            @pl.when((self.t > 0) & (self.t <= j))
            def _(j=j):
                self.copy(p, j, 0).wait_send()

            @pl.when((self.t < self.m - 1) & (self.t >= j))
            def _(j=j):
                self.copy(p, j, 1).wait_send()


def line_sems(pieces):
    m = lax.axis_size("tp")
    return [pltpu.SemaphoreType.DMA((pieces, m)), pltpu.SemaphoreType.DMA((pieces, m + 1)),
            pltpu.SemaphoreType.DMA((pieces, 2, m)), pltpu.SemaphoreType.DMA((pieces, m))]


class Plan:
    def __init__(self):
        self.steps = []

    def at(self, time, step, *args):
        self.steps.append((time, len(self.steps), step, args))

    def run(self):
        for _, _, step, args in sorted(self.steps, key=lambda one: one[:2]):
            step(*args)


def attn_fwd_block(q_ref, kv_ref, out_ref, sum_ref, bias_ref, kv, rows, tile):
    scale = HEAD_SIZE ** -0.5 * LOG2E
    all_rows = q_ref.shape[1]
    for h in range(kv):
        cols = slice(h * HEAD_SIZE, (h + 1) * HEAD_SIZE)
        v_cols = slice((kv + h) * HEAD_SIZE, (kv + h + 1) * HEAD_SIZE)
        for start in range(0, all_rows, tile):
            at = start % rows
            n_keys = rows if bias_ref is None else at + tile
            scores = mm(q_ref[h, start:start + tile], kv_ref[:n_keys, cols], NT) * scale
            if bias_ref is not None:
                scores = scores + bias_ref[at:at + tile, :n_keys]
            weights = jnp.exp2(scores)
            part = weights[:, :HEAD_SIZE]
            for c in range(HEAD_SIZE, n_keys, HEAD_SIZE):
                part = part + weights[:, c:c + HEAD_SIZE]
            sum_ref[h, start:start + tile] += part
            out_ref[h, start:start + tile] += mm(weights.astype(jnp.bfloat16), kv_ref[:n_keys, v_cols])


def rms_inverse(values):
    return lax.rsqrt(jnp.mean(values * values, axis=-1, keepdims=True) + EPS)


def forward_kernel(tok_ref, wq_ref, wk_ref, wv_ref, gain_ref, cos_ref, sin_ref, qd_ref, kd_ref, o_ref, gate_ref,
                   norm_ref, proj_ref, q_ref, kv_ref, att_all, lse_ref, gains_ref, w, o_all, gate_all,
                   inv, acc, total, bias, local_sem, *sems):
    f32, b16 = jnp.float32, jnp.bfloat16
    n, rows, _ = kv_ref.shape
    kv, all_rows, _ = q_ref.shape
    group = all_rows // rows
    me = lax.axis_index("seq")
    bits = seq_bits()
    tile = cut(rows)
    depth = w.shape[1]
    q_width, k_width = wq_ref.shape[1], wk_ref.shape[1]
    w_gather = SeqGather(w, sems[0], sems[1])
    gain_gather = SeqGather(gains_ref, sems[2], sems[3], halves=1)
    kv_gather = SeqGather(kv_ref, sems[4], sems[5])
    o_gather = SeqGather(o_all, sems[6], sems[7])
    gate_gather = SeqGather(gate_all, sems[8], sems[9])
    o_line = LineGather(o_all.at[pl.ds(me, 1)], sems[10], sems[11])
    att_gather = LineGather(att_all, sems[12], sems[13])
    t, m = lax.axis_index("tp"), lax.axis_size("tp")
    pieces, _, piece, _ = att_all.shape

    own = [pltpu.make_async_copy(wq_ref, w.at[me, :, pl.ds(0, q_width)], local_sem.at[0]),
           pltpu.make_async_copy(wk_ref, w.at[me, :, pl.ds(q_width, k_width)], local_sem.at[1]),
           pltpu.make_async_copy(wv_ref, w.at[me, :, pl.ds(q_width + k_width, k_width)], local_sem.at[2]),
           pltpu.make_async_copy(o_ref, o_all.at[me, t], local_sem.at[3]),
           pltpu.make_async_copy(gate_ref, gate_all.at[me], local_sem.at[4])]
    for copy in own:
        copy.start()
    gains_ref[me] = gain_ref[...]
    greet(True, True)
    for copy in own[:3]:
        copy.wait()
    w_gather.start(0)
    w_gather.start(1)
    gain_gather.start(0)
    own[3].wait()
    o_line.start(0)

    @pl.loop(0, rows // tile)
    def _(i):
        at = pl.ds(i * tile, tile)
        inv[at] = rms_inverse(tok_ref[at].astype(f32))

    visible = (lax.broadcasted_iota(jnp.int32, (rows, rows), 1)
               <= lax.broadcasted_iota(jnp.int32, (rows, rows), 0)) & (qd_ref[...] == kd_ref[...])
    bias[...] = jnp.where(visible, 0.0, -1e30)
    for event in gain_gather.events():
        gain_gather.arrive(*event)

    def project(offset):
        source = toggled(me, offset, bits)
        cols = pl.ds(pl.multiple_of(source * depth, depth), depth)

        @pl.loop(0, rows // tile)
        def _(i):
            at = pl.ds(i * tile, tile)
            block = (tok_ref[at, cols].astype(f32) * inv[at] * gains_ref[source, 0:1, :depth]).astype(b16)
            norm_ref[at, cols] = block
            part = mm(block, w[source])
            if offset == 0:
                proj_ref[at] = part
            else:
                proj_ref[at] += part

    project(0)
    came = {}
    hops = [len(w_gather.events()) * d // m for d in range(1, m)]
    for i, (half, offset) in enumerate(w_gather.events()):
        if i in hops:
            o_line.arrive(0, hops.index(i) + 1)
        w_gather.arrive(half, offset)
        came[offset] = came.get(offset, 0) + 1
        if came[offset] == 2:
            project(offset)

    own[4].wait()
    gain_q, gain_k = gains_ref[0, 2:3, :HEAD_SIZE], gains_ref[0, 3:4, :HEAD_SIZE]
    for j in range(1, n):
        gain_q = gain_q + gains_ref[j, 2:3, :HEAD_SIZE]
        gain_k = gain_k + gains_ref[j, 3:4, :HEAD_SIZE]

    def rotated(at, first, gain):
        u = proj_ref[at, first:first + HEAD_SIZE]
        u = u * rms_inverse(u) * gain
        return (u * cos_ref[at] + pltpu.roll(u, HEAD_SIZE // 2, 1) * sin_ref[at]).astype(b16)

    @pl.loop(0, rows // tile)
    def _(i):
        at = pl.ds(i * tile, tile)
        for h in range(kv):
            kv_ref[me, at, h * HEAD_SIZE:(h + 1) * HEAD_SIZE] = rotated(at, q_width + h * HEAD_SIZE, gain_k)
        kv_ref[me, at, k_width:] = proj_ref[at, q_width + k_width:].astype(b16)

    kv_gather.start(0)
    kv_gather.start(1)

    @pl.loop(0, rows // tile)
    def _(i):
        at = pl.ds(i * tile, tile)
        for h in range(kv):
            for g in range(group):
                q_ref[h, pl.ds(g * rows + i * tile, tile)] = rotated(at, (h * group + g) * HEAD_SIZE, gain_q)

    acc[...] = jnp.zeros_like(acc)
    total[...] = jnp.zeros_like(total)
    attn_fwd_block(q_ref, kv_ref.at[me], acc.at[0], total.at[0], bias, kv, rows, tile)
    kv_steps = [[] for _ in range(n)]
    seen = set()
    order = kv_gather.events()
    offsets = sorted(range(1, n), key=lambda r: max(order.index((h, r)) for h in range(2)))
    taken = 0
    for k, offset in enumerate(offsets):
        need = max(order.index((h, offset)) for h in range(2)) + 1
        kv_steps[k] = order[taken:max(need, taken)]
        taken = max(need, taken)
    only_first = jnp.where(qd_ref[...] == 0, 1.0, 0.0)

    def attended(p):
        for h in range(kv):
            for g in range(group):
                for start in range(p * piece, (p + 1) * piece, tile):
                    at = slice(g * rows + start, g * rows + start + tile)
                    total_row = total[0, h, at] + total[1, h, at] * only_first[start:start + tile]
                    out = acc[0, h, at] + acc[1, h, at] * only_first[start:start + tile]
                    cols = slice((h * group + g) * HEAD_SIZE, (h * group + g + 1) * HEAD_SIZE)
                    out = (out / jnp.sum(total_row, axis=1, keepdims=True)).astype(b16)
                    att_all[p, t, start - p * piece:start - p * piece + tile, cols] = out
                    lse_ref[h, :, at] = jnp.log2(jnp.sum(total_row.T, axis=0, keepdims=True))
        att_gather.start(p)

    @pl.loop(0, n - 1)
    def _(k):
        source = 0
        for i, offset in enumerate(offsets):
            source = source + jnp.where(k == i, toggled(me, offset, bits), 0)

            @pl.when(k == i)
            def _(i=i):
                for event in kv_steps[i]:
                    kv_gather.arrive(*event)
                if i == max(n - 6, 0):
                    for gather in (o_gather, gate_gather):
                        gather.start(0)
                        gather.start(1)

        @pl.when(source < me)
        def _():
            attn_fwd_block(q_ref, kv_ref.at[source], acc.at[1], total.at[1], None, kv, rows, tile)

    plan = Plan()
    for p in range(pieces):
        plan.at(p, attended, p)
        for d in range(1, m):
            plan.at(pieces + 6.0 * (pieces * (d - 1) + p + 1), att_gather.arrive, p, d)
    for gather in (o_gather, gate_gather):
        for event in gather.events():
            plan.at((4.0, 25.0, 42.0, 48.0)[min(gather.level(*event), 3)], gather.arrive, *event)
    plan.run()
    o_line.finish(0)
    for p in range(pieces):
        att_gather.finish(p)
    for gather in (w_gather, gain_gather, kv_gather, o_gather, gate_gather):
        gather.finish()


def forward_attention(tokens, q_weight, key_matrix, value_matrix, gains, cosines, sines, doc_column, doc_row, o_weight, gate_weight, pieces):
    n, m = lax.axis_size("seq"), lax.axis_size("tp")
    rows, width = tokens.shape
    depth, q_width = q_weight.shape
    k_width = key_matrix.shape[1]
    kv, group = k_width // HEAD_SIZE, q_width // k_width
    f32, b16 = jnp.float32, jnp.bfloat16
    wide = q_width + 2 * k_width
    heads = (kv, group * rows, HEAD_SIZE)
    out = [((rows, width), b16), ((rows, wide), f32), (heads, b16), ((n, rows, 2 * k_width), b16), ((pieces, m, rows // pieces, q_width), b16),
           ((kv, 1, group * rows), f32), ((n,) + gains.shape, f32), ((n, depth, wide), b16), ((n, m) + o_weight.shape, b16), ((n,) + gate_weight.shape, b16)]
    sems = []
    for halves in (2, 1, 2, 2, 2):
        sems += gather_sems(halves)
    sems += line_sems(1)[2:] + line_sems(pieces)[2:]
    return pl.pallas_call(
        forward_kernel,
        out_shape=[jax.ShapeDtypeStruct(*one) for one in out],
        in_specs=[VM] + [ANY] * 3 + [VM] * 5 + [ANY] * 2,
        out_specs=[VM] * 8 + [ANY] * 2,
        scratch_shapes=[pltpu.VMEM((rows, 1), f32), pltpu.VMEM((2,) + heads, f32),
                        pltpu.VMEM((2,) + heads, f32), pltpu.VMEM((rows, rows), f32), pltpu.SemaphoreType.DMA((5,))] + sems,
        compiler_params=pltpu.CompilerParams(vmem_limit_bytes=VMEM_BYTES, collective_id=1, has_side_effects=True),
        name="forward_attention",
    )(tokens, q_weight, key_matrix, value_matrix, gains, cosines, sines, doc_column, doc_row, o_weight, gate_weight)


class SeqSum:
    def __init__(self, source, loc, near, far, sems):
        self.source, self.loc, self.near, self.far = source, loc, near, far
        self.load_sem, self.near_sem, self.far_sem = sems
        self.bits = seq_bits()
        self.count = 1 << (self.bits - 1)
        self.me, self.t = lax.axis_index("seq"), lax.axis_index("tp")
        self.half_rows = loc.shape[1] // 2

    def first(self, half, e):
        order = bit_order(half)[:-1]
        return min(order.index(b) for b in range(1, self.bits) if 2 * e >> b & 1)

    def load(self, e):
        return pltpu.make_async_copy(self.source(toggled(self.me, 2 * e, self.bits)), self.loc.at[e], self.load_sem.at[e])

    def cross(self, e):
        return pltpu.make_async_remote_copy(
            src_ref=self.source(toggled(self.me, 2 * e + 1, self.bits)), dst_ref=self.near.at[e],
            send_sem=self.near_sem.at[0, e], recv_sem=self.near_sem.at[1, e],
            device_id=(toggled(self.me, 1, self.bits), self.t), device_id_type=MESH)

    def begin(self):
        for e in reversed(range(self.count)):
            self.cross(e).start()
            self.load(e).start()

    def meet(self, e):
        self.load(e).wait()
        self.cross(e).wait_recv()
        self.loc[e] += self.near[e]
        for half in range(2):
            if e and self.first(half, e) == 0:
                self.hop(half, e).start()

    def hop(self, half, e):
        bit = bit_order(half)[self.first(half, e)]
        return pltpu.make_async_remote_copy(
            src_ref=self.loc.at[e, pl.ds(half * self.half_rows, self.half_rows)], dst_ref=self.far.at[half, e - 1],
            send_sem=self.far_sem.at[0, half, e - 1], recv_sem=self.far_sem.at[1, half, e - 1],
            device_id=(toggled(self.me, 1 << bit, self.bits), self.t), device_id_type=MESH)

    def arrive(self, half, e):
        place = self.first(half, e)
        to = (2 * e ^ 1 << bit_order(half)[place]) // 2
        self.hop(half, e).wait_recv()
        self.loc[to, half * self.half_rows:(half + 1) * self.half_rows] += self.far[half, e - 1]
        if to and self.first(half, to) == place + 1:
            self.hop(half, to).start()

    def rounds(self):
        found = [[] for _ in range(self.bits - 1)]
        for e in reversed(range(1, self.count)):
            for half in range(2):
                found[self.first(half, e)].append((half, e))
        return found

    def finish(self):
        for e in range(self.count):
            self.cross(e).wait_send()
            for half in range(2 if e else 0):
                self.hop(half, e).wait_send()


def sum_scratch(rows, columns):
    count = lax.axis_size("seq") // 2
    b16 = jnp.bfloat16
    return [pltpu.VMEM((count, rows, columns), b16), pltpu.VMEM((count, rows, columns), b16),
            pltpu.VMEM((2, max(count - 1, 1), rows // 2, columns), b16), pltpu.SemaphoreType.DMA((count,)),
            pltpu.SemaphoreType.DMA((2, count)), pltpu.SemaphoreType.DMA((2, 2, max(count - 1, 1)))]


SUM_SCRATCH = 6


def seq_sum(source, scratch):
    return SeqSum(source, *scratch[:3], scratch[3:])


def middle_kernel(att_ref, o_ref, gate_ref, up_ref, down_ref, tok_ref, cot_in, gains_ref,
                  low_ref, after_grad_ref, do_ref, gain_out, mlp_ref, grads_ref,
                  o_all, gate_all, up_all, down_all, cot_ref, part, recv, norm_mid, act, gg, gu, after, after_own, att, rows_buf,
                  do_send, stage, local_sem, att_sem, rows_sem, stage_sem, do_send_sem, do_recv_sem, *sems):
    f32, b16 = jnp.float32, jnp.bfloat16
    pieces, m, sub, width = cot_ref.shape
    n, depth, ff = gate_all.shape
    piece = m * sub
    me, t = lax.axis_index("seq"), lax.axis_index("tp")
    up_gather = SeqGather(up_all, sems[0], sems[1])
    down_gather = SeqGather(down_all, sems[2], sems[3])
    mid_sum = DirectSum(part, recv, sems[4], sems[5])

    whole = [pltpu.make_async_copy(up_ref, up_all.at[me], local_sem.at[0]),
             pltpu.make_async_copy(down_ref, down_all.at[me], local_sem.at[1]),
             pltpu.make_async_copy(o_ref, o_all, local_sem.at[2]),
             pltpu.make_async_copy(gate_ref, gate_all, local_sem.at[3]),
             pltpu.make_async_copy(cot_in, cot_ref, local_sem.at[4])]

    def att_copy(p):
        return pltpu.make_async_copy(att_ref.at[p], att, att_sem.at[0])

    def tok_copy(p):
        return pltpu.make_async_copy(tok_ref.at[p], rows_buf.at[p % 2], rows_sem.at[p % 2])

    def mlp_copy(p):
        return pltpu.make_async_copy(rows_buf.at[p % 2], mlp_ref.at[p], rows_sem.at[p % 2])

    for copy in whole:
        copy.start()
    att_copy(0).start()
    for p in range(min(2, pieces)):
        tok_copy(p).start()
    greet(True, "all")
    for copy in whole[:2]:
        copy.wait()
    for gather in (up_gather, down_gather):
        for half in range(2):
            gather.start(half)
    gain_out[...] = jnp.zeros_like(gain_out)
    plan = Plan()

    def mlp_gain(j):
        return gains_ref[j, 1:2, :depth]

    def project(p):
        if p == 0:
            whole[2].wait()
        att_copy(p).wait()
        tok_copy(p).wait()
        squares = jnp.zeros((piece, 1), f32)
        for j in range(n):
            cols = slice(j * depth, (j + 1) * depth)
            block = rows_buf[p % 2, :, :, cols].reshape(piece, depth).astype(f32)
            for k in range(m):
                block = block + mm(att[k], o_all[j, k])
            after[:, cols] = block
            squares = squares + jnp.sum(block * block, axis=1, keepdims=True)
        if p + 1 < pieces:
            att_copy(p + 1).start()
        inverse = lax.rsqrt(squares * (1.0 / width) + EPS)
        for j in range(n):
            cols = slice(j * depth, (j + 1) * depth)
            norm_mid[p, :, :, cols] = (after[:, cols] * inverse * mlp_gain(j)).astype(b16).reshape(m, sub, depth)
        after_own[p] = after[pl.ds(pl.multiple_of(t * sub, sub), sub)]
        if p + 2 < pieces:
            tok_copy(p + 2).start()

    def hidden(p, first, count):
        rows = slice(p * piece, (p + 1) * piece)
        cols = slice(first, first + count)
        x = norm_mid[p].reshape(piece, width)
        gate = mm(x, gate_all[:, :, cols].reshape(width, count))
        up = mm(x, up_all[:, :, cols].reshape(width, count))
        grad = mm(cot_ref[p, :, :, :depth].reshape(piece, depth), down_all[0, cols], NT)
        for j in range(1, n):
            c = cot_ref[p, :, :, j * depth:(j + 1) * depth].reshape(piece, depth)
            grad = grad + mm(c, down_all[j, cols], NT)
        sig = jax.nn.sigmoid(gate)
        silu = gate * sig
        act[rows, cols] = (silu * up).astype(b16)
        gg[rows, cols] = (grad * up * sig * (1.0 + gate * (1.0 - sig))).astype(b16)
        gu[rows, cols] = (grad * silu).astype(b16)

    def mid(p, first, count):
        rows = slice(p * piece, (p + 1) * piece)
        for j in range(first, first + count):
            block = mm(gg[rows], gate_all[j], NT) + mm(gu[rows], up_all[j], NT)
            part[p, :, :, j * depth:(j + 1) * depth] = block.astype(b16).reshape(m, sub, depth)

    def mlp_out(p):
        if p >= 2:
            mlp_copy(p - 2).wait()
        rows = slice(p * piece, (p + 1) * piece)
        for j in range(n):
            block = mm(act[rows], down_all[j]).astype(b16)
            rows_buf[p % 2, :, :, j * depth:(j + 1) * depth] = block.reshape(m, sub, depth)
        rows_buf[p % 2, t] = (rows_buf[p % 2, t].astype(f32) + after_own[p]).astype(b16)
        mlp_copy(p).start()

    def do_copy(p, j):
        return pltpu.make_async_remote_copy(
            src_ref=do_send.at[p, j], dst_ref=do_ref.at[p, t], send_sem=do_send_sem.at[p, j], recv_sem=do_recv_sem.at[p, t],
            device_id=(me, j), device_id_type=MESH)

    def do_arrival(p, j):
        return pltpu.make_async_remote_copy(
            src_ref=do_send.at[p, j], dst_ref=do_ref.at[p, j], send_sem=do_send_sem.at[p, j], recv_sem=do_recv_sem.at[p, j],
            device_id=(me, j), device_id_type=MESH)

    def attended_back(p):
        for k in range(m):
            grad = mm(o_all[0, k], low_ref[p, :, :depth], NT)
            for j in range(1, n):
                grad = grad + mm(o_all[j, k], low_ref[p, :, j * depth:(j + 1) * depth], NT)
            do_send[p, k] = grad.T.astype(b16)

            @pl.when(t != k)
            def _(k=k):
                do_copy(p, k).start()

        do_ref[p, t] = do_send[p, t]

    def mid_back(p):
        grad = mid_sum.total(p)
        after = after_own[p]
        inverse = rms_inverse(after)
        normed = after * inverse
        mean = 0.0
        for j in range(n):
            cols = slice(j * depth, (j + 1) * depth)
            gain_out[:, cols] += jnp.sum(grad[:, cols] * normed[:, cols], axis=0, keepdims=True)
            mean = mean + jnp.sum(grad[:, cols] * mlp_gain(j) * normed[:, cols], axis=1, keepdims=True)
        mean = mean * (1.0 / width)
        for j in range(n):
            cols = slice(j * depth, (j + 1) * depth)
            back = inverse * (grad[:, cols] * mlp_gain(j) - normed[:, cols] * mean)
            back = back + cot_ref[p, t, :, cols].astype(f32)
            after_grad_ref[p, :, cols] = back
            low_ref[p, :, cols] = back.astype(b16)
        attended_back(p)

    def staged(j, slot):
        return pltpu.make_async_copy(stage.at[slot], grads_ref.at[j, slot], stage_sem.at[slot])

    def weight_grads(j):
        cols = slice(j * depth, (j + 1) * depth)
        for slot, terms in enumerate((act, gg, gu)):
            if slot < 2:
                x = (cot_ref if slot == 0 else norm_mid)[:, :, :, cols].reshape(pieces * piece, depth)
            if j:
                staged(j - 1, slot).wait()
            stage[slot] = mm(x, terms[...], TN).astype(b16)
            staged(j, slot).start()

    for p in range(pieces):
        plan.at(3.0 * p, project, p)

    def loaded():
        for copy in whole[3:]:
            copy.wait()

    plan.at(3.0 * pieces, loaded)
    for gather in (up_gather, down_gather):
        for event in gather.events():
            plan.at(10.0 + gather.level(*event), gather.arrive, *event)

    chunk = cut(ff, 512)
    chunks = ff // chunk
    clock = 58.0
    for p in range(pieces):
        for c in range(chunks):
            plan.at(clock, hidden, p, c * chunk, chunk)
            clock += 1.8
        for half in range(2):
            plan.at(clock, mid, p, half * (n // 2), n // 2)
            clock += 1.7
        plan.at(clock, mid_sum.start, p)
        arrived = 92.0 + 25.0 * p
        plan.at(arrived, mid_back, p)
    for j in range(n):
        plan.at(clock, weight_grads, j)
        clock += 2.0
    for p in range(pieces):
        plan.at(clock, mlp_out, p)
        clock += 2.0
    plan.run()

    for slot in range(3):
        staged(n - 1, slot).wait()
    for p in range(max(pieces - 2, 0), pieces):
        mlp_copy(p).wait()
    up_gather.finish()
    down_gather.finish()
    for p in range(pieces):
        mid_sum.finish(p)
        for j in range(m):
            @pl.when(t != j)
            def _(p=p, j=j):
                do_arrival(p, j).wait_recv()
                do_copy(p, j).wait_send()


def middle(attended, o_all, gate_all, up_weight, down_weight, tokens, cotangent, gains):
    f32, b16 = jnp.float32, jnp.bfloat16
    pieces, m, sub, width = tokens.shape
    n, depth, ff = gate_all.shape
    rows = pieces * m * sub
    blocks = tokens.shape
    heads = attended.shape[3]
    out = [((pieces, sub, width), b16), ((pieces, sub, width), f32), ((pieces, m, sub, heads), b16), ((1, width), f32),
           (blocks, b16), ((n, 3, depth, ff), b16)]
    dma = pltpu.SemaphoreType.DMA
    return pl.pallas_call(
        middle_kernel,
        out_shape=[jax.ShapeDtypeStruct(*one) for one in out],
        in_specs=[ANY] * 7 + [VM],
        out_specs=[VM] * 4 + [ANY] * 2,
        scratch_shapes=[pltpu.VMEM(o_all.shape, b16), pltpu.VMEM((n, depth, ff), b16), pltpu.VMEM((n, depth, ff), b16),
                        pltpu.VMEM((n, ff, depth), b16), pltpu.VMEM(blocks, b16), pltpu.VMEM(blocks, b16),
                        pltpu.VMEM(blocks, b16), pltpu.VMEM(blocks, b16),
                        pltpu.VMEM((rows, ff), b16), pltpu.VMEM((rows, ff), b16), pltpu.VMEM((rows, ff), b16),
                        pltpu.VMEM((m * sub, width), f32), pltpu.VMEM((pieces, sub, width), f32),
                        pltpu.VMEM(attended.shape[1:], b16), pltpu.VMEM((2, m, sub, width), b16),
                        pltpu.VMEM((pieces, m, sub, heads), b16), pltpu.VMEM((3, depth, ff), b16),
                        dma((5,)), dma((2,)), dma((2,)), dma((3,)), dma((pieces, m)), dma((pieces, m))]
        + gather_sems() + gather_sems() + [dma((pieces, m)), dma((pieces, m))],
        compiler_params=pltpu.CompilerParams(vmem_limit_bytes=VMEM_BYTES, collective_id=2, has_side_effects=True),
        name="middle",
    )(attended, o_all, gate_all, up_weight, down_weight, tokens, cotangent, gains)


def attn_bwd_block(h, q_ref, do_ref, lse_ref, delta_ref, kv_ref, dq_ref, dk_ref, dv_ref, bias_ref, kv, rows, tile):
    scale = HEAD_SIZE ** -0.5 * LOG2E
    all_rows = q_ref.shape[1]
    k_cols = pl.ds(pl.multiple_of(h * HEAD_SIZE, HEAD_SIZE), HEAD_SIZE)
    v_cols = pl.ds(pl.multiple_of((kv + h) * HEAD_SIZE, HEAD_SIZE), HEAD_SIZE)
    dk_ref[...] = jnp.zeros_like(dk_ref)
    dv_ref[...] = jnp.zeros_like(dv_ref)
    for start in range(0, all_rows, tile):
        at = start % rows
        n_keys = rows if bias_ref is None else at + tile
        q = q_ref[h, start:start + tile]
        do = do_ref[h, start:start + tile]
        k = kv_ref[:n_keys, k_cols]
        scores = mm(k, q, NT) * scale - lse_ref[h, :, start:start + tile]
        if bias_ref is not None:
            scores = scores + bias_ref[:n_keys, at:at + tile]
        probs = jnp.exp2(scores)
        grad = mm(kv_ref[:n_keys, v_cols], do, NT)
        grad = (probs * (grad - delta_ref[h, :, start:start + tile])).astype(jnp.bfloat16)
        dv_ref[:n_keys] += mm(probs.astype(jnp.bfloat16), do)
        dk_ref[:n_keys] += mm(grad, q)
        dq_ref[h, start:start + tile] += mm(grad, k, TN)


def backward_kernel(q_ref, do_ref, lse_ref, kv_ref, kd_ref, qdr_ref, low_ref, att_ref, grads_ref,
                    dq_ref, dkv_ref, gate_out, up_out, down_out, o_grads, do, delta, lse_off, dk, dv, bias, att, att_rows, stage,
                    local_sem, stage_sem, *scratch):
    f32, b16 = jnp.float32, jnp.bfloat16
    kv, all_rows, _ = q_ref.shape
    n, rows, _ = kv_ref.shape
    group = all_rows // rows
    pieces, m, sub, heads = att_rows.shape
    piece = m * sub
    depth = grads_ref.shape[2]
    me, t = lax.axis_index("seq"), lax.axis_index("tp")
    copies = [pltpu.make_async_copy(att_ref.at[:, t], att, local_sem.at[0]),
              pltpu.make_async_copy(att_ref.at[:, :, pl.ds(pl.multiple_of(t * sub, sub), sub)], att_rows, local_sem.at[1])]
    for copy in copies:
        copy.start()
    tile = cut(rows)
    scale = HEAD_SIZE ** -0.5
    gate_sum = seq_sum(lambda j: grads_ref.at[j, 1], scratch[:SUM_SCRATCH])
    up_sum = seq_sum(lambda j: grads_ref.at[j, 2], scratch[SUM_SCRATCH:2 * SUM_SCRATCH])
    down_sum = seq_sum(lambda j: grads_ref.at[j, 0], scratch[2 * SUM_SCRATCH:])

    greet(True, False)
    gate_sum.begin()
    dq_ref[...] = jnp.zeros_like(dq_ref)
    off = jnp.where(qdr_ref[...] == 0, 0.0, 1e30)
    visible = (lax.broadcasted_iota(jnp.int32, (rows, rows), 0)
               <= lax.broadcasted_iota(jnp.int32, (rows, rows), 1)) & (kd_ref[...] == qdr_ref[...])
    bias[...] = jnp.where(visible, 0.0, -1e30)
    for copy in copies:
        copy.wait()
    for p in range(pieces):
        for h in range(kv):
            for g in range(group):
                cols = slice((h * group + g) * HEAD_SIZE, (h * group + g + 1) * HEAD_SIZE)
                at = slice(g * rows + p * piece, g * rows + (p + 1) * piece)
                grad = do_ref[p * piece:(p + 1) * piece, cols]
                do[h, at] = grad
                prod = grad.astype(f32) * att[p, :, cols].astype(f32)
                delta[h, :, at] = jnp.sum(prod.T, axis=0, keepdims=True)

    def staged(j):
        return pltpu.make_async_copy(stage.at[j % 2], o_grads.at[j], stage_sem.at[j % 2])

    for j in range(n):
        if j >= 2:
            staged(j - 2).wait()
        rows_low = low_ref[:, :, j * depth:(j + 1) * depth].reshape(pieces * sub, depth)
        for k in range(m):
            rows_att = att_rows[:, k].reshape(pieces * sub, heads)
            stage[j % 2, :, k * heads:(k + 1) * heads] = mm(rows_low, rows_att, TN).astype(b16)
        staged(j).start()
    for h in range(kv):
        for g in range(group):
            at = slice(g * rows, (g + 1) * rows)
            lse_off[h, :, at] = lse_ref[h, :, at] + off

    def keep(j, h):
        k_cols = pl.ds(pl.multiple_of(h * HEAD_SIZE, HEAD_SIZE), HEAD_SIZE)
        v_cols = pl.ds(pl.multiple_of((kv + h) * HEAD_SIZE, HEAD_SIZE), HEAD_SIZE)
        dkv_ref[j, :, k_cols] = (dk[...] * scale).astype(b16)
        dkv_ref[j, :, v_cols] = dv[...].astype(b16)

    @pl.loop(0, kv)
    def _(h):
        attn_bwd_block(h, q_ref, do, lse_ref, delta, kv_ref.at[me], dq_ref, dk, dv, bias, kv, rows, tile)
        keep(me, h)

    steps = n * kv
    events = [[] for _ in range(steps + 1)]

    def at_time(time, step, *args):
        events[min(int(time / 3.8), steps)].append((step, args))

    def plan_sum(one, meet, *arrivals):
        for e in reversed(range(one.count)):
            at_time(meet, one.meet, e)
        for k, found in enumerate(one.rounds()):
            for event in found:
                at_time(arrivals[min(k, 1)] + k, one.arrive, *event)

    plan_sum(gate_sum, 0.0, 22.0, 34.0)
    at_time(4.0, up_sum.begin)
    plan_sum(up_sum, 15.0, 42.0, 52.0)
    at_time(23.0, down_sum.begin)
    plan_sum(down_sum, 34.0, 61.0, 70.0)

    @pl.loop(0, steps)
    def _(i):
        for k in range(steps):
            if events[k]:
                @pl.when(i == k)
                def _(k=k):
                    for step, args in events[k]:
                        step(*args)

        j, h = i // kv, i % kv

        @pl.when(j < me)
        def _():
            attn_bwd_block(h, q_ref, do, lse_off, delta, kv_ref.at[j], dq_ref, dk, dv, None, kv, rows, tile)
            keep(j, h)

    for step, args in events[steps]:
        step(*args)

    @pl.loop(me + 1, n)
    def _(j):
        dkv_ref[j] = jnp.zeros(dkv_ref.shape[1:], b16)

    dq_ref[...] *= scale
    gate_out[...] = gate_sum.loc[0]
    up_out[...] = up_sum.loc[0]
    down_out[...] = down_sum.loc[0]
    for one in (gate_sum, up_sum, down_sum):
        one.finish()
    for j in range(max(n - 2, 0), n):
        staged(j).wait()


def attention_backward(queries, grad_attended, lse, all_kv, doc_column, doc_row, low, attended, grads):
    f32, b16 = jnp.float32, jnp.bfloat16
    kv, all_rows, _ = queries.shape
    n, rows, _ = all_kv.shape
    _, _, depth, ff = grads.shape
    pieces, m, piece, heads = attended.shape
    out = [(queries.shape, f32), (all_kv.shape, b16), ((depth, ff), b16), ((depth, ff), b16), ((depth, ff), b16),
           ((n, depth, m * heads), b16)]
    dma = pltpu.SemaphoreType.DMA
    return pl.pallas_call(
        backward_kernel,
        out_shape=[jax.ShapeDtypeStruct(*one) for one in out],
        in_specs=[VM] * 7 + [ANY] * 2,
        out_specs=[VM] * 5 + [ANY],
        scratch_shapes=[pltpu.VMEM(queries.shape, b16), pltpu.VMEM((kv, 1, all_rows), f32), pltpu.VMEM((kv, 1, all_rows), f32),
                        pltpu.VMEM((rows, HEAD_SIZE), f32), pltpu.VMEM((rows, HEAD_SIZE), f32), pltpu.VMEM((rows, rows), f32),
                        pltpu.VMEM((pieces, piece, heads), b16), pltpu.VMEM((pieces, m, piece // m, heads), b16),
                        pltpu.VMEM((2, depth, m * heads), b16), dma((2,)), dma((2,))]
        + sum_scratch(depth, ff) + sum_scratch(depth, ff) + sum_scratch(depth, ff),
        compiler_params=pltpu.CompilerParams(vmem_limit_bytes=VMEM_BYTES, collective_id=3, has_side_effects=True),
        name="attention_backward",
    )(queries, grad_attended, lse, all_kv, doc_column, doc_row, low, attended, grads)


def final_kernel(dq_in, proj_in, norm_in, w_in, cos_in, sin_in, after_in, gains_ref, mlp_gain_ref,
                 dkv_ref, o_grads_ref, tok_ref,
                 buf, o_out, w_out, gain_out, dq_ref, proj_ref, norm_ref, w_ref, cos_ref, sin_ref, after_ref,
                 dproj, part, recv, tok_own, w_grads, gain_seq, gain_line, o_part, o_recv, local_sem, *scratch):
    f32, b16 = jnp.float32, jnp.bfloat16
    pieces, m, sub, width = part.shape
    n, depth, wide = w_ref.shape
    kv, all_rows, _ = dq_ref.shape
    rows = norm_ref.shape[0]
    group = all_rows // rows
    q_width, k_width = kv * group * HEAD_SIZE, kv * HEAD_SIZE
    piece = m * sub
    me, t = lax.axis_index("seq"), lax.axis_index("tp")
    tile = cut(rows)
    kv_sum = seq_sum(lambda j: dkv_ref.at[j], scratch[:6])
    o_sum = seq_sum(lambda j: o_grads_ref.at[j], scratch[6:12])
    w_sum = seq_sum(lambda j: w_grads.at[j], scratch[12:18])
    in_sum = LineSum(part, recv, scratch[18], scratch[19])
    out_gather = LineGather(buf, scratch[20], scratch[21])
    gain_gather = SeqGather(gain_seq, scratch[22], scratch[23], halves=1)
    gain_total = LineGather(gain_line, scratch[24], scratch[25])
    o_total = DirectSum(o_part, o_recv, scratch[26], scratch[27])

    own = [pltpu.make_async_copy(tok_ref.at[p, t], tok_own.at[p], local_sem.at[p]) for p in range(pieces)]
    loads = [pltpu.make_async_copy(source, into, local_sem.at[pieces + i]) for i, (source, into) in enumerate((
        (dq_in, dq_ref), (proj_in, proj_ref), (cos_in, cos_ref), (sin_in, sin_ref), (norm_in, norm_ref), (w_in, w_ref),
        (after_in, after_ref)))]
    for copy in own + loads:
        copy.start()
    greet(True, "all")
    kv_sum.begin()
    gain_q, gain_k = gains_ref[0, 2:3, :HEAD_SIZE], gains_ref[0, 3:4, :HEAD_SIZE]
    for j in range(1, n):
        gain_q = gain_q + gains_ref[j, 2:3, :HEAD_SIZE]
        gain_k = gain_k + gains_ref[j, 3:4, :HEAD_SIZE]
    gain_seq[me] = jnp.zeros(gain_seq.shape[1:], f32)
    gain_seq[me, 1:2] = mlp_gain_ref[...]
    for p in range(pieces):
        in_sum.clear(p)
    for copy in own + loads:
        copy.wait()
    plan = Plan()

    def head_back(grad, at, first, gain):
        e = grad * cos_ref[at] - pltpu.roll(grad, HEAD_SIZE // 2, 1) * sin_ref[at]
        u = proj_ref[at, first:first + HEAD_SIZE]
        inverse = rms_inverse(u)
        normed = u * inverse
        scaled = e * gain
        back = inverse * (scaled - normed * jnp.mean(scaled * normed, axis=-1, keepdims=True))
        dproj[at, first:first + HEAD_SIZE] = back.astype(b16)
        return jnp.sum(e * normed, axis=0, keepdims=True)

    def queries_back(h, g):
        terms = jnp.zeros((1, HEAD_SIZE), f32)
        for start in range(0, rows, tile):
            grad = dq_ref[h, g * rows + start:g * rows + start + tile]
            terms += head_back(grad, slice(start, start + tile), (h * group + g) * HEAD_SIZE, gain_q)
        gain_seq[me, 2:3, :HEAD_SIZE] += terms

    def keys_back():
        for h in range(kv):
            cols = slice(h * HEAD_SIZE, (h + 1) * HEAD_SIZE)
            terms = jnp.zeros((1, HEAD_SIZE), f32)
            for start in range(0, rows, tile):
                at = slice(start, start + tile)
                terms += head_back(kv_sum.loc[0, at, cols].astype(f32), at, q_width + h * HEAD_SIZE, gain_k)
            gain_seq[me, 3:4, :HEAD_SIZE] += terms
        dproj[:, q_width + k_width:] = kv_sum.loc[0, :, k_width:]

    def in_part(p):
        for j in range(n):
            block = mm(dproj[p * piece:(p + 1) * piece], w_ref[j], NT)
            part[p, :, :, j * depth:(j + 1) * depth] = block.astype(b16).reshape(m, sub, depth)

    def weight_grads(j):
        w_grads[j] = mm(norm_ref[:, j * depth:(j + 1) * depth], dproj[...], TN).astype(b16)

    def norm_back(p):
        grad = in_sum.total(p)
        tok = tok_own[p].astype(f32)
        inverse = rms_inverse(tok)
        normed = tok * inverse
        mean = 0.0
        for j in range(n):
            cols = slice(j * depth, (j + 1) * depth)
            gain_seq[me, 0:1, cols] += jnp.sum(grad[:, cols] * normed[:, cols], axis=0, keepdims=True)
            mean = mean + jnp.sum(grad[:, cols] * gains_ref[j, 0:1, :depth] * normed[:, cols], axis=1, keepdims=True)
        mean = mean * (1.0 / width)
        for j in range(n):
            cols = slice(j * depth, (j + 1) * depth)
            back = inverse * (grad[:, cols] * gains_ref[j, 0:1, :depth] - normed[:, cols] * mean)
            buf[p, t, :, cols] = (after_ref[p, :, cols] + back).astype(b16)
        out_gather.start(p)

    def plan_sum(one, base, length):
        for e in reversed(range(one.count)):
            plan.at(base, one.meet, e)
        for k, found in enumerate(one.rounds()):
            for event in found:
                plan.at(base + length * (2.0 - 0.5 ** k), one.arrive, *event)

    for h in range(kv):
        for g in range(group):
            plan.at(1.0, queries_back, h, g)
    plan_sum(kv_sum, 7.0, 18.0)
    plan.at(30.0, o_sum.begin)
    plan.at(43.5, keys_back)
    clock = 44.0
    hop = 8.0
    last = 0.0
    for p in range(pieces):
        plan.at(clock, in_part, p)
        clock += 2.2
        start = 47.0 + 3 * hop * p
        for k in range(m - 1):
            plan.at(start + hop * k, in_sum.step, p, k)
        start += hop * (m - 1) + 1
        plan.at(start, norm_back, p)
        for d in range(1, m):
            last = start + hop * d
            plan.at(last, out_gather.arrive, p, d)
    for j in range(n):
        plan.at(50.0 + 0.8 * j, weight_grads, j)
    plan.at(57.0, w_sum.begin)
    plan_sum(o_sum, 56.0, 34.0)
    plan_sum(w_sum, 90.0, 22.0)

    def o_over_tp():
        heads = o_part.shape[3]
        for k in range(m):
            o_part[0, k] = o_sum.loc[0, :, k * heads:(k + 1) * heads]
        o_total.start(0)

    plan.at(108.5, o_over_tp)
    gain_time = last - 3 * hop + 0.5
    plan.at(gain_time, gain_gather.start, 0)
    for k, event in enumerate(gain_gather.events()):
        plan.at(gain_time + 1.0 + 0.5 * k, gain_gather.arrive, *event)

    def over_tp():
        total = gain_seq[0]
        for j in range(1, n):
            total = total + gain_seq[j]
        gain_line[0, t] = total
        gain_total.start(0)

    plan.at(gain_time + 1.0 + 0.5 * n, over_tp)
    for d in range(1, m):
        plan.at(gain_time + 2.0 + 0.5 * n + 2.0 * d, gain_total.arrive, 0, d)
    plan.run()

    total = gain_line[0, 0]
    for j in range(1, m):
        total = total + gain_line[0, j]
    gain_out[...] = total
    o_out[...] = o_total.total(0).T
    w_out[...] = w_sum.loc[0]
    for one in (kv_sum, o_sum, w_sum, gain_gather):
        one.finish()
    in_sum.finish(pieces - 1)
    for p in range(pieces):
        out_gather.finish(p)
    gain_total.finish(0)
    o_total.finish(0)


def final(grad_queries, projected, normalized, w_all, cosines, sines, after_grad, gains, mlp_gain, grad_kv, o_grads, tokens):
    f32, b16 = jnp.float32, jnp.bfloat16
    pieces, m, sub, width = tokens.shape
    n, depth, wide = w_all.shape
    kv, all_rows, _ = grad_queries.shape
    rows, k_width = normalized.shape[0], kv * HEAD_SIZE
    q_width = wide - 2 * k_width
    out = [(tokens.shape, b16), ((q_width, depth), f32), ((depth, wide), b16), ((8, width), f32)]
    held = (grad_queries, projected, normalized, w_all, cosines, sines, after_grad)
    return pl.pallas_call(
        final_kernel,
        out_shape=[jax.ShapeDtypeStruct(*one) for one in out],
        in_specs=[ANY] * 7 + [VM] * 2 + [ANY] * 3,
        out_specs=[VM] * 4,
        scratch_shapes=[pltpu.VMEM(one.shape, one.dtype) for one in held] + [pltpu.VMEM((rows, wide), b16), pltpu.VMEM(tokens.shape, b16),
                        pltpu.VMEM((pieces, m + 1, sub, width), b16), pltpu.VMEM((pieces, sub, width), b16),
                        pltpu.VMEM((n, depth, wide), b16), pltpu.VMEM((n, 8, width), f32), pltpu.VMEM((1, m, 8, width), f32),
                        pltpu.VMEM((1, m, depth, q_width), b16), pltpu.VMEM((1, m, depth, q_width), b16),
                        pltpu.SemaphoreType.DMA((pieces + 7,))]
        + sum_scratch(rows, 2 * k_width) + sum_scratch(depth, m * q_width) + sum_scratch(depth, wide)
        + line_sems(pieces) + gather_sems(1) + line_sems(1)[2:]
        + [pltpu.SemaphoreType.DMA((1, m)), pltpu.SemaphoreType.DMA((1, m))],
        compiler_params=pltpu.CompilerParams(vmem_limit_bytes=VMEM_BYTES, collective_id=4, has_side_effects=True),
        name="final",
    )(grad_queries, projected, normalized, w_all, cosines, sines, after_grad, gains, mlp_gain, grad_kv, o_grads, tokens)


def finish_kernel(tokens_ref, layer_ref, gate_ref, up_ref, down_ref, o_ref, w_ref,
                  tokens_out, layer_out, gate_out, up_out, down_out, o_out, q_out, k_out, v_out):
    f32 = jnp.float32
    tile = cut(tokens_ref.shape[0], 128)

    @pl.loop(0, tokens_ref.shape[0] // tile)
    def _(i):
        at = pl.ds(i * tile, tile)
        tokens_out[at] = tokens_ref[at].astype(f32)
        layer_out[at] = layer_ref[at]

    gate_out[...] = gate_ref[...].astype(f32)
    up_out[...] = up_ref[...].astype(f32)
    down_out[...] = down_ref[...].astype(f32).T
    o_out[...] = o_ref[...]
    first = 0
    for out in (q_out, k_out, v_out):
        out[...] = w_ref[:, first:first + out.shape[1]].astype(f32)
        first += out.shape[1]


def finish(tokens, layer, gate, up, down, o, w, q_width):
    f32 = jnp.float32
    depth, ff = gate.shape
    k_width = (w.shape[1] - q_width) // 2
    out = [(tokens.shape, f32), (layer.shape, layer.dtype), (gate.shape, f32), (up.shape, f32), ((ff, depth), f32), (o.shape, f32),
           ((depth, q_width), f32), ((depth, k_width), f32), ((depth, k_width), f32)]
    return pl.pallas_call(
        finish_kernel,
        out_shape=[jax.ShapeDtypeStruct(*one) for one in out],
        in_specs=[VM] * 7, out_specs=[VM] * 9,
        compiler_params=pltpu.CompilerParams(vmem_limit_bytes=VMEM_BYTES),
        name="finish",
    )(tokens, layer, gate, up, down, o, w)


def pack_gains(attn_gain, mlp_gain, query_gain, key_gain):
    width = max(attn_gain.shape[0], HEAD_SIZE)
    place = lax.axis_index("seq") * query_gain.shape[0]

    def placed(gain):
        return lax.dynamic_update_slice(jnp.zeros((width,), jnp.float32), gain.astype(jnp.float32), (place,))

    def padded(gain):
        return jnp.pad(gain.astype(jnp.float32), (0, width - gain.shape[0]))

    lines = [padded(attn_gain), padded(mlp_gain), placed(query_gain), placed(key_gain)]
    return jnp.stack(lines + [jnp.zeros((width,), jnp.float32)] * 4)


def norm_rows(values, gain_vec):
    return values * lax.rsqrt(jnp.mean(values * values, axis=-1, keepdims=True) + EPS) * gain_vec


def norm_back(values, gain_vec, grad_out):
    inverse = lax.rsqrt(jnp.mean(values * values, axis=-1, keepdims=True) + EPS)
    normed = values * inverse
    scaled = grad_out * gain_vec
    grad_in = inverse * (scaled - normed * jnp.mean(scaled * normed, axis=-1, keepdims=True))
    return (grad_in, grad_out * normed)


def rope_tables(positions, head_dim):
    half_dim = head_dim // 2
    frequency = BASE ** (-2.0 * jnp.arange(half_dim, dtype=jnp.float32) / head_dim)
    angles = positions.astype(jnp.float32)[:, None] * frequency[None, :]
    return (jnp.cos(angles)[:, None, :], jnp.sin(angles)[:, None, :])


def rotate(values, cosines, sine_values, direction):
    half_dim = values.shape[-1] // 2
    lower_half = values[..., :half_dim]
    upper_half = values[..., half_dim:]
    signed = sine_values * direction
    return jnp.concatenate(
        [lower_half * cosines - upper_half * signed, upper_half * cosines + lower_half * signed],
        axis=-1,
    )


def per_device(
    tokens,
    q_weight,
    key_matrix,
    value_matrix,
    o_weight,
    gate_weight,
    up_weight,
    down_weight,
    attn_gain,
    mlp_gain,
    query_gain,
    key_gain,
    positions,
    seq_ids,
    cotangent,
):
    f32 = jnp.float32
    b16 = jnp.bfloat16
    local_rows = tokens.shape[0]
    q_local = q_weight.shape[1] // HEAD_SIZE
    kv_local = key_matrix.shape[1] // HEAD_SIZE
    heads_per_group = q_local // kv_local
    share_rows = local_rows // lax.axis_size("tp")
    share_start = lax.axis_index("tp") * share_rows
    s = lax.axis_index("seq")
    own_docs = lax.dynamic_slice_in_dim(seq_ids, s * local_rows, local_rows)
    doc_column, doc_row = own_docs[:, None], own_docs[None, :]
    seq_count = lax.axis_size("seq")
    gains = pack_gains(attn_gain, mlp_gain, query_gain, key_gain)
    cosines, sine_values = rope_tables(positions, HEAD_SIZE)
    cos_wide = jnp.concatenate([cosines, cosines], axis=-1).reshape(local_rows, HEAD_SIZE)
    sin_wide = jnp.concatenate([-sine_values, sine_values], axis=-1).reshape(local_rows, HEAD_SIZE)
    model = tokens.shape[1]
    tp_count = lax.axis_size("tp")
    sub = math.gcd(local_rows // tp_count, 64)
    while local_rows // tp_count // sub > 3:
        sub *= 2
    split = (local_rows // tp_count // sub, tp_count, sub, model)
    (normalized_input, projected, queries_h, all_kv, attended_all, lse, all_gains, w_all, o_all, gate_all) = forward_attention(
        tokens, q_weight, key_matrix, value_matrix, gains, cos_wide, sin_wide, doc_column, doc_row, o_weight, gate_weight, split[0])
    ff = gate_weight.shape[1]
    q_width, k_width = q_local * HEAD_SIZE, kv_local * HEAD_SIZE
    low_own, after_grad_own, grad_attended, mlp_gain_own, mlp_part, mlp_grads = middle(
        attended_all, o_all, gate_all, up_weight, down_weight, tokens.reshape(split), cotangent.reshape(split), all_gains)
    layer_out = lax.psum(mlp_part, "tp").reshape(local_rows, model)

    q_width = q_local * HEAD_SIZE
    grad_query_h, grad_kv, gate_sum, up_sum, down_sum, o_grads = attention_backward(
        queries_h, grad_attended.reshape(local_rows, q_width), lse, all_kv, doc_column, doc_row, low_own, attended_all, mlp_grads)
    token_blocks, grad_o, grad_w, gain_sums = final(
        grad_query_h, projected, normalized_input, w_all, cos_wide, sin_wide, after_grad_own, all_gains, mlp_gain_own,
        grad_kv, o_grads, tokens.reshape(split))
    (grad_tokens, layer_out, grad_gate_w, grad_up_w, grad_down, grad_o_w, grad_q_w, grad_k_w, grad_v_w) = finish(
        token_blocks.reshape(local_rows, model), layer_out, gate_sum, up_sum, down_sum, grad_o, grad_w, q_width)

    def own_part(line, width):
        count = width // seq_count
        return lax.dynamic_slice_in_dim(gain_sums[line], s * count, count)

    return (
        layer_out,
        grad_tokens,
        grad_q_w,
        grad_k_w,
        grad_v_w,
        grad_o_w,
        grad_gate_w,
        grad_up_w,
        grad_down,
        own_part(0, model),
        own_part(1, model),
        own_part(2, HEAD_SIZE),
        own_part(3, HEAD_SIZE),
    )


def solution(mesh):
    placed = (
        P("seq", None),
        P("seq", "tp"),
        P("seq", "tp"),
        P("seq", "tp"),
        P("tp", "seq"),
        P("seq", "tp"),
        P("seq", "tp"),
        P("tp", "seq"),
        P("seq"),
        P("seq"),
        P("seq"),
        P("seq"),
        P("seq"),
        P(),
        P("seq", None),
    )
    return jax.shard_map(
        per_device,
        mesh=mesh,
        in_specs=placed,
        out_specs=(
            P("seq", None),
            P("seq", None),
            P("seq", "tp"),
            P("seq", "tp"),
            P("seq", "tp"),
            P("tp", "seq"),
            P("seq", "tp"),
            P("seq", "tp"),
            P("tp", "seq"),
            P("seq"),
            P("seq"),
            P("seq"),
            P("seq"),
        ),
        check_vma=False,
    )
```

```python
import functools
import math

import jax
import jax.numpy as jnp
from jax import lax
from jax.experimental import pallas as pl
from jax.experimental.pallas import tpu as pltpu

from jax.sharding import PartitionSpec as P

HEAD_SIZE = 128
EPS = 1e-06
BASE = 1000000.0
LOG2E = 1.4426950408889634
VMEM_BYTES = 62 << 20
NT = (((1,), (1,)), ((), ()))
TN = (((0,), (0,)), ((), ()))


def mm(a, b, dims=(((1,), (0,)), ((), ()))):
    return lax.dot_general(a, b, dims, preferred_element_type=jnp.float32)


def cut(rows, most=256):
    return math.gcd(rows, most)


MESH = pl.DeviceIdType.MESH
ANY = pl.BlockSpec(memory_space=pl.ANY)
VM = pl.BlockSpec(memory_space=pltpu.VMEM)


def bit_of(index, bit):
    return lax.rem(index // (1 << bit), 2)


def toggled(index, offset, bits):
    for bit in range(bits):
        if offset >> bit & 1:
            index = index + (1 - 2 * bit_of(index, bit)) * (1 << bit)
    return index


def seq_bits():
    return lax.axis_size("seq").bit_length() - 1


def bit_order(half):
    outer = list(range(1, seq_bits()))
    return (outer if half == 0 else outer[::-1]) + [0]


def last_bit(half, offset):
    return [b for b in bit_order(half) if offset >> b & 1][-1]


def greet(over_seq, over_tp):
    barrier = pltpu.get_barrier_semaphore()
    s, t, count = lax.axis_index("seq"), lax.axis_index("tp"), lax.axis_size("tp")
    expected = 0
    if over_seq:
        for bit in range(seq_bits()):
            pl.semaphore_signal(barrier, inc=1, device_id=(toggled(s, 1 << bit, seq_bits()), t), device_id_type=MESH)
        expected = seq_bits()
    if over_tp == "all":
        for j in range(count):
            @pl.when(t != j)
            def _(j=j):
                pl.semaphore_signal(barrier, inc=1, device_id=(s, j), device_id_type=MESH)
        expected = expected + count - 1
    elif over_tp:
        @pl.when(t > 0)
        def _():
            pl.semaphore_signal(barrier, inc=1, device_id=(s, t - 1), device_id_type=MESH)

        @pl.when(t < count - 1)
        def _():
            pl.semaphore_signal(barrier, inc=1, device_id=(s, t + 1), device_id_type=MESH)

        expected = expected + jnp.where(t > 0, 1, 0) + jnp.where(t < count - 1, 1, 0)
    pl.semaphore_wait(barrier, expected)


class SeqGather:
    def __init__(self, buf, send, recv, halves=2):
        self.buf, self.send, self.recv, self.halves = buf, send, recv, halves
        self.bits = seq_bits()
        self.n = 1 << self.bits
        self.me, self.t = lax.axis_index("seq"), lax.axis_index("tp")

    def block(self, half, offset):
        rows = self.buf.shape[1] // self.halves
        return self.buf.at[toggled(self.me, offset, self.bits), pl.ds(half * rows, rows)]

    def copy(self, half, offset):
        bit = last_bit(half, offset)
        ref = self.block(half, offset ^ (1 << bit))
        return pltpu.make_async_remote_copy(
            src_ref=ref, dst_ref=ref, send_sem=self.send.at[half, offset], recv_sem=self.recv.at[half, offset],
            device_id=(toggled(self.me, 1 << bit, self.bits), self.t), device_id_type=MESH)

    def start(self, half):
        for bit in bit_order(half):
            self.copy(half, 1 << bit).start()

    def arrive(self, half, offset):
        ref = self.block(half, offset)
        pltpu.make_async_remote_copy(
            src_ref=ref, dst_ref=ref, send_sem=self.send.at[half, offset], recv_sem=self.recv.at[half, offset],
            device_id=(self.me, self.t), device_id_type=MESH).wait_recv()
        order = bit_order(half)
        for bit in order[order.index(last_bit(half, offset)) + 1:]:
            self.copy(half, offset | 1 << bit).start()

    def finish(self):
        for half in range(self.halves):
            for offset in range(1, self.n):
                self.copy(half, offset).wait_send()

    def level(self, half, offset):
        order = bit_order(half)
        return sum(2 ** order.index(b) for b in range(1, self.bits) if offset >> b & 1)

    def events(self):
        def due(event):
            return self.level(*event), event[1] & 1, event[0]
        return sorted(((h, r) for h in range(self.halves) for r in range(1, self.n)), key=due)


def gather_sems(halves=2):
    n = lax.axis_size("seq")
    return [pltpu.SemaphoreType.DMA((halves, n)), pltpu.SemaphoreType.DMA((halves, n))]


class LineSum:
    def __init__(self, part, recv, send_sem, recv_sem):
        self.part, self.recv, self.send_sem, self.recv_sem = part, recv, send_sem, recv_sem
        self.m = part.shape[1]
        self.s, self.t = lax.axis_index("seq"), lax.axis_index("tp")

    def copy(self, p, j, slot, to):
        return pltpu.make_async_remote_copy(
            src_ref=self.part.at[p, j], dst_ref=self.recv.at[p, slot], send_sem=self.send_sem.at[p, j],
            recv_sem=self.recv_sem.at[p, slot], device_id=(self.s, to), device_id_type=MESH)

    def add(self, p, j):
        self.copy(p, j, j, self.t).wait_recv()
        self.part[p, j] = (self.part[p, j].astype(jnp.float32) + self.recv[p, j].astype(jnp.float32)).astype(jnp.bfloat16)

    def left(self, p, j):
        @pl.when(self.t > j)
        def _():
            @pl.when(self.t < self.m - 1)
            def _():
                self.add(p, j)

            self.sent(p, j - 1, j > 0)
            if p > 0 and j == 0:
                self.sent(p - 1, self.t - 1, True)
            self.copy(p, j, j, self.t - 1).start()

    def right(self, p, j):
        @pl.when(self.t < j)
        def _():
            @pl.when(self.t > 0)
            def _():
                self.add(p, j)

            self.sent(p, j + 1, j < self.m - 1)
            if p > 0 and j == self.m - 1:
                self.sent(p - 1, self.t + 1, True)
            self.copy(p, j, jnp.where(self.t + 1 == j, self.m, j), self.t + 1).start()

    def sent(self, p, j, some):
        if some:
            self.copy(p, j, j, self.t).wait_send()

    def step(self, p, k):
        self.left(p, k)
        self.right(p, self.m - 1 - k)

    def clear(self, p):
        @pl.when(self.t == self.m - 1)
        def _():
            self.recv[p, self.m - 1] = jnp.zeros(self.recv.shape[2:], self.recv.dtype)

        @pl.when(self.t == 0)
        def _():
            self.recv[p, self.m] = jnp.zeros(self.recv.shape[2:], self.recv.dtype)

    def total(self, p):
        @pl.when(self.t < self.m - 1)
        def _():
            self.copy(p, self.t, self.t, self.t).wait_recv()

        @pl.when(self.t > 0)
        def _():
            self.copy(p, self.t, self.m, self.t).wait_recv()

        f32 = jnp.float32
        return self.part[p, self.t].astype(f32) + (self.recv[p, self.t].astype(f32) + self.recv[p, self.m].astype(f32))

    def finish(self, p):
        @pl.when(self.t > 0)
        def _():
            self.copy(p, self.t - 1, 0, self.t).wait_send()

        @pl.when(self.t < self.m - 1)
        def _():
            self.copy(p, self.t + 1, 0, self.t).wait_send()


class DirectSum:
    def __init__(self, part, recv, send_sem, recv_sem):
        self.part, self.recv, self.send_sem, self.recv_sem = part, recv, send_sem, recv_sem
        self.m = part.shape[1]
        self.s, self.t = lax.axis_index("seq"), lax.axis_index("tp")

    def copy(self, p, j, sender):
        return pltpu.make_async_remote_copy(
            src_ref=self.part.at[p, j], dst_ref=self.recv.at[p, sender], send_sem=self.send_sem.at[p, j],
            recv_sem=self.recv_sem.at[p, sender], device_id=(self.s, j), device_id_type=MESH)

    def others(self, act):
        for j in range(self.m):
            @pl.when(self.t != j)
            def _(j=j):
                act(j)

    def start(self, p):
        self.others(lambda j: self.copy(p, j, self.t).start())
        self.recv[p, self.t] = self.part[p, self.t]

    def total(self, p):
        self.others(lambda j: self.copy(p, j, j).wait_recv())
        total = self.recv[p, 0].astype(jnp.float32)
        for j in range(1, self.m):
            total = total + self.recv[p, j].astype(jnp.float32)
        return total

    def finish(self, p):
        self.others(lambda j: self.copy(p, j, self.t).wait_send())


class LineGather:
    def __init__(self, buf, send_sem, recv_sem):
        self.buf, self.send_sem, self.recv_sem = buf, send_sem, recv_sem
        self.m = buf.shape[1]
        self.s, self.t = lax.axis_index("seq"), lax.axis_index("tp")

    def copy(self, p, j, way):
        ref = self.buf.at[p, j]
        return pltpu.make_async_remote_copy(
            src_ref=ref, dst_ref=ref, send_sem=self.send_sem.at[p, way, j], recv_sem=self.recv_sem.at[p, j],
            device_id=(self.s, self.t + (2 * way - 1)), device_id_type=MESH)

    def pass_on(self, p, j, way):
        @pl.when(self.t > 0 if way == 0 else self.t < self.m - 1)
        def _():
            self.copy(p, j, way).start()

    def start(self, p):
        self.pass_on(p, self.t, 0)
        self.pass_on(p, self.t, 1)

    def arrive(self, p, distance):
        @pl.when(self.t + distance < self.m)
        def _():
            self.copy(p, self.t + distance, 0).wait_recv()
            self.pass_on(p, self.t + distance, 0)

        @pl.when(self.t >= distance)
        def _():
            self.copy(p, self.t - distance, 1).wait_recv()
            self.pass_on(p, self.t - distance, 1)

    def finish(self, p):
        for j in range(self.m):
            @pl.when((self.t > 0) & (self.t <= j))
            def _(j=j):
                self.copy(p, j, 0).wait_send()

            @pl.when((self.t < self.m - 1) & (self.t >= j))
            def _(j=j):
                self.copy(p, j, 1).wait_send()


def line_sems(pieces):
    m = lax.axis_size("tp")
    return [pltpu.SemaphoreType.DMA((pieces, m)), pltpu.SemaphoreType.DMA((pieces, m + 1)),
            pltpu.SemaphoreType.DMA((pieces, 2, m)), pltpu.SemaphoreType.DMA((pieces, m))]


class Plan:
    def __init__(self):
        self.steps = []

    def at(self, time, step, *args):
        self.steps.append((time, len(self.steps), step, args))

    def run(self):
        for _, _, step, args in sorted(self.steps, key=lambda one: one[:2]):
            step(*args)


def attn_fwd_block(q_ref, kv_ref, out_ref, sum_ref, bias_ref, kv, rows, tile):
    scale = HEAD_SIZE ** -0.5 * LOG2E
    all_rows = q_ref.shape[1]
    for h in range(kv):
        cols = slice(h * HEAD_SIZE, (h + 1) * HEAD_SIZE)
        v_cols = slice((kv + h) * HEAD_SIZE, (kv + h + 1) * HEAD_SIZE)
        for start in range(0, all_rows, tile):
            at = start % rows
            n_keys = rows if bias_ref is None else at + tile
            scores = mm(q_ref[h, start:start + tile], kv_ref[:n_keys, cols], NT) * scale
            if bias_ref is not None:
                scores = scores + bias_ref[at:at + tile, :n_keys]
            weights = jnp.exp2(scores)
            part = weights[:, :HEAD_SIZE]
            for c in range(HEAD_SIZE, n_keys, HEAD_SIZE):
                part = part + weights[:, c:c + HEAD_SIZE]
            sum_ref[h, start:start + tile] += part
            out_ref[h, start:start + tile] += mm(weights.astype(jnp.bfloat16), kv_ref[:n_keys, v_cols])


def rms_inverse(values):
    return lax.rsqrt(jnp.mean(values * values, axis=-1, keepdims=True) + EPS)


def forward_kernel(tok_in, wq_ref, wk_ref, wv_ref, gain_ref, cos_ref, sin_ref, qd_ref, kd_ref, o_ref, gate_ref,
                   norm_out, proj_out, q_ref, kv_out, att_all, lse_ref, gains_ref, w_out, o_all, gate_all,
                   tok_ref, norm_ref, proj_ref, kv_ref, w, inv, acc, total, bias, local_sem, *sems):
    f32, b16 = jnp.float32, jnp.bfloat16
    n, rows, _ = kv_ref.shape
    kv, all_rows, _ = q_ref.shape
    group = all_rows // rows
    me = lax.axis_index("seq")
    bits = seq_bits()
    tile = cut(rows)
    depth = w.shape[1]
    q_width, k_width = wq_ref.shape[1], wk_ref.shape[1]
    w_gather = SeqGather(w, sems[0], sems[1])
    gain_gather = SeqGather(gains_ref, sems[2], sems[3], halves=1)
    kv_gather = SeqGather(kv_ref, sems[4], sems[5])
    o_gather = SeqGather(o_all, sems[6], sems[7])
    gate_gather = SeqGather(gate_all, sems[8], sems[9])
    o_line = LineGather(o_all.at[pl.ds(me, 1)], sems[10], sems[11])
    att_gather = LineGather(att_all, sems[12], sems[13])
    t, m = lax.axis_index("tp"), lax.axis_size("tp")
    pieces, _, piece, _ = att_all.shape

    own = [pltpu.make_async_copy(wq_ref, w.at[me, :, pl.ds(0, q_width)], local_sem.at[0]),
           pltpu.make_async_copy(wk_ref, w.at[me, :, pl.ds(q_width, k_width)], local_sem.at[1]),
           pltpu.make_async_copy(wv_ref, w.at[me, :, pl.ds(q_width + k_width, k_width)], local_sem.at[2]),
           pltpu.make_async_copy(o_ref, o_all.at[me, t], local_sem.at[3]),
           pltpu.make_async_copy(gate_ref, gate_all.at[me], local_sem.at[4])]
    tok_copy = pltpu.make_async_copy(tok_in, tok_ref, local_sem.at[5])
    results = [pltpu.make_async_copy(here, there, local_sem.at[6 + i]) for i, (here, there) in enumerate(
        ((norm_ref, norm_out), (proj_ref, proj_out), (w, w_out), (kv_ref, kv_out)))]
    for copy in own + [tok_copy]:
        copy.start()
    gains_ref[me] = gain_ref[...]
    greet(True, True)
    for copy in own[:3]:
        copy.wait()
    w_gather.start(0)
    w_gather.start(1)
    gain_gather.start(0)
    own[3].wait()
    o_line.start(0)

    tok_copy.wait()

    @pl.loop(0, rows // tile)
    def _(i):
        at = pl.ds(i * tile, tile)
        inv[at] = rms_inverse(tok_ref[at].astype(f32))

    visible = (lax.broadcasted_iota(jnp.int32, (rows, rows), 1)
               <= lax.broadcasted_iota(jnp.int32, (rows, rows), 0)) & (qd_ref[...] == kd_ref[...])
    bias[...] = jnp.where(visible, 0.0, -1e30)
    for event in gain_gather.events():
        gain_gather.arrive(*event)

    def project(offset):
        source = toggled(me, offset, bits)
        cols = pl.ds(pl.multiple_of(source * depth, depth), depth)

        @pl.loop(0, rows // tile)
        def _(i):
            at = pl.ds(i * tile, tile)
            block = (tok_ref[at, cols].astype(f32) * inv[at] * gains_ref[source, 0:1, :depth]).astype(b16)
            norm_ref[at, cols] = block
            part = mm(block, w[source])
            if offset == 0:
                proj_ref[at] = part
            else:
                proj_ref[at] += part

    project(0)
    came = {}
    hops = [len(w_gather.events()) * d // m for d in range(1, m)]
    for i, (half, offset) in enumerate(w_gather.events()):
        if i in hops:
            o_line.arrive(0, hops.index(i) + 1)
        w_gather.arrive(half, offset)
        came[offset] = came.get(offset, 0) + 1
        if came[offset] == 2:
            project(offset)

    own[4].wait()
    gain_q, gain_k = gains_ref[0, 2:3, :HEAD_SIZE], gains_ref[0, 3:4, :HEAD_SIZE]
    for j in range(1, n):
        gain_q = gain_q + gains_ref[j, 2:3, :HEAD_SIZE]
        gain_k = gain_k + gains_ref[j, 3:4, :HEAD_SIZE]

    def rotated(at, first, gain):
        u = proj_ref[at, first:first + HEAD_SIZE]
        u = u * rms_inverse(u) * gain
        return (u * cos_ref[at] + pltpu.roll(u, HEAD_SIZE // 2, 1) * sin_ref[at]).astype(b16)

    @pl.loop(0, rows // tile)
    def _(i):
        at = pl.ds(i * tile, tile)
        for h in range(kv):
            kv_ref[me, at, h * HEAD_SIZE:(h + 1) * HEAD_SIZE] = rotated(at, q_width + h * HEAD_SIZE, gain_k)
        kv_ref[me, at, k_width:] = proj_ref[at, q_width + k_width:].astype(b16)

    kv_gather.start(0)
    kv_gather.start(1)

    @pl.loop(0, rows // tile)
    def _(i):
        at = pl.ds(i * tile, tile)
        for h in range(kv):
            for g in range(group):
                q_ref[h, pl.ds(g * rows + i * tile, tile)] = rotated(at, (h * group + g) * HEAD_SIZE, gain_q)

    for copy in results[:3]:
        copy.start()
    acc[...] = jnp.zeros_like(acc)
    total[...] = jnp.zeros_like(total)
    attn_fwd_block(q_ref, kv_ref.at[me], acc.at[0], total.at[0], bias, kv, rows, tile)
    kv_steps = [[] for _ in range(n)]
    seen = set()
    order = kv_gather.events()
    offsets = sorted(range(1, n), key=lambda r: max(order.index((h, r)) for h in range(2)))
    taken = 0
    for k, offset in enumerate(offsets):
        need = max(order.index((h, offset)) for h in range(2)) + 1
        kv_steps[k] = order[taken:max(need, taken)]
        taken = max(need, taken)
    only_first = jnp.where(qd_ref[...] == 0, 1.0, 0.0)

    def attended(p):
        for h in range(kv):
            for g in range(group):
                for start in range(p * piece, (p + 1) * piece, tile):
                    at = slice(g * rows + start, g * rows + start + tile)
                    total_row = total[0, h, at] + total[1, h, at] * only_first[start:start + tile]
                    out = acc[0, h, at] + acc[1, h, at] * only_first[start:start + tile]
                    cols = slice((h * group + g) * HEAD_SIZE, (h * group + g + 1) * HEAD_SIZE)
                    out = (out / jnp.sum(total_row, axis=1, keepdims=True)).astype(b16)
                    att_all[p, t, start - p * piece:start - p * piece + tile, cols] = out
                    lse_ref[h, :, at] = jnp.log2(jnp.sum(total_row.T, axis=0, keepdims=True))
        att_gather.start(p)

    @pl.loop(0, n - 1)
    def _(k):
        source = 0
        for i, offset in enumerate(offsets):
            source = source + jnp.where(k == i, toggled(me, offset, bits), 0)

            @pl.when(k == i)
            def _(i=i):
                for event in kv_steps[i]:
                    kv_gather.arrive(*event)
                if i == max(n - 6, 0):
                    for gather in (o_gather, gate_gather):
                        gather.start(0)
                        gather.start(1)

        @pl.when(source < me)
        def _():
            attn_fwd_block(q_ref, kv_ref.at[source], acc.at[1], total.at[1], None, kv, rows, tile)

    results[3].start()
    plan = Plan()
    for p in range(pieces):
        plan.at(p, attended, p)
        for d in range(1, m):
            plan.at(pieces + 6.0 * (pieces * (d - 1) + p + 1), att_gather.arrive, p, d)
    for gather in (o_gather, gate_gather):
        for event in gather.events():
            plan.at((4.0, 25.0, 42.0, 48.0)[min(gather.level(*event), 3)], gather.arrive, *event)
    plan.run()
    for copy in results:
        copy.wait()
    o_line.finish(0)
    for p in range(pieces):
        att_gather.finish(p)
    for gather in (w_gather, gain_gather, kv_gather, o_gather, gate_gather):
        gather.finish()


def forward_attention(tokens, q_weight, key_matrix, value_matrix, gains, cosines, sines, doc_column, doc_row, o_weight, gate_weight, pieces):
    n, m = lax.axis_size("seq"), lax.axis_size("tp")
    rows, width = tokens.shape
    depth, q_width = q_weight.shape
    k_width = key_matrix.shape[1]
    kv, group = k_width // HEAD_SIZE, q_width // k_width
    f32, b16 = jnp.float32, jnp.bfloat16
    wide = q_width + 2 * k_width
    heads = (kv, group * rows, HEAD_SIZE)
    out = [((rows, width), b16), ((rows, wide), f32), (heads, b16), ((n, rows, 2 * k_width), b16), ((pieces, m, rows // pieces, q_width), b16),
           ((kv, 1, group * rows), f32), ((n,) + gains.shape, f32), ((n, depth, wide), b16), ((n, m) + o_weight.shape, b16), ((n,) + gate_weight.shape, b16)]
    sems = []
    for halves in (2, 1, 2, 2, 2):
        sems += gather_sems(halves)
    sems += line_sems(1)[2:] + line_sems(pieces)[2:]
    return pl.pallas_call(
        forward_kernel,
        out_shape=[jax.ShapeDtypeStruct(*one) for one in out],
        in_specs=[ANY] * 4 + [VM] * 5 + [ANY] * 2,
        out_specs=[ANY, ANY, VM, ANY, VM, VM, VM, ANY, ANY, ANY],
        scratch_shapes=[pltpu.VMEM((rows, width), b16), pltpu.VMEM((rows, width), b16), pltpu.VMEM((rows, wide), f32),
                        pltpu.VMEM((n, rows, 2 * k_width), b16), pltpu.VMEM((n, depth, wide), b16), pltpu.VMEM((rows, 1), f32), pltpu.VMEM((2,) + heads, f32),
                        pltpu.VMEM((2,) + heads, f32), pltpu.VMEM((rows, rows), f32), pltpu.SemaphoreType.DMA((10,))] + sems,
        compiler_params=pltpu.CompilerParams(vmem_limit_bytes=VMEM_BYTES, collective_id=1, has_side_effects=True),
        name="forward_attention",
    )(tokens, q_weight, key_matrix, value_matrix, gains, cosines, sines, doc_column, doc_row, o_weight, gate_weight)


class SeqSum:
    def __init__(self, source, loc, near, far, sems):
        self.source, self.loc, self.near, self.far = source, loc, near, far
        self.load_sem, self.near_sem, self.far_sem = sems
        self.bits = seq_bits()
        self.count = 1 << (self.bits - 1)
        self.me, self.t = lax.axis_index("seq"), lax.axis_index("tp")
        self.half_rows = loc.shape[1] // 2

    def first(self, half, e):
        order = bit_order(half)[:-1]
        return min(order.index(b) for b in range(1, self.bits) if 2 * e >> b & 1)

    def load(self, e):
        return pltpu.make_async_copy(self.source(toggled(self.me, 2 * e, self.bits)), self.loc.at[e], self.load_sem.at[e])

    def cross(self, e):
        return pltpu.make_async_remote_copy(
            src_ref=self.source(toggled(self.me, 2 * e + 1, self.bits)), dst_ref=self.near.at[e],
            send_sem=self.near_sem.at[0, e], recv_sem=self.near_sem.at[1, e],
            device_id=(toggled(self.me, 1, self.bits), self.t), device_id_type=MESH)

    def begin(self):
        for e in reversed(range(self.count)):
            self.cross(e).start()
            self.load(e).start()

    def meet(self, e):
        self.load(e).wait()
        self.cross(e).wait_recv()
        self.loc[e] += self.near[e]
        for half in range(2):
            if e and self.first(half, e) == 0:
                self.hop(half, e).start()

    def hop(self, half, e):
        bit = bit_order(half)[self.first(half, e)]
        return pltpu.make_async_remote_copy(
            src_ref=self.loc.at[e, pl.ds(half * self.half_rows, self.half_rows)], dst_ref=self.far.at[half, e - 1],
            send_sem=self.far_sem.at[0, half, e - 1], recv_sem=self.far_sem.at[1, half, e - 1],
            device_id=(toggled(self.me, 1 << bit, self.bits), self.t), device_id_type=MESH)

    def arrive(self, half, e):
        place = self.first(half, e)
        to = (2 * e ^ 1 << bit_order(half)[place]) // 2
        self.hop(half, e).wait_recv()
        self.loc[to, half * self.half_rows:(half + 1) * self.half_rows] += self.far[half, e - 1]
        if to and self.first(half, to) == place + 1:
            self.hop(half, to).start()

    def rounds(self):
        found = [[] for _ in range(self.bits - 1)]
        for e in reversed(range(1, self.count)):
            for half in range(2):
                found[self.first(half, e)].append((half, e))
        return found

    def finish(self):
        for e in range(self.count):
            self.cross(e).wait_send()
            for half in range(2 if e else 0):
                self.hop(half, e).wait_send()


def sum_scratch(rows, columns):
    count = lax.axis_size("seq") // 2
    b16 = jnp.bfloat16
    return [pltpu.VMEM((count, rows, columns), b16), pltpu.VMEM((count, rows, columns), b16),
            pltpu.VMEM((2, max(count - 1, 1), rows // 2, columns), b16), pltpu.SemaphoreType.DMA((count,)),
            pltpu.SemaphoreType.DMA((2, count)), pltpu.SemaphoreType.DMA((2, 2, max(count - 1, 1)))]


SUM_SCRATCH = 6


def seq_sum(source, scratch):
    return SeqSum(source, *scratch[:3], scratch[3:])


def middle_kernel(att_ref, o_ref, gate_ref, up_ref, down_ref, tok_ref, cot_in, gains_ref,
                  low_ref, after_grad_ref, do_ref, gain_out, mlp_ref, grads_ref,
                  o_all, gate_all, up_all, down_all, cot_ref, part, recv, norm_mid, act, gg, gu, after, after_own, att, rows_buf,
                  do_send, stage, local_sem, att_sem, rows_sem, stage_sem, do_send_sem, do_recv_sem, *sems):
    f32, b16 = jnp.float32, jnp.bfloat16
    pieces, m, sub, width = cot_ref.shape
    n, depth, ff = gate_all.shape
    piece = m * sub
    me, t = lax.axis_index("seq"), lax.axis_index("tp")
    up_gather = SeqGather(up_all, sems[0], sems[1])
    down_gather = SeqGather(down_all, sems[2], sems[3])
    mid_sum = DirectSum(part, recv, sems[4], sems[5])

    whole = [pltpu.make_async_copy(up_ref, up_all.at[me], local_sem.at[0]),
             pltpu.make_async_copy(down_ref, down_all.at[me], local_sem.at[1]),
             pltpu.make_async_copy(o_ref, o_all, local_sem.at[2]),
             pltpu.make_async_copy(gate_ref, gate_all, local_sem.at[3]),
             pltpu.make_async_copy(cot_in, cot_ref, local_sem.at[4])]

    def att_copy(p):
        return pltpu.make_async_copy(att_ref.at[p], att, att_sem.at[0])

    def tok_copy(p):
        return pltpu.make_async_copy(tok_ref.at[p], rows_buf.at[p % 2], rows_sem.at[p % 2])

    def mlp_copy(p):
        return pltpu.make_async_copy(rows_buf.at[p % 2], mlp_ref.at[p], rows_sem.at[p % 2])

    for copy in whole:
        copy.start()
    att_copy(0).start()
    for p in range(min(2, pieces)):
        tok_copy(p).start()
    greet(True, "all")
    for copy in whole[:2]:
        copy.wait()
    for gather in (up_gather, down_gather):
        for half in range(2):
            gather.start(half)
    gain_out[...] = jnp.zeros_like(gain_out)
    plan = Plan()

    def mlp_gain(j):
        return gains_ref[j, 1:2, :depth]

    def project(p):
        if p == 0:
            whole[2].wait()
        att_copy(p).wait()
        tok_copy(p).wait()
        squares = jnp.zeros((piece, 1), f32)
        for j in range(n):
            cols = slice(j * depth, (j + 1) * depth)
            block = rows_buf[p % 2, :, :, cols].reshape(piece, depth).astype(f32)
            for k in range(m):
                block = block + mm(att[k], o_all[j, k])
            after[:, cols] = block
            squares = squares + jnp.sum(block * block, axis=1, keepdims=True)
        if p + 1 < pieces:
            att_copy(p + 1).start()
        inverse = lax.rsqrt(squares * (1.0 / width) + EPS)
        for j in range(n):
            cols = slice(j * depth, (j + 1) * depth)
            norm_mid[p, :, :, cols] = (after[:, cols] * inverse * mlp_gain(j)).astype(b16).reshape(m, sub, depth)
        after_own[p] = after[pl.ds(pl.multiple_of(t * sub, sub), sub)]
        if p + 2 < pieces:
            tok_copy(p + 2).start()

    def hidden(p, first, count):
        rows = slice(p * piece, (p + 1) * piece)
        cols = slice(first, first + count)
        x = norm_mid[p].reshape(piece, width)
        gate = mm(x, gate_all[:, :, cols].reshape(width, count))
        up = mm(x, up_all[:, :, cols].reshape(width, count))
        grad = mm(cot_ref[p, :, :, :depth].reshape(piece, depth), down_all[0, cols], NT)
        for j in range(1, n):
            c = cot_ref[p, :, :, j * depth:(j + 1) * depth].reshape(piece, depth)
            grad = grad + mm(c, down_all[j, cols], NT)
        sig = jax.nn.sigmoid(gate)
        silu = gate * sig
        act[rows, cols] = (silu * up).astype(b16)
        gg[rows, cols] = (grad * up * sig * (1.0 + gate * (1.0 - sig))).astype(b16)
        gu[rows, cols] = (grad * silu).astype(b16)

    def mid(p, first, count):
        rows = slice(p * piece, (p + 1) * piece)
        for j in range(first, first + count):
            block = mm(gg[rows], gate_all[j], NT) + mm(gu[rows], up_all[j], NT)
            part[p, :, :, j * depth:(j + 1) * depth] = block.astype(b16).reshape(m, sub, depth)

    def mlp_out(p):
        if p >= 2:
            mlp_copy(p - 2).wait()
        rows = slice(p * piece, (p + 1) * piece)
        for j in range(n):
            block = mm(act[rows], down_all[j]).astype(b16)
            rows_buf[p % 2, :, :, j * depth:(j + 1) * depth] = block.reshape(m, sub, depth)
        rows_buf[p % 2, t] = (rows_buf[p % 2, t].astype(f32) + after_own[p]).astype(b16)
        mlp_copy(p).start()

    def do_copy(p, j):
        return pltpu.make_async_remote_copy(
            src_ref=do_send.at[p, j], dst_ref=do_ref.at[p, t], send_sem=do_send_sem.at[p, j], recv_sem=do_recv_sem.at[p, t],
            device_id=(me, j), device_id_type=MESH)

    def do_arrival(p, j):
        return pltpu.make_async_remote_copy(
            src_ref=do_send.at[p, j], dst_ref=do_ref.at[p, j], send_sem=do_send_sem.at[p, j], recv_sem=do_recv_sem.at[p, j],
            device_id=(me, j), device_id_type=MESH)

    def attended_back(p):
        for k in range(m):
            grad = mm(o_all[0, k], low_ref[p, :, :depth], NT)
            for j in range(1, n):
                grad = grad + mm(o_all[j, k], low_ref[p, :, j * depth:(j + 1) * depth], NT)
            do_send[p, k] = grad.T.astype(b16)

            @pl.when(t != k)
            def _(k=k):
                do_copy(p, k).start()

        do_ref[p, t] = do_send[p, t]

    def mid_back(p):
        grad = mid_sum.total(p)
        after = after_own[p]
        inverse = rms_inverse(after)
        normed = after * inverse
        mean = 0.0
        for j in range(n):
            cols = slice(j * depth, (j + 1) * depth)
            gain_out[:, cols] += jnp.sum(grad[:, cols] * normed[:, cols], axis=0, keepdims=True)
            mean = mean + jnp.sum(grad[:, cols] * mlp_gain(j) * normed[:, cols], axis=1, keepdims=True)
        mean = mean * (1.0 / width)
        for j in range(n):
            cols = slice(j * depth, (j + 1) * depth)
            back = inverse * (grad[:, cols] * mlp_gain(j) - normed[:, cols] * mean)
            back = back + cot_ref[p, t, :, cols].astype(f32)
            after_grad_ref[p, :, cols] = back
            low_ref[p, :, cols] = back.astype(b16)
        attended_back(p)

    def staged(j, slot):
        return pltpu.make_async_copy(stage.at[slot], grads_ref.at[j, slot], stage_sem.at[slot])

    def weight_grads(j):
        cols = slice(j * depth, (j + 1) * depth)
        for slot, terms in enumerate((act, gg, gu)):
            if slot < 2:
                x = (cot_ref if slot == 0 else norm_mid)[:, :, :, cols].reshape(pieces * piece, depth)
            if j:
                staged(j - 1, slot).wait()
            stage[slot] = mm(x, terms[...], TN).astype(b16)
            staged(j, slot).start()

    for p in range(pieces):
        plan.at(3.0 * p, project, p)

    def loaded():
        for copy in whole[3:]:
            copy.wait()

    plan.at(3.0 * pieces, loaded)
    for gather in (up_gather, down_gather):
        for event in gather.events():
            plan.at(10.0 + gather.level(*event), gather.arrive, *event)

    chunk = cut(ff, 512)
    chunks = ff // chunk
    clock = 58.0
    for p in range(pieces):
        for c in range(chunks):
            plan.at(clock, hidden, p, c * chunk, chunk)
            clock += 1.8
        for half in range(2):
            plan.at(clock, mid, p, half * (n // 2), n // 2)
            clock += 1.7
        plan.at(clock, mid_sum.start, p)
        arrived = 92.0 + 25.0 * p
        plan.at(arrived, mid_back, p)
    for j in range(n):
        plan.at(clock, weight_grads, j)
        clock += 2.0
    for p in range(pieces):
        plan.at(clock, mlp_out, p)
        clock += 2.0
    plan.run()

    for slot in range(3):
        staged(n - 1, slot).wait()
    for p in range(max(pieces - 2, 0), pieces):
        mlp_copy(p).wait()
    up_gather.finish()
    down_gather.finish()
    for p in range(pieces):
        mid_sum.finish(p)
        for j in range(m):
            @pl.when(t != j)
            def _(p=p, j=j):
                do_arrival(p, j).wait_recv()
                do_copy(p, j).wait_send()


def middle(attended, o_all, gate_all, up_weight, down_weight, tokens, cotangent, gains):
    f32, b16 = jnp.float32, jnp.bfloat16
    pieces, m, sub, width = tokens.shape
    n, depth, ff = gate_all.shape
    rows = pieces * m * sub
    blocks = tokens.shape
    heads = attended.shape[3]
    out = [((pieces, sub, width), b16), ((pieces, sub, width), f32), ((pieces, m, sub, heads), b16), ((1, width), f32),
           (blocks, b16), ((n, 3, depth, ff), b16)]
    dma = pltpu.SemaphoreType.DMA
    return pl.pallas_call(
        middle_kernel,
        out_shape=[jax.ShapeDtypeStruct(*one) for one in out],
        in_specs=[ANY] * 7 + [VM],
        out_specs=[VM] * 4 + [ANY] * 2,
        scratch_shapes=[pltpu.VMEM(o_all.shape, b16), pltpu.VMEM((n, depth, ff), b16), pltpu.VMEM((n, depth, ff), b16),
                        pltpu.VMEM((n, ff, depth), b16), pltpu.VMEM(blocks, b16), pltpu.VMEM(blocks, b16),
                        pltpu.VMEM(blocks, b16), pltpu.VMEM(blocks, b16),
                        pltpu.VMEM((rows, ff), b16), pltpu.VMEM((rows, ff), b16), pltpu.VMEM((rows, ff), b16),
                        pltpu.VMEM((m * sub, width), f32), pltpu.VMEM((pieces, sub, width), f32),
                        pltpu.VMEM(attended.shape[1:], b16), pltpu.VMEM((2, m, sub, width), b16),
                        pltpu.VMEM((pieces, m, sub, heads), b16), pltpu.VMEM((3, depth, ff), b16),
                        dma((5,)), dma((2,)), dma((2,)), dma((3,)), dma((pieces, m)), dma((pieces, m))]
        + gather_sems() + gather_sems() + [dma((pieces, m)), dma((pieces, m))],
        compiler_params=pltpu.CompilerParams(vmem_limit_bytes=VMEM_BYTES, collective_id=2, has_side_effects=True),
        name="middle",
    )(attended, o_all, gate_all, up_weight, down_weight, tokens, cotangent, gains)


def attn_bwd_block(h, q_ref, do_ref, lse_ref, delta_ref, kv_ref, dq_ref, dk_ref, dv_ref, bias_ref, kv, rows, tile):
    scale = HEAD_SIZE ** -0.5 * LOG2E
    all_rows = q_ref.shape[1]
    k_cols = pl.ds(pl.multiple_of(h * HEAD_SIZE, HEAD_SIZE), HEAD_SIZE)
    v_cols = pl.ds(pl.multiple_of((kv + h) * HEAD_SIZE, HEAD_SIZE), HEAD_SIZE)
    dk_ref[...] = jnp.zeros_like(dk_ref)
    dv_ref[...] = jnp.zeros_like(dv_ref)
    for start in range(0, all_rows, tile):
        at = start % rows
        n_keys = rows if bias_ref is None else at + tile
        q = q_ref[h, start:start + tile]
        do = do_ref[h, start:start + tile]
        k = kv_ref[:n_keys, k_cols]
        scores = mm(k, q, NT) * scale - lse_ref[h, :, start:start + tile]
        if bias_ref is not None:
            scores = scores + bias_ref[:n_keys, at:at + tile]
        probs = jnp.exp2(scores)
        grad = mm(kv_ref[:n_keys, v_cols], do, NT)
        grad = (probs * (grad - delta_ref[h, :, start:start + tile])).astype(jnp.bfloat16)
        dv_ref[:n_keys] += mm(probs.astype(jnp.bfloat16), do)
        dk_ref[:n_keys] += mm(grad, q)
        dq_ref[h, start:start + tile] += mm(grad, k, TN)


def backward_kernel(q_ref, do_ref, lse_ref, kv_ref, kd_ref, qdr_ref, low_ref, att_ref, grads_ref,
                    dq_ref, dkv_ref, gate_out, up_out, down_out, o_grads, do, delta, lse_off, dk, dv, bias, att, att_rows, stage,
                    local_sem, stage_sem, *scratch):
    f32, b16 = jnp.float32, jnp.bfloat16
    kv, all_rows, _ = q_ref.shape
    n, rows, _ = kv_ref.shape
    group = all_rows // rows
    pieces, m, sub, heads = att_rows.shape
    piece = m * sub
    depth = grads_ref.shape[2]
    me, t = lax.axis_index("seq"), lax.axis_index("tp")
    copies = [pltpu.make_async_copy(att_ref.at[:, t], att, local_sem.at[0]),
              pltpu.make_async_copy(att_ref.at[:, :, pl.ds(pl.multiple_of(t * sub, sub), sub)], att_rows, local_sem.at[1])]
    for copy in copies:
        copy.start()
    tile = cut(rows)
    scale = HEAD_SIZE ** -0.5
    gate_sum = seq_sum(lambda j: grads_ref.at[j, 1], scratch[:SUM_SCRATCH])
    up_sum = seq_sum(lambda j: grads_ref.at[j, 2], scratch[SUM_SCRATCH:2 * SUM_SCRATCH])
    down_sum = seq_sum(lambda j: grads_ref.at[j, 0], scratch[2 * SUM_SCRATCH:])

    greet(True, False)
    gate_sum.begin()
    dq_ref[...] = jnp.zeros_like(dq_ref)
    off = jnp.where(qdr_ref[...] == 0, 0.0, 1e30)
    visible = (lax.broadcasted_iota(jnp.int32, (rows, rows), 0)
               <= lax.broadcasted_iota(jnp.int32, (rows, rows), 1)) & (kd_ref[...] == qdr_ref[...])
    bias[...] = jnp.where(visible, 0.0, -1e30)
    for copy in copies:
        copy.wait()
    for p in range(pieces):
        for h in range(kv):
            for g in range(group):
                cols = slice((h * group + g) * HEAD_SIZE, (h * group + g + 1) * HEAD_SIZE)
                at = slice(g * rows + p * piece, g * rows + (p + 1) * piece)
                grad = do_ref[p * piece:(p + 1) * piece, cols]
                do[h, at] = grad
                prod = grad.astype(f32) * att[p, :, cols].astype(f32)
                delta[h, :, at] = jnp.sum(prod.T, axis=0, keepdims=True)

    def staged(j):
        return pltpu.make_async_copy(stage.at[j % 2], o_grads.at[j], stage_sem.at[j % 2])

    for j in range(n):
        if j >= 2:
            staged(j - 2).wait()
        rows_low = low_ref[:, :, j * depth:(j + 1) * depth].reshape(pieces * sub, depth)
        for k in range(m):
            rows_att = att_rows[:, k].reshape(pieces * sub, heads)
            stage[j % 2, :, k * heads:(k + 1) * heads] = mm(rows_low, rows_att, TN).astype(b16)
        staged(j).start()
    for h in range(kv):
        for g in range(group):
            at = slice(g * rows, (g + 1) * rows)
            lse_off[h, :, at] = lse_ref[h, :, at] + off

    def keep(j, h):
        k_cols = pl.ds(pl.multiple_of(h * HEAD_SIZE, HEAD_SIZE), HEAD_SIZE)
        v_cols = pl.ds(pl.multiple_of((kv + h) * HEAD_SIZE, HEAD_SIZE), HEAD_SIZE)
        dkv_ref[j, :, k_cols] = (dk[...] * scale).astype(b16)
        dkv_ref[j, :, v_cols] = dv[...].astype(b16)

    @pl.loop(0, kv)
    def _(h):
        attn_bwd_block(h, q_ref, do, lse_ref, delta, kv_ref.at[me], dq_ref, dk, dv, bias, kv, rows, tile)
        keep(me, h)

    steps = n * kv
    events = [[] for _ in range(steps + 1)]

    def at_time(time, step, *args):
        events[min(int(time / 3.8), steps)].append((step, args))

    def plan_sum(one, meet, *arrivals):
        for e in reversed(range(one.count)):
            at_time(meet, one.meet, e)
        for k, found in enumerate(one.rounds()):
            for event in found:
                at_time(arrivals[min(k, 1)] + k, one.arrive, *event)

    plan_sum(gate_sum, 0.0, 22.0, 34.0)
    at_time(4.0, up_sum.begin)
    plan_sum(up_sum, 15.0, 42.0, 52.0)
    at_time(23.0, down_sum.begin)
    plan_sum(down_sum, 34.0, 61.0, 70.0)

    @pl.loop(0, steps)
    def _(i):
        for k in range(steps):
            if events[k]:
                @pl.when(i == k)
                def _(k=k):
                    for step, args in events[k]:
                        step(*args)

        j, h = i // kv, i % kv

        @pl.when(j < me)
        def _():
            attn_bwd_block(h, q_ref, do, lse_off, delta, kv_ref.at[j], dq_ref, dk, dv, None, kv, rows, tile)
            keep(j, h)

    for step, args in events[steps]:
        step(*args)

    @pl.loop(me + 1, n)
    def _(j):
        dkv_ref[j] = jnp.zeros(dkv_ref.shape[1:], b16)

    dq_ref[...] *= scale
    gate_out[...] = gate_sum.loc[0]
    up_out[...] = up_sum.loc[0]
    down_out[...] = down_sum.loc[0]
    for one in (gate_sum, up_sum, down_sum):
        one.finish()
    for j in range(max(n - 2, 0), n):
        staged(j).wait()


def attention_backward(queries, grad_attended, lse, all_kv, doc_column, doc_row, low, attended, grads):
    f32, b16 = jnp.float32, jnp.bfloat16
    kv, all_rows, _ = queries.shape
    n, rows, _ = all_kv.shape
    _, _, depth, ff = grads.shape
    pieces, m, piece, heads = attended.shape
    out = [(queries.shape, f32), (all_kv.shape, b16), ((depth, ff), b16), ((depth, ff), b16), ((depth, ff), b16),
           ((n, depth, m * heads), b16)]
    dma = pltpu.SemaphoreType.DMA
    return pl.pallas_call(
        backward_kernel,
        out_shape=[jax.ShapeDtypeStruct(*one) for one in out],
        in_specs=[VM] * 7 + [ANY] * 2,
        out_specs=[VM] * 5 + [ANY],
        scratch_shapes=[pltpu.VMEM(queries.shape, b16), pltpu.VMEM((kv, 1, all_rows), f32), pltpu.VMEM((kv, 1, all_rows), f32),
                        pltpu.VMEM((rows, HEAD_SIZE), f32), pltpu.VMEM((rows, HEAD_SIZE), f32), pltpu.VMEM((rows, rows), f32),
                        pltpu.VMEM((pieces, piece, heads), b16), pltpu.VMEM((pieces, m, piece // m, heads), b16),
                        pltpu.VMEM((2, depth, m * heads), b16), dma((2,)), dma((2,))]
        + sum_scratch(depth, ff) + sum_scratch(depth, ff) + sum_scratch(depth, ff),
        compiler_params=pltpu.CompilerParams(vmem_limit_bytes=VMEM_BYTES, collective_id=3, has_side_effects=True),
        name="attention_backward",
    )(queries, grad_attended, lse, all_kv, doc_column, doc_row, low, attended, grads)


def final_kernel(dq_in, proj_in, norm_in, w_in, cos_in, sin_in, after_in, gains_ref, mlp_gain_ref,
                 dkv_ref, o_grads_ref, tok_ref,
                 buf, o_out, w_out, gain_out, dq_ref, proj_ref, norm_ref, w_ref, cos_ref, sin_ref, after_ref,
                 dproj, part, recv, tok_own, w_grads, gain_seq, gain_line, o_part, o_recv, local_sem, *scratch):
    f32, b16 = jnp.float32, jnp.bfloat16
    pieces, m, sub, width = part.shape
    n, depth, wide = w_ref.shape
    kv, all_rows, _ = dq_ref.shape
    rows = norm_ref.shape[0]
    group = all_rows // rows
    q_width, k_width = kv * group * HEAD_SIZE, kv * HEAD_SIZE
    piece = m * sub
    me, t = lax.axis_index("seq"), lax.axis_index("tp")
    tile = cut(rows)
    kv_sum = seq_sum(lambda j: dkv_ref.at[j], scratch[:6])
    o_sum = seq_sum(lambda j: o_grads_ref.at[j], scratch[6:12])
    w_sum = seq_sum(lambda j: w_grads.at[j], scratch[12:18])
    in_sum = LineSum(part, recv, scratch[18], scratch[19])
    out_gather = LineGather(buf, scratch[20], scratch[21])
    gain_gather = SeqGather(gain_seq, scratch[22], scratch[23], halves=1)
    gain_total = LineGather(gain_line, scratch[24], scratch[25])
    o_total = DirectSum(o_part, o_recv, scratch[26], scratch[27])

    own = [pltpu.make_async_copy(tok_ref.at[p, t], tok_own.at[p], local_sem.at[p]) for p in range(pieces)]
    loads = [pltpu.make_async_copy(source, into, local_sem.at[pieces + i]) for i, (source, into) in enumerate((
        (dq_in, dq_ref), (proj_in, proj_ref), (cos_in, cos_ref), (sin_in, sin_ref), (norm_in, norm_ref), (w_in, w_ref),
        (after_in, after_ref)))]
    for copy in own + loads:
        copy.start()
    greet(True, "all")
    kv_sum.begin()
    gain_q, gain_k = gains_ref[0, 2:3, :HEAD_SIZE], gains_ref[0, 3:4, :HEAD_SIZE]
    for j in range(1, n):
        gain_q = gain_q + gains_ref[j, 2:3, :HEAD_SIZE]
        gain_k = gain_k + gains_ref[j, 3:4, :HEAD_SIZE]
    gain_seq[me] = jnp.zeros(gain_seq.shape[1:], f32)
    gain_seq[me, 1:2] = mlp_gain_ref[...]
    for p in range(pieces):
        in_sum.clear(p)
    for copy in own + loads:
        copy.wait()
    plan = Plan()

    def head_back(grad, at, first, gain):
        e = grad * cos_ref[at] - pltpu.roll(grad, HEAD_SIZE // 2, 1) * sin_ref[at]
        u = proj_ref[at, first:first + HEAD_SIZE]
        inverse = rms_inverse(u)
        normed = u * inverse
        scaled = e * gain
        back = inverse * (scaled - normed * jnp.mean(scaled * normed, axis=-1, keepdims=True))
        dproj[at, first:first + HEAD_SIZE] = back.astype(b16)
        return jnp.sum(e * normed, axis=0, keepdims=True)

    def queries_back(h, g):
        terms = jnp.zeros((1, HEAD_SIZE), f32)
        for start in range(0, rows, tile):
            grad = dq_ref[h, g * rows + start:g * rows + start + tile]
            terms += head_back(grad, slice(start, start + tile), (h * group + g) * HEAD_SIZE, gain_q)
        gain_seq[me, 2:3, :HEAD_SIZE] += terms

    def keys_back():
        for h in range(kv):
            cols = slice(h * HEAD_SIZE, (h + 1) * HEAD_SIZE)
            terms = jnp.zeros((1, HEAD_SIZE), f32)
            for start in range(0, rows, tile):
                at = slice(start, start + tile)
                terms += head_back(kv_sum.loc[0, at, cols].astype(f32), at, q_width + h * HEAD_SIZE, gain_k)
            gain_seq[me, 3:4, :HEAD_SIZE] += terms
        dproj[:, q_width + k_width:] = kv_sum.loc[0, :, k_width:]

    def in_part(p):
        for j in range(n):
            block = mm(dproj[p * piece:(p + 1) * piece], w_ref[j], NT)
            part[p, :, :, j * depth:(j + 1) * depth] = block.astype(b16).reshape(m, sub, depth)

    def weight_grads(j):
        w_grads[j] = mm(norm_ref[:, j * depth:(j + 1) * depth], dproj[...], TN).astype(b16)

    def norm_back(p):
        grad = in_sum.total(p)
        tok = tok_own[p].astype(f32)
        inverse = rms_inverse(tok)
        normed = tok * inverse
        mean = 0.0
        for j in range(n):
            cols = slice(j * depth, (j + 1) * depth)
            gain_seq[me, 0:1, cols] += jnp.sum(grad[:, cols] * normed[:, cols], axis=0, keepdims=True)
            mean = mean + jnp.sum(grad[:, cols] * gains_ref[j, 0:1, :depth] * normed[:, cols], axis=1, keepdims=True)
        mean = mean * (1.0 / width)
        for j in range(n):
            cols = slice(j * depth, (j + 1) * depth)
            back = inverse * (grad[:, cols] * gains_ref[j, 0:1, :depth] - normed[:, cols] * mean)
            buf[p, t, :, cols] = (after_ref[p, :, cols] + back).astype(b16)
        out_gather.start(p)

    def plan_sum(one, base, length):
        for e in reversed(range(one.count)):
            plan.at(base, one.meet, e)
        for k, found in enumerate(one.rounds()):
            for event in found:
                plan.at(base + length * (2.0 - 0.5 ** k), one.arrive, *event)

    for h in range(kv):
        for g in range(group):
            plan.at(1.0, queries_back, h, g)
    plan_sum(kv_sum, 7.0, 18.0)
    plan.at(30.0, o_sum.begin)
    plan.at(43.5, keys_back)
    clock = 44.0
    hop = 8.0
    last = 0.0
    for p in range(pieces):
        plan.at(clock, in_part, p)
        clock += 2.2
        start = 47.0 + 3 * hop * p
        for k in range(m - 1):
            plan.at(start + hop * k, in_sum.step, p, k)
        start += hop * (m - 1) + 1
        plan.at(start, norm_back, p)
        for d in range(1, m):
            last = start + hop * d
            plan.at(last, out_gather.arrive, p, d)
    for j in range(n):
        plan.at(50.0 + 0.8 * j, weight_grads, j)
    plan.at(57.0, w_sum.begin)
    plan_sum(o_sum, 56.0, 34.0)
    plan_sum(w_sum, 90.0, 22.0)

    def o_over_tp():
        heads = o_part.shape[3]
        for k in range(m):
            o_part[0, k] = o_sum.loc[0, :, k * heads:(k + 1) * heads]
        o_total.start(0)

    plan.at(108.5, o_over_tp)
    gain_time = last - 3 * hop + 0.5
    plan.at(gain_time, gain_gather.start, 0)
    for k, event in enumerate(gain_gather.events()):
        plan.at(gain_time + 1.0 + 0.5 * k, gain_gather.arrive, *event)

    def over_tp():
        total = gain_seq[0]
        for j in range(1, n):
            total = total + gain_seq[j]
        gain_line[0, t] = total
        gain_total.start(0)

    plan.at(gain_time + 1.0 + 0.5 * n, over_tp)
    for d in range(1, m):
        plan.at(gain_time + 2.0 + 0.5 * n + 2.0 * d, gain_total.arrive, 0, d)
    plan.run()

    total = gain_line[0, 0]
    for j in range(1, m):
        total = total + gain_line[0, j]
    gain_out[...] = total
    o_out[...] = o_total.total(0).T
    w_out[...] = w_sum.loc[0]
    for one in (kv_sum, o_sum, w_sum, gain_gather):
        one.finish()
    in_sum.finish(pieces - 1)
    for p in range(pieces):
        out_gather.finish(p)
    gain_total.finish(0)
    o_total.finish(0)


def final(grad_queries, projected, normalized, w_all, cosines, sines, after_grad, gains, mlp_gain, grad_kv, o_grads, tokens):
    f32, b16 = jnp.float32, jnp.bfloat16
    pieces, m, sub, width = tokens.shape
    n, depth, wide = w_all.shape
    kv, all_rows, _ = grad_queries.shape
    rows, k_width = normalized.shape[0], kv * HEAD_SIZE
    q_width = wide - 2 * k_width
    out = [(tokens.shape, b16), ((q_width, depth), f32), ((depth, wide), b16), ((8, width), f32)]
    held = (grad_queries, projected, normalized, w_all, cosines, sines, after_grad)
    return pl.pallas_call(
        final_kernel,
        out_shape=[jax.ShapeDtypeStruct(*one) for one in out],
        in_specs=[ANY] * 7 + [VM] * 2 + [ANY] * 3,
        out_specs=[VM] * 4,
        scratch_shapes=[pltpu.VMEM(one.shape, one.dtype) for one in held] + [pltpu.VMEM((rows, wide), b16), pltpu.VMEM(tokens.shape, b16),
                        pltpu.VMEM((pieces, m + 1, sub, width), b16), pltpu.VMEM((pieces, sub, width), b16),
                        pltpu.VMEM((n, depth, wide), b16), pltpu.VMEM((n, 8, width), f32), pltpu.VMEM((1, m, 8, width), f32),
                        pltpu.VMEM((1, m, depth, q_width), b16), pltpu.VMEM((1, m, depth, q_width), b16),
                        pltpu.SemaphoreType.DMA((pieces + 7,))]
        + sum_scratch(rows, 2 * k_width) + sum_scratch(depth, m * q_width) + sum_scratch(depth, wide)
        + line_sems(pieces) + gather_sems(1) + line_sems(1)[2:]
        + [pltpu.SemaphoreType.DMA((1, m)), pltpu.SemaphoreType.DMA((1, m))],
        compiler_params=pltpu.CompilerParams(vmem_limit_bytes=VMEM_BYTES, collective_id=4, has_side_effects=True),
        name="final",
    )(grad_queries, projected, normalized, w_all, cosines, sines, after_grad, gains, mlp_gain, grad_kv, o_grads, tokens)


def finish_kernel(tokens_ref, layer_ref, gate_ref, up_ref, down_ref, o_ref, w_ref,
                  tokens_out, layer_out, gate_out, up_out, down_out, o_out, q_out, k_out, v_out):
    f32 = jnp.float32
    tile = cut(tokens_ref.shape[0], 128)

    @pl.loop(0, tokens_ref.shape[0] // tile)
    def _(i):
        at = pl.ds(i * tile, tile)
        tokens_out[at] = tokens_ref[at].astype(f32)
        layer_out[at] = layer_ref[at]

    gate_out[...] = gate_ref[...].astype(f32)
    up_out[...] = up_ref[...].astype(f32)
    down_out[...] = down_ref[...].astype(f32).T
    o_out[...] = o_ref[...]
    first = 0
    for out in (q_out, k_out, v_out):
        out[...] = w_ref[:, first:first + out.shape[1]].astype(f32)
        first += out.shape[1]


def finish(tokens, layer, gate, up, down, o, w, q_width):
    f32 = jnp.float32
    depth, ff = gate.shape
    k_width = (w.shape[1] - q_width) // 2
    out = [(tokens.shape, f32), (layer.shape, layer.dtype), (gate.shape, f32), (up.shape, f32), ((ff, depth), f32), (o.shape, f32),
           ((depth, q_width), f32), ((depth, k_width), f32), ((depth, k_width), f32)]
    return pl.pallas_call(
        finish_kernel,
        out_shape=[jax.ShapeDtypeStruct(*one) for one in out],
        in_specs=[VM] * 7, out_specs=[VM] * 9,
        compiler_params=pltpu.CompilerParams(vmem_limit_bytes=VMEM_BYTES),
        name="finish",
    )(tokens, layer, gate, up, down, o, w)


def pack_gains(attn_gain, mlp_gain, query_gain, key_gain):
    width = max(attn_gain.shape[0], HEAD_SIZE)
    place = lax.axis_index("seq") * query_gain.shape[0]

    def placed(gain):
        return lax.dynamic_update_slice(jnp.zeros((width,), jnp.float32), gain.astype(jnp.float32), (place,))

    def padded(gain):
        return jnp.pad(gain.astype(jnp.float32), (0, width - gain.shape[0]))

    lines = [padded(attn_gain), padded(mlp_gain), placed(query_gain), placed(key_gain)]
    return jnp.stack(lines + [jnp.zeros((width,), jnp.float32)] * 4)


def norm_rows(values, gain_vec):
    return values * lax.rsqrt(jnp.mean(values * values, axis=-1, keepdims=True) + EPS) * gain_vec


def norm_back(values, gain_vec, grad_out):
    inverse = lax.rsqrt(jnp.mean(values * values, axis=-1, keepdims=True) + EPS)
    normed = values * inverse
    scaled = grad_out * gain_vec
    grad_in = inverse * (scaled - normed * jnp.mean(scaled * normed, axis=-1, keepdims=True))
    return (grad_in, grad_out * normed)


def rope_tables(positions, head_dim):
    half_dim = head_dim // 2
    frequency = BASE ** (-2.0 * jnp.arange(half_dim, dtype=jnp.float32) / head_dim)
    angles = positions.astype(jnp.float32)[:, None] * frequency[None, :]
    return (jnp.cos(angles)[:, None, :], jnp.sin(angles)[:, None, :])


def rotate(values, cosines, sine_values, direction):
    half_dim = values.shape[-1] // 2
    lower_half = values[..., :half_dim]
    upper_half = values[..., half_dim:]
    signed = sine_values * direction
    return jnp.concatenate(
        [lower_half * cosines - upper_half * signed, upper_half * cosines + lower_half * signed],
        axis=-1,
    )


def per_device(
    tokens,
    q_weight,
    key_matrix,
    value_matrix,
    o_weight,
    gate_weight,
    up_weight,
    down_weight,
    attn_gain,
    mlp_gain,
    query_gain,
    key_gain,
    positions,
    seq_ids,
    cotangent,
):
    f32 = jnp.float32
    b16 = jnp.bfloat16
    local_rows = tokens.shape[0]
    q_local = q_weight.shape[1] // HEAD_SIZE
    kv_local = key_matrix.shape[1] // HEAD_SIZE
    heads_per_group = q_local // kv_local
    share_rows = local_rows // lax.axis_size("tp")
    share_start = lax.axis_index("tp") * share_rows
    s = lax.axis_index("seq")
    own_docs = lax.dynamic_slice_in_dim(seq_ids, s * local_rows, local_rows)
    doc_column, doc_row = own_docs[:, None], own_docs[None, :]
    seq_count = lax.axis_size("seq")
    gains = pack_gains(attn_gain, mlp_gain, query_gain, key_gain)
    cosines, sine_values = rope_tables(positions, HEAD_SIZE)
    cos_wide = jnp.concatenate([cosines, cosines], axis=-1).reshape(local_rows, HEAD_SIZE)
    sin_wide = jnp.concatenate([-sine_values, sine_values], axis=-1).reshape(local_rows, HEAD_SIZE)
    model = tokens.shape[1]
    tp_count = lax.axis_size("tp")
    sub = math.gcd(local_rows // tp_count, 64)
    while local_rows // tp_count // sub > 3:
        sub *= 2
    split = (local_rows // tp_count // sub, tp_count, sub, model)
    (normalized_input, projected, queries_h, all_kv, attended_all, lse, all_gains, w_all, o_all, gate_all) = forward_attention(
        tokens, q_weight, key_matrix, value_matrix, gains, cos_wide, sin_wide, doc_column, doc_row, o_weight, gate_weight, split[0])
    ff = gate_weight.shape[1]
    q_width, k_width = q_local * HEAD_SIZE, kv_local * HEAD_SIZE
    low_own, after_grad_own, grad_attended, mlp_gain_own, mlp_part, mlp_grads = middle(
        attended_all, o_all, gate_all, up_weight, down_weight, tokens.reshape(split), cotangent.reshape(split), all_gains)
    layer_out = lax.psum(mlp_part, "tp").reshape(local_rows, model)

    q_width = q_local * HEAD_SIZE
    grad_query_h, grad_kv, gate_sum, up_sum, down_sum, o_grads = attention_backward(
        queries_h, grad_attended.reshape(local_rows, q_width), lse, all_kv, doc_column, doc_row, low_own, attended_all, mlp_grads)
    token_blocks, grad_o, grad_w, gain_sums = final(
        grad_query_h, projected, normalized_input, w_all, cos_wide, sin_wide, after_grad_own, all_gains, mlp_gain_own,
        grad_kv, o_grads, tokens.reshape(split))
    (grad_tokens, layer_out, grad_gate_w, grad_up_w, grad_down, grad_o_w, grad_q_w, grad_k_w, grad_v_w) = finish(
        token_blocks.reshape(local_rows, model), layer_out, gate_sum, up_sum, down_sum, grad_o, grad_w, q_width)

    def own_part(line, width):
        count = width // seq_count
        return lax.dynamic_slice_in_dim(gain_sums[line], s * count, count)

    return (
        layer_out,
        grad_tokens,
        grad_q_w,
        grad_k_w,
        grad_v_w,
        grad_o_w,
        grad_gate_w,
        grad_up_w,
        grad_down,
        own_part(0, model),
        own_part(1, model),
        own_part(2, HEAD_SIZE),
        own_part(3, HEAD_SIZE),
    )


def solution(mesh):
    placed = (
        P("seq", None),
        P("seq", "tp"),
        P("seq", "tp"),
        P("seq", "tp"),
        P("tp", "seq"),
        P("seq", "tp"),
        P("seq", "tp"),
        P("tp", "seq"),
        P("seq"),
        P("seq"),
        P("seq"),
        P("seq"),
        P("seq"),
        P(),
        P("seq", None),
    )
    return jax.shard_map(
        per_device,
        mesh=mesh,
        in_specs=placed,
        out_specs=(
            P("seq", None),
            P("seq", None),
            P("seq", "tp"),
            P("seq", "tp"),
            P("seq", "tp"),
            P("tp", "seq"),
            P("seq", "tp"),
            P("seq", "tp"),
            P("tp", "seq"),
            P("seq"),
            P("seq"),
            P("seq"),
            P("seq"),
        ),
        check_vma=False,
    )
```
